512 devices in a mesh: dom: 32 (over x, z), level: 16 (over y, core).
Axes of the slice: x: 4, y: 8, z: 8, core: 2. Of those that a mesh axis runs over, the one named last changes fastest.
Arguments:
- right_side: bfloat16 [2048, 64, 128], P(('dom', 'level')), may hold values from -6 to 6
- diag_inverse: bfloat16 [2048, 128, 128], P(('dom', 'level'))
- off_blocks: bfloat16 [2048, 3, 128, 128], P(('dom', 'level')), may hold values from -0.25 to 0.25
- columns: int32 [2048, 3], replicated, may hold values from -1 to 2047, as said below
- plan: int32 [16], replicated, may hold values from 0 to 15, as said below
Outputs:
- forward_solution: bfloat16 [2048, 64, 128], P(('dom', 'level'))
- preconditioned: bfloat16 [2048, 64, 128], P(('dom', 'level'))
The draws below stay inside these ranges and needn't reach their ends.
Inputs may be any that keep to these rules, and one draw needn't show every extreme that they name: For block row g of partition d = g // 64 and level-axis index p = (g // 4) % 16: every entry is -1 where plan[p] // 2 == 0; otherwise columns[g, n] is a block row of partition (d + n - 1) mod 32 whose level-axis index q has plan[q] // 2 == plan[p] // 2 - 1. `plan`: A permutation of the level-axis indices; each level is held by exactly two of them.
All inputs are finite; a program needn't handle non-finite values.
Results may differ from the reference program's by a relative error of at most 0.03.
Values may be sent and summed in bfloat16 or wider, within the bound.
No kernel may reach another device: no remote copies, remote signals or barrier semaphores. Data moves between devices by JAX's collectives and lax.ppermute only.
A program may use at most 64 MiB of HBM per device.

```python
import jax
import jax.numpy as jnp
from jax import lax

B = 128
K = 64
R = 4
NB = 3
LEVELS = 8
ROWS = 2048
N_DOM = 32
N_LEVEL = 16


def shared_ordering(key):
    return jax.random.permutation(key, N_LEVEL).astype(jnp.int32)


def draw_plan(key, part):
    ordering = shared_ordering(key)
    return ordering


def draw_columns(key, part):
    ordering = shared_ordering(key)
    key = jax.random.fold_in(key, 5)
    first_key, second_key = jax.random.split(key)
    level_ids = jnp.arange(N_LEVEL, dtype=jnp.int32)
    inverse = jnp.sum(jnp.where(ordering[None, :] == level_ids[:, None], level_ids[None, :], 0), axis=1)
    row_ids = jnp.arange(ROWS, dtype=jnp.int32)
    own_part = row_ids // (N_LEVEL * R)
    row_level = ordering[row_ids // R % N_LEVEL] // 2
    which_half = jax.random.randint(first_key, (ROWS, NB), 0, 2)
    drawn_slot = 2 * jnp.maximum(row_level - 1, 0)[:, None] + which_half
    within = jax.random.randint(second_key, (ROWS, NB), 0, R)
    source = inverse[drawn_slot]
    partition = (own_part[:, None] + jnp.arange(NB, dtype=jnp.int32)[None, :] - 1) % N_DOM
    target = (partition * N_LEVEL + source) * R + within
    return jnp.where(row_level[:, None] > 0, target, -1).astype(jnp.int32)


def draw_diag_inverse(key, part):
    key = jax.random.fold_in(key, 11)
    first_key, second_key = jax.random.split(key)
    identity = jnp.eye(B, dtype=jnp.float32)
    spread = jax.random.normal(first_key, (ROWS, B, B), jnp.float32) * 0.3
    diagonal = jax.random.uniform(second_key, (ROWS, 1, B), jnp.float32, 0.6, 1.4)
    return (identity * diagonal + spread * B ** (-0.5)).astype(jnp.bfloat16)


def shard_levels(key, shape, cuts, least, top_value):
    loudness, own = 1.0, jax.random.fold_in(key, 6)
    for axis_at, blocks in cuts:
        heights = jnp.exp(jax.random.uniform(jax.random.fold_in(own, axis_at), (blocks,), jnp.float32, least / len(cuts), top_value / len(cuts)))
        loudness = loudness * jnp.repeat(heights, shape[axis_at] // blocks).reshape([-1 if axis == axis_at else 1 for axis in range(len(shape))])
    return loudness


def scatter_about(rng, dims, scale, limit, pieces=(), kind=jnp.bfloat16):
    level = shard_levels(rng, dims, pieces, -0.22, 0.18) if pieces else 1.0
    values = jax.random.normal(rng, dims, jnp.float32) * scale * level
    return jnp.minimum(jnp.maximum(values, -limit), limit).astype(kind)


def setup_inputs(seed: int = 0) -> dict:
    arg_keys = jax.random.split(jax.random.key(seed), 6)
    right_side = scatter_about(arg_keys[0], (ROWS, K, B), 1.0, 6.0, ((0, 512),))
    diag_inverse = draw_diag_inverse(jax.random.fold_in(arg_keys[5], 71), 0)
    off_blocks = scatter_about(arg_keys[2], (ROWS, NB, B, B), (4 * B) ** -0.5, 0.25, ((0, 512),))
    columns = draw_columns(jax.random.fold_in(arg_keys[5], 71), 0)
    plan = draw_plan(jax.random.fold_in(arg_keys[5], 71), 0)
    return {"right_side": right_side, "diag_inverse": diag_inverse, "off_blocks": off_blocks, "columns": columns, "plan": plan}


def reference(right_side, diag_inverse, off_blocks, columns, plan):
    row_ids = jnp.arange(ROWS, dtype=jnp.int32)
    row_level = plan[(row_ids // R) % N_LEVEL] // 2
    present = columns >= 0
    clamped = jnp.where(present, columns, 0).astype(jnp.int32)
    inverse = diag_inverse.astype(jnp.float32)
    blocks = off_blocks.astype(jnp.float32)
    running = jnp.zeros(right_side.shape, jnp.float32)
    solved = jnp.zeros(right_side.shape, jnp.bfloat16)
    for level_now in range(LEVELS):
        shifted = lax.optimization_barrier((right_side.astype(jnp.float32) - running).astype(jnp.bfloat16))
        candidate = jnp.einsum("rkb,rbc->rkc", shifted.astype(jnp.float32), inverse).astype(jnp.bfloat16)
        solved = jnp.where((row_level == level_now)[:, None, None], candidate, solved)
        solved = lax.optimization_barrier(solved)
        chosen = jnp.logical_and(present, row_level[clamped] == level_now)
        picked = jnp.where(chosen[:, :, None, None], solved[clamped].astype(jnp.float32), 0.0)
        running = running + jnp.einsum("rnkb,rnbc->rkc", picked, blocks)
    target = jnp.where(present, columns, ROWS).astype(jnp.int32).reshape(-1)
    running = jnp.zeros(right_side.shape, jnp.float32)
    result = jnp.zeros(right_side.shape, jnp.bfloat16)
    for level_now in range(LEVELS - 1, -1, -1):
        folded = lax.optimization_barrier(running.astype(jnp.bfloat16))
        candidate = (solved.astype(jnp.float32) - jnp.einsum("rkb,rbc->rkc", folded.astype(jnp.float32), inverse)).astype(jnp.bfloat16)
        result = jnp.where((row_level == level_now)[:, None, None], candidate, result)
        result = lax.optimization_barrier(result)
        pushes = lax.optimization_barrier(jnp.einsum("rkc,rnbc->rnkb", result.astype(jnp.float32), blocks).astype(jnp.bfloat16))
        chosen = jnp.logical_and(present, (row_level == level_now)[:, None])
        summands = jnp.where(chosen[:, :, None, None], pushes.astype(jnp.float32), 0.0).reshape(ROWS * NB, K, B)
        running = running + jax.ops.segment_sum(summands, target, num_segments=ROWS + 1)[:ROWS]
    return solved, result
```

```python
import functools

import jax
import jax.numpy as jnp
from jax import lax
from jax.experimental import pallas as pl
from jax.experimental.pallas import tpu as pltpu
from jax.sharding import PartitionSpec as P

BF16 = jnp.bfloat16
F32 = jnp.float32


def dot(a, b):
    return lax.dot_general(a, b, (((1,), (0,)), ((), ())), preferred_element_type=F32)


def dot_t(a, b):
    return lax.dot_general(a, b, (((1,), (1,)), ((), ())), preferred_element_type=F32)


def fetch(owners, weights, held, sems, level, half):
    return pltpu.make_async_copy(
        weights.at[owners[2 * level + half]], held.at[half], sems.at[half]
    )


def either(low, high, share):
    top = lax.broadcasted_iota(jnp.int32, low.shape, 0) < share
    return jnp.where(top, low, high)


def forward_kernel(level, share, owners, weights, pick, side, left, own, right, out, held, sems):
    copies = [fetch(owners, weights, held, sems, level, half) for half in range(2)]
    for copy in copies:
        copy.start()
    rows = held.shape[1]
    count = 2 * rows
    span = count * share
    near = jnp.concatenate([left[...], own[...], right[...]], axis=0)
    picked = dot(pick[level], near)
    copies[0].wait()
    for pair in range(count // 2):
        if pair == rows // 2:
            copies[1].wait()
        half, row = divmod(2 * pair, rows)
        at = 2 * share * pair
        terms = [picked[n * span + at : n * span + at + 2 * share] for n in range(3)]
        terms = jnp.concatenate(terms, axis=1).astype(BF16)
        total = either(
            *[dot(terms, held[half, row + one, 1:].reshape(-1, held.shape[-1])) for one in range(2)],
            share,
        )
        shifted = (side[level, at : at + 2 * share].astype(F32) - total).astype(BF16)
        solved = either(*[dot(shifted, held[half, row + one, 0]) for one in range(2)], share)
        out[at : at + 2 * share] = solved.astype(BF16)


def backward_kernel(
    level, share, last, owners, weights, spread, solved, from_left, own, from_right, result, *rest
):
    *outs, held, sems = rest
    copies = [fetch(owners, weights, held, sems, level, half) for half in range(2)]
    for copy in copies:
        copy.start()
    rows = held.shape[1]
    count = 2 * rows
    folded = (from_left[...] + own[...] + from_right[...]).astype(BF16)
    pushes = [[], [], []]
    copies[0].wait()
    for pair in range(count // 2):
        if pair == rows // 2:
            copies[1].wait()
        half, row = divmod(2 * pair, rows)
        at = 2 * share * pair
        part = folded[at : at + 2 * share]
        part = either(*[dot(part, held[half, row + one, 0]) for one in range(2)], share)
        done = (solved[at : at + 2 * share].astype(F32) - part).astype(BF16)
        result[at : at + 2 * share] = done
        if not last:
            for n in range(3):
                pushes[n].append(
                    either(*[dot_t(done, held[half, row + one, 1 + n]) for one in range(2)], share)
                )
    if not last:
        pushed = jnp.concatenate(pushes[0] + pushes[1] + pushes[2], axis=0).astype(BF16)
        total = dot(spread[level], pushed)
        span = count * share
        for n in range(3):
            outs[n][...] = total[n * span : (n + 1) * span]


def call(kernel, outs, owners, weights, *rest):
    vmem = pl.BlockSpec(memory_space=pltpu.VMEM)
    return pl.pallas_call(
        kernel,
        out_shape=outs,
        in_specs=[
            pl.BlockSpec(memory_space=pltpu.SMEM),
            pl.BlockSpec(memory_space=pl.ANY),
            *[vmem] * len(rest),
        ],
        out_specs=[vmem] * len(outs),
        scratch_shapes=[
            pltpu.VMEM((2,) + weights.shape[1:], weights.dtype),
            pltpu.SemaphoreType.DMA((2,)),
        ],
        compiler_params=pltpu.CompilerParams(vmem_limit_bytes=16 * 2**20),
    )(owners, weights, *rest)


def local(right_side, diag_inverse, off_blocks, columns, plan):
    rows, depth, width = right_side.shape
    doms = lax.axis_size("dom")
    levs = lax.axis_size("level")
    levels = levs // 2
    share = depth // levs
    count = 2 * rows
    dom = lax.axis_index("dom")
    lev = lax.axis_index("level")
    up = [(i, (i + 1) % doms) for i in range(doms)]
    down = [(target, source) for source, target in up]

    weights = jnp.concatenate([diag_inverse[:, None], off_blocks], axis=1)
    weights = lax.all_gather(weights, "level")

    ids = jnp.arange(levs, dtype=jnp.int32)
    own_level = jnp.sum(jnp.where(ids == lev, plan, 0)) // 2
    inverse = jnp.sum(jnp.where(plan[None, :] == ids[:, None], ids[None, :], 0), axis=1)

    first = jnp.einsum("rkb,rbc->rkc", right_side, diag_inverse, preferred_element_type=F32)
    side = jnp.where(own_level == 0, first.astype(BF16), right_side)
    side = side.reshape(rows, levs, share, width)
    side = lax.all_to_all(side, "level", 1, 0, tiled=False)
    side = side.reshape(levs, rows * share, width)[inverse].reshape(levels, count * share, width)

    part = lax.dynamic_slice_in_dim(columns, dom * levs * rows, levs * rows, 0)
    part = part.reshape(levs, rows * 3)[inverse].reshape(levels, count, 3)
    source = plan[(part // rows) % levs] % 2 * rows + part % rows
    j = jnp.arange(count, dtype=jnp.int32)
    meets = source[:, :, :, None] == j
    eye_n = jnp.eye(3, dtype=bool)
    eye_k = jnp.eye(share, dtype=bool)
    pick = (
        meets.transpose(0, 2, 1, 3)[:, :, :, None, None, :, None]
        & eye_n[None, :, None, None, :, None, None]
        & eye_k[None, None, None, :, None, None, :]
    )
    size = 3 * count * share
    pick = pick.reshape(levels, size, size).astype(BF16)
    spread = pick.transpose(0, 2, 1)

    vector = jax.ShapeDtypeStruct((count * share, width), BF16)
    summed = jax.ShapeDtypeStruct((count * share, width), F32)

    solved = [side[0]]
    for level in range(1, levels):
        own = solved[-1]
        left = lax.ppermute(own, "dom", up)
        right = lax.ppermute(own, "dom", down)
        kernel = functools.partial(forward_kernel, level, share)
        solved += call(kernel, [vector], inverse, weights, pick, side, left, own, right)

    zero = jnp.zeros(summed.shape, F32)
    left, own, right = zero, zero, zero
    results = []
    for level in range(levels - 1, -1, -1):
        last = level == 0
        kernel = functools.partial(backward_kernel, level, share, last)
        outs = [vector] if last else [vector, summed, summed, summed]
        result, *sums = call(
            kernel, outs, inverse, weights, spread, solved[level], left, own, right
        )
        results.append(result)
        if not last:
            right = lax.ppermute(sums[0], "dom", down)
            left = lax.ppermute(sums[2], "dom", up)
            own = sums[1]

    both = jnp.stack([jnp.stack(solved), jnp.stack(results[::-1])])
    both = both.reshape(2, levs, rows, share, width)[:, plan]
    both = lax.all_to_all(both, "level", 1, 0, tiled=False)
    both = both.transpose(1, 2, 0, 3, 4).reshape(2, rows, depth, width)
    return both[0], both[1]


def solution(mesh):
    return jax.shard_map(
        local,
        mesh=mesh,
        in_specs=(
            P(("dom", "level"), None, None),
            P(("dom", "level"), None, None),
            P(("dom", "level"), None, None, None),
            P(),
            P(),
        ),
        out_specs=(P(("dom", "level"), None, None), P(("dom", "level"), None, None)),
        check_vma=False,
    )
```

```python
import functools

import jax
import jax.numpy as jnp
from jax import lax
from jax.experimental import pallas as pl
from jax.experimental.pallas import tpu as pltpu
from jax.sharding import PartitionSpec as P

BF16 = jnp.bfloat16
F32 = jnp.float32


def dot(a, b):
    return lax.dot_general(a, b, (((1,), (0,)), ((), ())), preferred_element_type=F32)


def dot_t(a, b):
    return lax.dot_general(a, b, (((1,), (1,)), ((), ())), preferred_element_type=F32)


def either(low, high, share):
    top = lax.broadcasted_iota(jnp.int32, low.shape, 0) < share
    return jnp.where(top, low, high)


def forward_kernel(level, share, owners, weights, pick, side, far, own, near, out):
    rows = weights.shape[1]
    count = 2 * rows
    span = count * share
    around = jnp.concatenate([far[...], own[...], near[...]], axis=0)
    picked = dot(pick[level], around)
    for pair in range(count // 2):
        half, row = divmod(2 * pair, rows)
        owner = owners[2 * level + half]
        at = 2 * share * pair
        terms = [picked[n * span + at : n * span + at + 2 * share] for n in range(3)]
        terms = jnp.concatenate(terms, axis=1).astype(BF16)
        blocks = [weights[owner, row + one, 1:].reshape(-1, terms.shape[1] // 3) for one in range(2)]
        total = either(*[dot(terms, block) for block in blocks], share)
        shifted = (side[level, at : at + 2 * share].astype(F32) - total).astype(BF16)
        solved = either(*[dot(shifted, weights[owner, row + one, 0]) for one in range(2)], share)
        out[at : at + 2 * share] = solved.astype(BF16)


def backward_kernel(
    level, share, last, owners, weights, spread, solved, far, own, near, result, *outs
):
    rows = weights.shape[1]
    count = 2 * rows
    folded = (far[...] + own[...] + near[...]).astype(BF16)
    pushes = [[], [], []]
    for pair in range(count // 2):
        half, row = divmod(2 * pair, rows)
        owner = owners[2 * level + half]
        at = 2 * share * pair
        part = folded[at : at + 2 * share]
        part = either(*[dot(part, weights[owner, row + one, 0]) for one in range(2)], share)
        done = (solved[at : at + 2 * share].astype(F32) - part).astype(BF16)
        result[at : at + 2 * share] = done
        if not last:
            for n in range(3):
                pushes[n].append(
                    either(*[dot_t(done, weights[owner, row + one, 1 + n]) for one in range(2)], share)
                )
    if not last:
        pushed = jnp.concatenate(pushes[0] + pushes[1] + pushes[2], axis=0).astype(BF16)
        total = dot(spread[level], pushed)
        span = count * share
        for n in range(3):
            outs[n][...] = total[n * span : (n + 1) * span]


def call(kernel, outs, owners, *rest):
    vmem = pl.BlockSpec(memory_space=pltpu.VMEM)
    return pl.pallas_call(
        kernel,
        out_shape=outs,
        in_specs=[pl.BlockSpec(memory_space=pltpu.SMEM)] + [vmem] * len(rest),
        out_specs=[vmem] * len(outs),
        compiler_params=pltpu.CompilerParams(vmem_limit_bytes=32 * 2**20),
    )(owners, *rest)


def local(right_side, diag_inverse, off_blocks, columns, plan):
    rows, depth, width = right_side.shape
    doms = lax.axis_size("dom")
    levs = lax.axis_size("level")
    levels = levs // 2
    share = depth // levs
    count = 2 * rows
    dom = lax.axis_index("dom")
    lev = lax.axis_index("level")
    near_pairs = [(i, i ^ 1) for i in range(doms)]
    far_pairs = [(i, ((i + 1) ^ 1) - 1) for i in range(1, doms - 1)] + [(0, doms - 1), (doms - 1, 0)]

    weights = jnp.concatenate([diag_inverse[:, None], off_blocks], axis=1)
    weights = lax.all_gather(weights, "level")

    ids = jnp.arange(levs, dtype=jnp.int32)
    own_level = jnp.sum(jnp.where(ids == lev, plan, 0)) // 2
    inverse = jnp.sum(jnp.where(plan[None, :] == ids[:, None], ids[None, :], 0), axis=1)

    first = jnp.einsum("rkb,rbc->rkc", right_side, diag_inverse, preferred_element_type=F32)
    side = jnp.where(own_level == 0, first.astype(BF16), right_side)
    side = side.reshape(rows, levs, share, width)
    side = lax.all_to_all(side, "level", 1, 0, tiled=False)
    side = side.reshape(levs, rows * share, width)[inverse].reshape(levels, count * share, width)

    part = lax.dynamic_slice_in_dim(columns, dom * levs * rows, levs * rows, 0)
    part = part.reshape(levs, rows * 3)[inverse].reshape(levels, count, 3)
    source = plan[(part // rows) % levs] % 2 * rows + part % rows
    j = jnp.arange(count, dtype=jnp.int32)
    meets = source[:, :, :, None] == j
    eye_n = jnp.eye(3, dtype=bool)
    eye_n = jnp.where(dom % 2 == 0, eye_n, eye_n[::-1])
    eye_k = jnp.eye(share, dtype=bool)
    pick = (
        meets.transpose(0, 2, 1, 3)[:, :, :, None, None, :, None]
        & eye_n[None, :, None, None, :, None, None]
        & eye_k[None, None, None, :, None, None, :]
    )
    size = 3 * count * share
    pick = pick.reshape(levels, size, size).astype(BF16)
    spread = pick.transpose(0, 2, 1)

    vector = jax.ShapeDtypeStruct((count * share, width), BF16)
    summed = jax.ShapeDtypeStruct((count * share, width), F32)

    solved = [side[0]]
    for level in range(1, levels):
        own = solved[-1]
        far = lax.ppermute(own, "dom", far_pairs)
        near = lax.ppermute(own, "dom", near_pairs)
        kernel = functools.partial(forward_kernel, level, share)
        solved += call(kernel, [vector], inverse, weights, pick, side, far, own, near)

    zero = jnp.zeros(summed.shape, F32)
    far, own, near = zero, zero, zero
    results = []
    for level in range(levels - 1, -1, -1):
        last = level == 0
        kernel = functools.partial(backward_kernel, level, share, last)
        outs = [vector] if last else [vector, summed, summed, summed]
        result, *sums = call(
            kernel, outs, inverse, weights, spread, solved[level], far, own, near
        )
        results.append(result)
        if not last:
            far = lax.ppermute(sums[0], "dom", far_pairs)
            near = lax.ppermute(sums[2], "dom", near_pairs)
            own = sums[1]

    both = jnp.stack([jnp.stack(solved), jnp.stack(results[::-1])])
    both = both.reshape(2, levs, rows, share, width)[:, plan]
    both = lax.all_to_all(both, "level", 1, 0, tiled=False)
    both = both.transpose(1, 2, 0, 3, 4).reshape(2, rows, depth, width)
    return both[0], both[1]


def solution(mesh):
    return jax.shard_map(
        local,
        mesh=mesh,
        in_specs=(
            P(("dom", "level"), None, None),
            P(("dom", "level"), None, None),
            P(("dom", "level"), None, None, None),
            P(),
            P(),
        ),
        out_specs=(P(("dom", "level"), None, None), P(("dom", "level"), None, None)),
        check_vma=False,
    )
```

```python
import functools

import jax
import jax.numpy as jnp
from jax import lax
from jax.experimental import pallas as pl
from jax.experimental.pallas import tpu as pltpu
from jax.sharding import PartitionSpec as P

BF16 = jnp.bfloat16
F32 = jnp.float32


def dot(a, b):
    return lax.dot_general(a, b, (((1,), (0,)), ((), ())), preferred_element_type=F32)


def dot_t(a, b):
    return lax.dot_general(a, b, (((1,), (1,)), ((), ())), preferred_element_type=F32)


def either(low, high, share):
    top = lax.broadcasted_iota(jnp.int32, low.shape, 0) < share
    return jnp.where(top, low, high)


def forward_kernel(level, share, owners, weights, pick, side, far, own, near, out):
    rows = weights.shape[1]
    count = 2 * rows
    span = count * share
    around = jnp.concatenate([far[...], own[...], near[...]], axis=0)
    picked = dot(pick[level], around)
    for pair in range(count // 2):
        half, row = divmod(2 * pair, rows)
        owner = owners[2 * level + half]
        at = 2 * share * pair
        terms = [picked[n * span + at : n * span + at + 2 * share] for n in range(3)]
        terms = jnp.concatenate(terms, axis=1).astype(BF16)
        blocks = [weights[owner, row + one, 1:].reshape(-1, terms.shape[1] // 3) for one in range(2)]
        total = either(*[dot(terms, block) for block in blocks], share)
        shifted = (side[level, at : at + 2 * share].astype(F32) - total).astype(BF16)
        solved = either(*[dot(shifted, weights[owner, row + one, 0]) for one in range(2)], share)
        out[at : at + 2 * share] = solved.astype(BF16)


def backward_kernel(
    level, share, top, owners, weights, mates, spread, solved, solved_mate, held, came, result, *outs
):
    rows = weights.shape[1]
    count = 2 * rows
    span = count * share
    side = 2 * owners[owners.shape[0] - 1]
    side = side if level % 2 else 2 - side
    if not top:
        folded = (held[:span] + came[span:]).astype(BF16)
        folded_mate = (held[span:] + came[:span]).astype(BF16)
    pushes = [[], [], []]
    for pair in range(count // 2):
        half, row = divmod(2 * pair, rows)
        owner = owners[2 * level + half]
        at = slice(2 * share * pair, 2 * share * (pair + 1))

        def both(product, vector, blocks, kind):
            return either(*[product(vector, blocks[owner, row + one, kind]) for one in range(2)], share)

        done, done_mate = solved[at], solved_mate[at]
        if not top:
            done = (done.astype(F32) - both(dot, folded[at], weights, 0)).astype(BF16)
        result[at] = done
        if outs:
            if not top:
                done_mate = done_mate.astype(F32) - both(dot, folded_mate[at], mates, 0)
                done_mate = done_mate.astype(BF16)
            pushes[0].append(both(dot_t, done, weights, 2))
            pushes[1].append(both(dot_t, done_mate, mates, 1))
            pushes[2].append(both(dot_t, done, weights, 1 + side))
    if outs:
        pushed = jnp.concatenate(pushes[0] + pushes[1] + pushes[2], axis=0).astype(BF16)
        outs[0][...] = dot(spread[level], pushed)


def call(kernel, outs, owners, *rest):
    vmem = pl.BlockSpec(memory_space=pltpu.VMEM)
    return pl.pallas_call(
        kernel,
        out_shape=outs,
        in_specs=[pl.BlockSpec(memory_space=pltpu.SMEM)] + [vmem] * len(rest),
        out_specs=[vmem] * len(outs),
        compiler_params=pltpu.CompilerParams(vmem_limit_bytes=32 * 2**20),
    )(owners, *rest)


def local(right_side, diag_inverse, off_blocks, columns, plan):
    rows, depth, width = right_side.shape
    doms = lax.axis_size("dom")
    levs = lax.axis_size("level")
    levels = levs // 2
    share = depth // levs
    count = 2 * rows
    dom = lax.axis_index("dom")
    lev = lax.axis_index("level")
    near_pairs = [(i, i ^ 1) for i in range(doms)]
    far_pairs = [(i, ((i + 1) ^ 1) - 1) for i in range(1, doms - 1)] + [(0, doms - 1), (doms - 1, 0)]

    weights = jnp.concatenate([diag_inverse[:, None], off_blocks], axis=1)
    weights = lax.all_gather(weights, "level")

    turn = dom % 2
    ids = jnp.arange(levs, dtype=jnp.int32)
    own_level = jnp.sum(jnp.where(ids == lev, plan, 0)) // 2
    inverse = jnp.sum(jnp.where(plan[None, :] == ids[:, None], ids[None, :], 0), axis=1)
    owners = jnp.concatenate([inverse, turn[None]])

    here = jnp.where(own_level % 2 == turn, off_blocks[:, 0], off_blocks[:, 2])
    mates = jnp.stack([diag_inverse, here], axis=1)
    by_near = lax.ppermute(mates, "dom", near_pairs)
    by_far = lax.ppermute(mates, "dom", far_pairs)
    mates = jnp.where(own_level % 2 == 1, by_near, by_far)
    mates, weights = lax.optimization_barrier((mates, weights))
    mates = lax.all_gather(mates, "level")

    first = jnp.einsum("rkb,rbc->rkc", right_side, diag_inverse, preferred_element_type=F32)
    side = jnp.where(own_level == 0, first.astype(BF16), right_side)
    side = side.reshape(rows, levs, share, width)
    side = lax.all_to_all(side, "level", 1, 0, tiled=False)
    side = side.reshape(levs, rows * share, width)[inverse].reshape(levels, count * share, width)

    def sources(partition):
        part = lax.dynamic_slice_in_dim(columns, partition * levs * rows, levs * rows, 0)
        part = part.reshape(levs, rows * 3)[inverse].reshape(levels, count, 3)
        return plan[(part // rows) % levs] % 2 * rows + part % rows

    source = sources(dom)
    j = jnp.arange(count, dtype=jnp.int32)
    meets = source[:, :, :, None] == j
    eye_n = jnp.eye(3, dtype=bool)
    eye_n = jnp.where(turn == 0, eye_n, eye_n[::-1])
    eye_k = jnp.eye(share, dtype=bool)
    pick = (
        meets.transpose(0, 2, 1, 3)[:, :, :, None, None, :, None]
        & eye_n[None, :, None, None, :, None, None]
        & eye_k[None, None, None, :, None, None, :]
    )
    size = 3 * count * share
    pick = pick.reshape(levels, size, size).astype(BF16)

    odd = (jnp.arange(levels) % 2 == 1)[:, None]
    near_dom = dom + 1 - 2 * turn
    far_dom = (dom - 1 + 2 * turn) % doms
    ahead = jnp.where(odd == (turn == 0), 0, 2)

    def target(which):
        rises = (which[:, None, :] == j[None, :, None])[:, :, None, :, None]
        rises = rises & eye_k[None, None, :, None, :]
        return rises.reshape(levels, count * share, count * share).astype(BF16)

    source_mate = jnp.where(odd[..., None], sources(near_dom), sources(far_dom))
    own_own = target(source[..., 1])
    own_mate = target(jnp.where(ahead == 0, source[..., 0], source[..., 2]))
    mate_own = target(jnp.where(ahead == 0, source_mate[..., 0], source_mate[..., 2]))
    none = jnp.zeros_like(own_own)
    spread = jnp.concatenate(
        [
            jnp.concatenate([own_own, mate_own, none], axis=2),
            jnp.concatenate([none, none, own_mate], axis=2),
        ],
        axis=1,
    )

    vector = jax.ShapeDtypeStruct((count * share, width), BF16)
    summed = jax.ShapeDtypeStruct((2 * count * share, width), F32)

    solved = [side[0]]
    around = []
    for level in range(1, levels):
        own = solved[-1]
        far = lax.ppermute(own, "dom", far_pairs)
        near = lax.ppermute(own, "dom", near_pairs)
        around.append(near if level % 2 == 0 else far)
        kernel = functools.partial(forward_kernel, level, share)
        solved += call(kernel, [vector], owners, weights, pick, side, far, own, near)
    around.append(lax.ppermute(solved[-1], "dom", near_pairs))

    held = came = jnp.zeros(summed.shape, F32)
    results = []
    for level in range(levels - 1, -1, -1):
        kernel = functools.partial(backward_kernel, level, share, level == levels - 1)
        outs = [vector, summed] if level else [vector]
        result, *rest = call(
            kernel, outs, owners, weights, mates, spread, solved[level], around[level], held, came
        )
        results.append(result)
        if level:
            held = rest[0]
            came = lax.ppermute(held, "dom", far_pairs if level % 2 else near_pairs)

    both = jnp.stack([jnp.stack(solved), jnp.stack(results[::-1])])
    both = both.reshape(2, levs, rows, share, width)[:, plan]
    both = lax.all_to_all(both, "level", 1, 0, tiled=False)
    both = both.transpose(1, 2, 0, 3, 4).reshape(2, rows, depth, width)
    return both[0], both[1]


def solution(mesh):
    return jax.shard_map(
        local,
        mesh=mesh,
        in_specs=(
            P(("dom", "level"), None, None),
            P(("dom", "level"), None, None),
            P(("dom", "level"), None, None, None),
            P(),
            P(),
        ),
        out_specs=(P(("dom", "level"), None, None), P(("dom", "level"), None, None)),
        check_vma=False,
    )
```

```python
import functools

import jax
import jax.numpy as jnp
from jax import lax
from jax.experimental import pallas as pl
from jax.experimental.pallas import tpu as pltpu
from jax.sharding import PartitionSpec as P

BF16 = jnp.bfloat16
F32 = jnp.float32


def dot(a, b):
    return lax.dot_general(a, b, (((1,), (0,)), ((), ())), preferred_element_type=F32)


def dot_t(a, b):
    return lax.dot_general(a, b, (((1,), (1,)), ((), ())), preferred_element_type=F32)


def either(low, high, share):
    top = lax.broadcasted_iota(jnp.int32, low.shape, 0) < share
    return jnp.where(top, low, high)


def fetches(level, owners, source, held, sems):
    copies = []
    for pair in range(held.shape[0]):
        half, part = divmod(2 * pair, source.shape[1])
        rows = source.at[owners[2 * level + half], part : part + 2]
        copies.append(pltpu.make_async_copy(rows, held.at[pair], sems.at[pair]))
    for copy in copies:
        copy.start()
    return copies


def forward_kernel(level, share, owners, weights, pick, side, far, own, near, out, blocks, sems):
    copies = fetches(level, owners, weights, blocks, sems)
    span = out.shape[0]
    around = jnp.concatenate([far[...], own[...], near[...]], axis=0)
    picked = dot(pick[level], around)
    for pair in range(blocks.shape[0]):
        at = 2 * share * pair
        terms = [picked[n * span + at : n * span + at + 2 * share] for n in range(3)]
        terms = jnp.concatenate(terms, axis=1).astype(BF16)
        copies[pair].wait()
        wide = [blocks[pair, one, 1:].reshape(-1, out.shape[1]) for one in range(2)]
        total = either(*[dot(terms, block) for block in wide], share)
        shifted = (side[level, at : at + 2 * share].astype(F32) - total).astype(BF16)
        solved = either(*[dot(shifted, blocks[pair, one, 0]) for one in range(2)], share)
        out[at : at + 2 * share] = solved.astype(BF16)


def backward_kernel(
    level, share, top, owners, weights, mates, spread, solved, solved_mate, held, came, result, *rest
):
    *outs, blocks, blocks_mate, sems, sems_mate = rest
    copies = fetches(level, owners, weights, blocks, sems)
    if outs:
        copies_mate = fetches(level, owners, mates, blocks_mate, sems_mate)
    span = result.shape[0]
    side = 2 * owners[owners.shape[0] - 1]
    side = side if level % 2 else 2 - side
    if not top:
        folded = (held[:span] + came[span:]).astype(BF16)
        folded_mate = (held[span:] + came[:span]).astype(BF16)
    pushes = [[], [], []]
    for pair in range(blocks.shape[0]):
        at = slice(2 * share * pair, 2 * share * (pair + 1))

        def both(product, vector, source, kind):
            return either(*[product(vector, source[pair, one, kind]) for one in range(2)], share)

        done, done_mate = solved[at], solved_mate[at]
        copies[pair].wait()
        if not top:
            done = (done.astype(F32) - both(dot, folded[at], blocks, 0)).astype(BF16)
        result[at] = done
        if outs:
            pushes[0].append(both(dot_t, done, blocks, 2))
            pushes[2].append(both(dot_t, done, blocks, 1 + side))
            copies_mate[pair].wait()
            if not top:
                done_mate = done_mate.astype(F32) - both(dot, folded_mate[at], blocks_mate, 0)
                done_mate = done_mate.astype(BF16)
            pushes[1].append(both(dot_t, done_mate, blocks_mate, 1))
    if outs:
        pushed = jnp.concatenate(pushes[0] + pushes[1] + pushes[2], axis=0).astype(BF16)
        outs[0][...] = dot(spread[level], pushed)


def call(kernel, outs, owners, blocks, *rest):
    vmem = pl.BlockSpec(memory_space=pltpu.VMEM)
    hbm = pl.BlockSpec(memory_space=pltpu.HBM)
    pairs = blocks[0].shape[1]
    return pl.pallas_call(
        kernel,
        out_shape=outs,
        in_specs=[pl.BlockSpec(memory_space=pltpu.SMEM)] + [hbm] * len(blocks) + [vmem] * len(rest),
        out_specs=[vmem] * len(outs),
        scratch_shapes=[
            *[pltpu.VMEM((pairs, 2) + block.shape[2:], block.dtype) for block in blocks],
            *[pltpu.SemaphoreType.DMA((pairs,)) for _ in blocks],
        ],
        compiler_params=pltpu.CompilerParams(vmem_limit_bytes=8 * 2**20),
    )(owners, *[pltpu.with_memory_space_constraint(block, pltpu.HBM) for block in blocks], *rest)


def local(right_side, diag_inverse, off_blocks, columns, plan):
    rows, depth, width = right_side.shape
    doms = lax.axis_size("dom")
    levs = lax.axis_size("level")
    levels = levs // 2
    share = depth // levs
    count = 2 * rows
    dom = lax.axis_index("dom")
    lev = lax.axis_index("level")
    near_pairs = [(i, i ^ 1) for i in range(doms)]
    far_pairs = [(i, ((i + 1) ^ 1) - 1) for i in range(1, doms - 1)] + [(0, doms - 1), (doms - 1, 0)]

    weights = jnp.concatenate([diag_inverse[:, None], off_blocks], axis=1)
    weights = lax.all_gather(weights, "level")

    turn = dom % 2
    ids = jnp.arange(levs, dtype=jnp.int32)
    own_level = jnp.sum(jnp.where(ids == lev, plan, 0)) // 2
    inverse = jnp.sum(jnp.where(plan[None, :] == ids[:, None], ids[None, :], 0), axis=1)
    owners = jnp.concatenate([inverse, turn[None]])

    here = jnp.where(own_level % 2 == turn, off_blocks[:, 0], off_blocks[:, 2])
    mates = jnp.stack([diag_inverse, here], axis=1)
    by_near = lax.ppermute(mates, "dom", near_pairs)
    by_far = lax.ppermute(mates, "dom", far_pairs)
    mates = jnp.where(own_level % 2 == 1, by_near, by_far)

    first = jnp.einsum("rkb,rbc->rkc", right_side, diag_inverse, preferred_element_type=F32)
    side = jnp.where(own_level == 0, first.astype(BF16), right_side)
    side = side.reshape(rows, levs, share, width)
    side = lax.all_to_all(side, "level", 1, 0, tiled=False)
    side = side.reshape(levs, rows * share, width)[inverse].reshape(levels, count * share, width)

    def sources(partition):
        part = lax.dynamic_slice_in_dim(columns, partition * levs * rows, levs * rows, 0)
        part = part.reshape(levs, rows * 3)[inverse].reshape(levels, count, 3)
        return plan[(part // rows) % levs] % 2 * rows + part % rows

    source = sources(dom)
    j = jnp.arange(count, dtype=jnp.int32)
    meets = source[:, :, :, None] == j
    eye_n = jnp.eye(3, dtype=bool)
    eye_n = jnp.where(turn == 0, eye_n, eye_n[::-1])
    eye_k = jnp.eye(share, dtype=bool)
    pick = (
        meets.transpose(0, 2, 1, 3)[:, :, :, None, None, :, None]
        & eye_n[None, :, None, None, :, None, None]
        & eye_k[None, None, None, :, None, None, :]
    )
    size = 3 * count * share
    pick = pick.reshape(levels, size, size).astype(BF16)

    odd = (jnp.arange(levels) % 2 == 1)[:, None]
    near_dom = dom + 1 - 2 * turn
    far_dom = (dom - 1 + 2 * turn) % doms
    ahead = jnp.where(odd == (turn == 0), 0, 2)

    def target(which):
        rises = (which[:, None, :] == j[None, :, None])[:, :, None, :, None]
        rises = rises & eye_k[None, None, :, None, :]
        return rises.reshape(levels, count * share, count * share).astype(BF16)

    source_mate = jnp.where(odd[..., None], sources(near_dom), sources(far_dom))
    own_own = target(source[..., 1])
    own_mate = target(jnp.where(ahead == 0, source[..., 0], source[..., 2]))
    mate_own = target(jnp.where(ahead == 0, source_mate[..., 0], source_mate[..., 2]))
    none = jnp.zeros_like(own_own)
    spread = jnp.concatenate(
        [
            jnp.concatenate([own_own, mate_own, none], axis=2),
            jnp.concatenate([none, none, own_mate], axis=2),
        ],
        axis=1,
    )

    vector = jax.ShapeDtypeStruct((count * share, width), BF16)
    summed = jax.ShapeDtypeStruct((2 * count * share, width), F32)

    solved = [side[0]]
    around = []
    for level in range(1, levels):
        own = solved[-1]
        far = lax.ppermute(own, "dom", far_pairs)
        near = lax.ppermute(own, "dom", near_pairs)
        if level == 1:
            mates, far, near = lax.optimization_barrier((mates, far, near))
            mates = lax.all_gather(mates, "level")
        around.append(near if level % 2 == 0 else far)
        kernel = functools.partial(forward_kernel, level, share)
        solved += call(kernel, [vector], owners, [weights], pick, side, far, own, near)
    around.append(lax.ppermute(solved[-1], "dom", near_pairs))

    held = came = jnp.zeros(summed.shape, F32)
    results = []
    for level in range(levels - 1, -1, -1):
        kernel = functools.partial(backward_kernel, level, share, level == levels - 1)
        outs = [vector, summed] if level else [vector]
        result, *rest = call(
            kernel, outs, owners, [weights, mates], spread, solved[level], around[level], held, came
        )
        results.append(result)
        if level:
            held = rest[0]
            came = lax.ppermute(held, "dom", far_pairs if level % 2 else near_pairs)

    both = jnp.stack([jnp.stack(solved), jnp.stack(results[::-1])])
    both = both.reshape(2, levs, rows, share, width)[:, plan]
    both = lax.all_to_all(both, "level", 1, 0, tiled=False)
    both = both.transpose(1, 2, 0, 3, 4).reshape(2, rows, depth, width)
    return both[0], both[1]


def solution(mesh):
    return jax.shard_map(
        local,
        mesh=mesh,
        in_specs=(
            P(("dom", "level"), None, None),
            P(("dom", "level"), None, None),
            P(("dom", "level"), None, None, None),
            P(),
            P(),
        ),
        out_specs=(P(("dom", "level"), None, None), P(("dom", "level"), None, None)),
        check_vma=False,
    )
```

```python
import functools

import jax
import jax.numpy as jnp
from jax import lax
from jax.experimental import pallas as pl
from jax.experimental.pallas import tpu as pltpu
from jax.sharding import PartitionSpec as P

BF16 = jnp.bfloat16
F32 = jnp.float32


def dot(a, b):
    return lax.dot_general(a, b, (((1,), (0,)), ((), ())), preferred_element_type=F32)


def dot_t(a, b):
    return lax.dot_general(a, b, (((1,), (1,)), ((), ())), preferred_element_type=F32)


def either(low, high, share):
    top = lax.broadcasted_iota(jnp.int32, low.shape, 0) < share
    return jnp.where(top, low, high)


def ones_where(condition):
    return jnp.where(condition, 1.0, 0.0).astype(BF16)


def forward_kernel(level, share, owners, weights, places, side, far, own, near, out):
    rows = weights.shape[1]
    span = out.shape[0]
    around = jnp.concatenate([far[...], own[...], near[...]], axis=0)
    at = lax.broadcasted_iota(jnp.int32, (3 * span, 3 * span), 1)
    picked = dot(ones_where(at == places[level]), around)
    for pair in range(rows):
        half, row = divmod(2 * pair, rows)
        owner = owners[2 * level + half]
        at = 2 * share * pair
        terms = [picked[n * span + at : n * span + at + 2 * share] for n in range(3)]
        terms = jnp.concatenate(terms, axis=1).astype(BF16)
        wide = [weights[owner, row + one, 1:].reshape(-1, out.shape[1]) for one in range(2)]
        total = either(*[dot(terms, block) for block in wide], share)
        shifted = (side[level, at : at + 2 * share].astype(F32) - total).astype(BF16)
        solved = either(*[dot(shifted, weights[owner, row + one, 0]) for one in range(2)], share)
        out[at : at + 2 * share] = solved.astype(BF16)


def backward_kernel(level, share, top, owners, weights, mates, targets, solved, solved_mate, *rest):
    if top:
        result, *outs = rest
    else:
        held, came, result, *outs = rest
    rows = weights.shape[1]
    span = result.shape[0]
    side = 2 * owners[owners.shape[0] - 1]
    side = side if level % 2 else 2 - side
    if not top:
        folded = (held[:span] + came[span:]).astype(BF16)
        folded_mate = (held[span:] + came[:span]).astype(BF16)
    pushes = [[], [], []]
    for pair in range(rows):
        half, row = divmod(2 * pair, rows)
        owner = owners[2 * level + half]
        at = slice(2 * share * pair, 2 * share * (pair + 1))

        def both(product, vector, blocks, kind):
            return either(*[product(vector, blocks[owner, row + one, kind]) for one in range(2)], share)

        done, done_mate = solved[at], solved_mate[at]
        if not top:
            done = (done.astype(F32) - both(dot, folded[at], weights, 0)).astype(BF16)
        result[at] = done
        if outs:
            if not top:
                done_mate = done_mate.astype(F32) - both(dot, folded_mate[at], mates, 0)
                done_mate = done_mate.astype(BF16)
            pushes[0].append(both(dot_t, done, weights, 2))
            pushes[1].append(both(dot_t, done_mate, mates, 1))
            pushes[2].append(both(dot_t, done, weights, 1 + side))
    if outs:
        pushed = jnp.concatenate(pushes[0] + pushes[1] + pushes[2], axis=0).astype(BF16)
        to = lax.broadcasted_iota(jnp.int32, (2 * span, 3 * span), 0)
        outs[0][...] = dot(ones_where(to == targets[level]), pushed)


def call(kernel, outs, owners, *rest):
    vmem = pl.BlockSpec(memory_space=pltpu.VMEM)
    return pl.pallas_call(
        kernel,
        out_shape=outs,
        in_specs=[pl.BlockSpec(memory_space=pltpu.SMEM)] + [vmem] * len(rest),
        out_specs=[vmem] * len(outs),
        compiler_params=pltpu.CompilerParams(vmem_limit_bytes=16 * 2**20),
    )(owners, *rest)


def local(right_side, diag_inverse, off_blocks, columns, plan):
    rows, depth, width = right_side.shape
    doms = lax.axis_size("dom")
    levs = lax.axis_size("level")
    levels = levs // 2
    share = depth // levs
    count = 2 * rows
    dom = lax.axis_index("dom")
    lev = lax.axis_index("level")
    near_pairs = [(i, i ^ 1) for i in range(doms)]
    far_pairs = [(i, ((i + 1) ^ 1) - 1) for i in range(1, doms - 1)] + [(0, doms - 1), (doms - 1, 0)]

    weights = jnp.concatenate([diag_inverse[:, None], off_blocks], axis=1)
    weights = lax.all_gather(weights, "level")

    turn = dom % 2
    ids = jnp.arange(levs, dtype=jnp.int32)
    own_level = jnp.sum(jnp.where(ids == lev, plan, 0)) // 2
    inverse = jnp.sum(jnp.where(plan[None, :] == ids[:, None], ids[None, :], 0), axis=1)
    owners = jnp.concatenate([inverse, turn[None]])

    here = jnp.where(own_level % 2 == turn, off_blocks[:, 0], off_blocks[:, 2])
    mates = jnp.stack([diag_inverse, here], axis=1)
    by_near = lax.ppermute(mates, "dom", near_pairs)
    by_far = lax.ppermute(mates, "dom", far_pairs)
    mates = jnp.where(own_level % 2 == 1, by_near, by_far)
    first = jnp.einsum("rkb,rbc->rkc", right_side, diag_inverse, preferred_element_type=F32)
    side = jnp.where(own_level == 0, first.astype(BF16), right_side)
    side = side.reshape(rows, levs, share, width)
    side = lax.all_to_all(side, "level", 1, 0, tiled=False)
    side = side.reshape(levs, rows * share, width)[inverse].reshape(levels, count * share, width)

    near_dom = dom + 1 - 2 * turn
    far_dom = (dom - 1 + 2 * turn) % doms
    part = jnp.stack(
        [
            lax.dynamic_slice_in_dim(columns, which * levs * rows, levs * rows, 0)
            for which in (dom, near_dom, far_dom)
        ]
    )
    part = part.reshape(3, levs, rows * 3)[:, inverse].reshape(3, levels, count, 3)
    second = jnp.roll(inverse[1::2], 1)[None, :, None, None]
    meets = jnp.where(part // rows % levs == second, rows, 0) + part % rows
    odd = (jnp.arange(levels) % 2 == 1)[:, None]
    meets_own = meets[0]
    meets_mate = jnp.where(odd[..., None], meets[1], meets[2])
    ahead = odd == (turn == 0)
    own_mate = jnp.where(ahead, meets_own[..., 0], meets_own[..., 2])
    mate_own = jnp.where(ahead, meets_mate[..., 0], meets_mate[..., 2])
    k = jnp.arange(share, dtype=jnp.int32)
    span = count * share
    slot = jnp.where(turn == 0, 1, -1) * (jnp.arange(3, dtype=jnp.int32) - 1) + 1
    places = meets_own.transpose(0, 2, 1) * share + slot[None, :, None] * span
    places = (places[..., None] + k).reshape(levels, 3 * span, 1)
    targets = jnp.stack([meets_own[..., 1], mate_own, own_mate + count], axis=1) * share
    targets = (targets[..., None] + k).reshape(levels, 1, 3 * span)

    vector = jax.ShapeDtypeStruct((count * share, width), BF16)
    summed = jax.ShapeDtypeStruct((2 * count * share, width), F32)

    own = side[0]
    far = lax.ppermute(own, "dom", far_pairs)
    near = lax.ppermute(own, "dom", near_pairs)
    mates, owners, side, places, targets, own, far, near = lax.optimization_barrier(
        (mates, owners, side, places, targets, own, far, near)
    )
    mates = lax.all_gather(mates, "level")

    solved = [own]
    around = []
    for level in range(1, levels):
        if level > 1:
            own = solved[-1]
            if level == levels - 1:
                own, mates = lax.optimization_barrier((own, mates))
                solved[-1] = own
            far = lax.ppermute(own, "dom", far_pairs)
            near = lax.ppermute(own, "dom", near_pairs)
        around.append(near if level % 2 == 0 else far)
        kernel = functools.partial(forward_kernel, level, share)
        solved += call(kernel, [vector], owners, weights, places, side, far, own, near)
    around.append(lax.ppermute(solved[-1], "dom", near_pairs))

    flow = []
    results = []
    for level in range(levels - 1, -1, -1):
        kernel = functools.partial(backward_kernel, level, share, level == levels - 1)
        outs = [vector, summed] if level else [vector]
        result, *rest = call(
            kernel, outs, owners, weights, mates, targets, solved[level], around[level], *flow
        )
        results.append(result)
        if level:
            held = rest[0]
            flow = [held, lax.ppermute(held, "dom", far_pairs if level % 2 else near_pairs)]

    both = jnp.stack([jnp.stack(solved), jnp.stack(results[::-1])])
    both = both.reshape(2, levs, rows, share, width)[:, plan]
    both = lax.all_to_all(both, "level", 1, 0, tiled=False)
    both = both.transpose(1, 2, 0, 3, 4).reshape(2, rows, depth, width)
    return both[0], both[1]


def solution(mesh):
    return jax.shard_map(
        local,
        mesh=mesh,
        in_specs=(
            P(("dom", "level"), None, None),
            P(("dom", "level"), None, None),
            P(("dom", "level"), None, None, None),
            P(),
            P(),
        ),
        out_specs=(P(("dom", "level"), None, None), P(("dom", "level"), None, None)),
        check_vma=False,
    )
```

```python
import functools

import jax
import jax.numpy as jnp
from jax import lax
from jax.experimental import pallas as pl
from jax.experimental.pallas import tpu as pltpu
from jax.sharding import PartitionSpec as P

BF16 = jnp.bfloat16
F32 = jnp.float32


def dot(a, b):
    return lax.dot_general(a, b, (((1,), (0,)), ((), ())), preferred_element_type=F32)


def dot_t(a, b):
    return lax.dot_general(a, b, (((1,), (1,)), ((), ())), preferred_element_type=F32)


def either(low, high, share):
    top = lax.broadcasted_iota(jnp.int32, low.shape, 0) < share
    return jnp.where(top, low, high)


def ones_where(condition):
    return jnp.where(condition, 1.0, 0.0).astype(BF16)


BITS = 8


def unpack(packed, level):
    value = jnp.max(packed[level : level + 1])
    mask = (1 << BITS) - 1
    return value & mask, (value >> BITS) & mask, value >> (2 * BITS)


def products(product, share, owners, vectors, blocks, kind):
    rows = blocks.shape[1]
    totals = []
    for pair in range(rows):
        half, row = divmod(2 * pair, rows)
        part = vectors[2 * share * pair : 2 * share * (pair + 1)]
        wide = [blocks[owners[half], row + one, kind] for one in range(2)]
        if isinstance(kind, slice):
            wide = [block.reshape(-1, block.shape[-1]) for block in wide]
        totals.append(either(*[product(part, block) for block in wide], share))
    return jnp.concatenate(totals, axis=0)


def forward_kernel(level, share, packed, weights, places, side, far, own, near, out):
    *owners, _ = unpack(packed, level)
    span = out.shape[0]
    around = jnp.concatenate([far[...], own[...], near[...]], axis=0)
    at = lax.broadcasted_iota(jnp.int32, (3 * span, 3 * span), 1)
    picked = dot(ones_where(at == places[level]), around)
    picked = jnp.concatenate([picked[n * span : (n + 1) * span] for n in range(3)], axis=1)
    total = products(dot, share, owners, picked.astype(BF16), weights, slice(1, None))
    shifted = (side[level].astype(F32) - total).astype(BF16)
    out[...] = products(dot, share, owners, shifted, weights, 0).astype(BF16)


def backward_kernel(level, share, top, packed, weights, mates, targets, solved, solved_mate, *rest):
    if top:
        result, *outs = rest
    else:
        held, came, result, *outs = rest
    *owners, side = unpack(packed, level)
    span = result.shape[0]
    done, done_mate = solved[...], solved_mate[...]
    if not top:
        folded = (held[:span] + came[span:]).astype(BF16)
        done = done.astype(F32) - products(dot, share, owners, folded, weights, 0)
        done = done.astype(BF16)
    result[...] = done
    if not outs:
        return
    if not top:
        folded = (held[span:] + came[:span]).astype(BF16)
        done_mate = done_mate.astype(F32) - products(dot, share, owners, folded, mates, 0)
        done_mate = done_mate.astype(BF16)
    pushed = [
        products(dot_t, share, owners, done, weights, 2),
        products(dot_t, share, owners, done_mate, mates, 1),
        products(dot_t, share, owners, done, weights, 1 + side),
    ]
    pushed = jnp.concatenate(pushed, axis=0).astype(BF16)
    to = lax.broadcasted_iota(jnp.int32, (2 * span, 3 * span), 0)
    outs[0][...] = dot(ones_where(to == targets[level]), pushed)


def call(kernel, outs, *args):
    vmem = pl.BlockSpec(memory_space=pltpu.VMEM)
    return pl.pallas_call(
        kernel,
        out_shape=outs,
        in_specs=[vmem] * len(args),
        out_specs=[vmem] * len(outs),
        compiler_params=pltpu.CompilerParams(vmem_limit_bytes=16 * 2**20),
    )(*args)


def local(right_side, diag_inverse, off_blocks, columns, plan):
    rows, depth, width = right_side.shape
    doms = lax.axis_size("dom")
    levs = lax.axis_size("level")
    levels = levs // 2
    share = depth // levs
    count = 2 * rows
    dom = lax.axis_index("dom")
    lev = lax.axis_index("level")
    near_pairs = [(i, i ^ 1) for i in range(doms)]
    far_pairs = [(i, ((i + 1) ^ 1) - 1) for i in range(1, doms - 1)] + [(0, doms - 1), (doms - 1, 0)]

    weights = jnp.concatenate([diag_inverse[:, None], off_blocks], axis=1)
    weights = lax.all_gather(weights, "level")

    turn = dom % 2
    ids = jnp.arange(levs, dtype=jnp.int32)
    own_level = jnp.sum(jnp.where(ids == lev, plan, 0)) // 2
    inverse = jnp.sum(jnp.where(plan[None, :] == ids[:, None], ids[None, :], 0), axis=1)
    side_of = jnp.where(jnp.arange(levels) % 2 == 1, 2 * turn, 2 - 2 * turn)
    packed = inverse[0::2] + (inverse[1::2] << BITS) + (side_of << (2 * BITS))
    packed = jnp.broadcast_to(packed[:, None], (levels, 128)).astype(jnp.int32)

    here = jnp.where(own_level % 2 == turn, off_blocks[:, 0], off_blocks[:, 2])
    mates = jnp.stack([diag_inverse, here], axis=1)
    by_near = lax.ppermute(mates, "dom", near_pairs)
    by_far = lax.ppermute(mates, "dom", far_pairs)
    mates = jnp.where(own_level % 2 == 1, by_near, by_far)
    first = jnp.einsum("rkb,rbc->rkc", right_side, diag_inverse, preferred_element_type=F32)
    side = jnp.where(own_level == 0, first.astype(BF16), right_side)
    side = side.reshape(rows, levs, share, width)
    side = lax.all_to_all(side, "level", 1, 0, tiled=False)
    side = side.reshape(levs, rows * share, width)[inverse].reshape(levels, count * share, width)

    near_dom = dom + 1 - 2 * turn
    far_dom = (dom - 1 + 2 * turn) % doms
    part = jnp.stack(
        [
            lax.dynamic_slice_in_dim(columns, which * levs * rows, levs * rows, 0)
            for which in (dom, near_dom, far_dom)
        ]
    )
    part = part.reshape(3, levs, rows * 3)[:, inverse].reshape(3, levels, count, 3)
    second = jnp.roll(inverse[1::2], 1)[None, :, None, None]
    meets = jnp.where(part // rows % levs == second, rows, 0) + part % rows
    odd = (jnp.arange(levels) % 2 == 1)[:, None]
    meets_own = meets[0]
    meets_mate = jnp.where(odd[..., None], meets[1], meets[2])
    ahead = odd == (turn == 0)
    own_mate = jnp.where(ahead, meets_own[..., 0], meets_own[..., 2])
    mate_own = jnp.where(ahead, meets_mate[..., 0], meets_mate[..., 2])
    k = jnp.arange(share, dtype=jnp.int32)
    span = count * share
    slot = jnp.where(turn == 0, 1, -1) * (jnp.arange(3, dtype=jnp.int32) - 1) + 1
    places = meets_own.transpose(0, 2, 1) * share + slot[None, :, None] * span
    places = (places[..., None] + k).reshape(levels, 3 * span, 1)
    targets = jnp.stack([meets_own[..., 1], mate_own, own_mate + count], axis=1) * share
    targets = (targets[..., None] + k).reshape(levels, 1, 3 * span)

    vector = jax.ShapeDtypeStruct((count * share, width), BF16)
    summed = jax.ShapeDtypeStruct((2 * count * share, width), F32)

    own = side[0]
    far = lax.ppermute(own, "dom", far_pairs)
    near = lax.ppermute(own, "dom", near_pairs)
    mates, packed, side, places, targets, own, far, near = lax.optimization_barrier(
        (mates, packed, side, places, targets, own, far, near)
    )
    mates = lax.all_gather(mates, "level")

    solved = [own]
    around = []
    for level in range(1, levels):
        if level > 1:
            own = solved[-1]
            far = lax.ppermute(own, "dom", far_pairs)
            near = lax.ppermute(own, "dom", near_pairs)
        around.append(near if level % 2 == 0 else far)
        kernel = functools.partial(forward_kernel, level, share)
        solved += call(kernel, [vector], packed, weights, places, side, far, own, near)
    solved[-1], mates = lax.optimization_barrier((solved[-1], mates))
    around.append(lax.ppermute(solved[-1], "dom", near_pairs))

    flow = []
    results = []
    for level in range(levels - 1, -1, -1):
        kernel = functools.partial(backward_kernel, level, share, level == levels - 1)
        outs = [vector, summed] if level else [vector]
        result, *rest = call(
            kernel, outs, packed, weights, mates, targets, solved[level], around[level], *flow
        )
        results.append(result)
        if level:
            held = rest[0]
            flow = [held, lax.ppermute(held, "dom", far_pairs if level % 2 else near_pairs)]

    both = jnp.stack([jnp.stack(solved), jnp.stack(results[::-1])])
    both = both.reshape(2, levs, rows, share, width)[:, plan]
    both = lax.all_to_all(both, "level", 1, 0, tiled=False)
    both = both.transpose(1, 2, 0, 3, 4).reshape(2, rows, depth, width)
    return both[0], both[1]


def solution(mesh):
    return jax.shard_map(
        local,
        mesh=mesh,
        in_specs=(
            P(("dom", "level"), None, None),
            P(("dom", "level"), None, None),
            P(("dom", "level"), None, None, None),
            P(),
            P(),
        ),
        out_specs=(P(("dom", "level"), None, None), P(("dom", "level"), None, None)),
        check_vma=False,
    )
```

```python
import functools

import jax
import jax.numpy as jnp
from jax import lax
from jax.experimental import pallas as pl
from jax.experimental.pallas import tpu as pltpu
from jax.sharding import PartitionSpec as P

BF16 = jnp.bfloat16
F32 = jnp.float32


def dot(a, b):
    return lax.dot_general(a, b, (((1,), (0,)), ((), ())), preferred_element_type=F32)


def dot_t(a, b):
    return lax.dot_general(a, b, (((1,), (1,)), ((), ())), preferred_element_type=F32)


def either(low, high, share):
    top = lax.broadcasted_iota(jnp.int32, low.shape, 0) < share
    return jnp.where(top, low, high)


def ones_where(condition):
    return jnp.where(condition, 1.0, 0.0).astype(BF16)


BITS = 8


def unpack(packed, level):
    value = jnp.max(packed[level : level + 1])
    mask = (1 << BITS) - 1
    return value & mask, (value >> BITS) & mask, value >> (2 * BITS)


def products(product, share, owners, vectors, blocks, kind):
    rows = blocks.shape[1]
    totals = []
    for pair in range(rows):
        half, row = divmod(2 * pair, rows)
        part = vectors[2 * share * pair : 2 * share * (pair + 1)]
        wide = [blocks[owners[half], row + one, kind] for one in range(2)]
        if isinstance(kind, slice):
            wide = [block.reshape(-1, block.shape[-1]) for block in wide]
        totals.append(either(*[product(part, block) for block in wide], share))
    return jnp.concatenate(totals, axis=0)


def picked_from(places, around):
    at = lax.broadcasted_iota(jnp.int32, (places.shape[0], around.shape[0]), 1)
    return dot(ones_where(at == places), around)


def forward_kernel(level, share, fetched, packed, weights, places, side, far, own, near, out, *held):
    *owners, _ = unpack(packed, level)
    if fetched:
        held, sems = held
        copies = [
            pltpu.make_async_copy(weights.at[owners[half]], held.at[half], sems.at[half])
            for half in range(2)
        ]
        for copy in copies:
            copy.start()
    span = out.shape[0]
    picked = picked_from(places[level], jnp.concatenate([far[...], own[...], near[...]], axis=0))
    picked = jnp.concatenate([picked[n * span : (n + 1) * span] for n in range(3)], axis=1)
    if fetched:
        for copy in copies:
            copy.wait()
        owners, weights = range(2), held
    total = products(dot, share, owners, picked.astype(BF16), weights, slice(1, None))
    shifted = (side[level].astype(F32) - total).astype(BF16)
    out[...] = products(dot, share, owners, shifted, weights, 0).astype(BF16)


def gathered_sums(level, share, packed, weights, mates, places, own, mate):
    *owners, side = unpack(packed, level)
    span = own.shape[0]
    picked = picked_from(places[level], jnp.concatenate([own, mate], axis=0)).astype(BF16)
    sums = products(dot, share, owners, picked[:span], weights, 2)
    sums += products(dot, share, owners, picked[2 * span :], weights, 1 + side)
    sums_mate = products(dot, share, owners, picked[span : 2 * span], mates, 1)
    return jnp.concatenate([sums, sums_mate], axis=0)


def pushed_sums(level, share, packed, weights, mates, targets, own, mate):
    *owners, side = unpack(packed, level)
    span = own.shape[0]
    pushed = [
        products(dot_t, share, owners, own, weights, 2),
        products(dot_t, share, owners, mate, mates, 1),
        products(dot_t, share, owners, own, weights, 1 + side),
    ]
    pushed = jnp.concatenate(pushed, axis=0).astype(BF16)
    to = lax.broadcasted_iota(jnp.int32, (2 * span, 3 * span), 0)
    return dot(ones_where(to == targets[level]), pushed)


def pass_on(sums, held, sent):
    held[...] = sums
    sent[...] = sums.astype(BF16)


def joined(held, came):
    span = held.shape[0] // 2
    came = came[...].astype(F32)
    return held[:span] + came[span:], held[span:] + came[:span]


def entry_kernel(level, share, packed, weights, mates, meets, own, mate, held, sent):
    sums = gathered_sums(level, share, packed, weights, mates, meets, own[...], mate[...])
    pass_on(sums, held, sent)


def forward_pair_kernel(
    level, share, last, packed, weights, mates, meets, targets, side, side_mate, held, came,
    solved, solved_mate, to_hold, to_send,
):
    *owners, _ = unpack(packed, level)
    pair = []
    for total, right, blocks in zip(joined(held, came), (side[level], side_mate[...]), (weights, mates)):
        shifted = (right.astype(F32) - total).astype(BF16)
        pair.append(products(dot, share, owners, shifted, blocks, 0).astype(BF16))
    solved[...], solved_mate[...] = pair
    if last:
        sums = pushed_sums(level, share, packed, weights, mates, targets, *pair)
    else:
        sums = gathered_sums(level + 1, share, packed, weights, mates, meets, *pair)
    pass_on(sums, to_hold, to_send)


def backward_kernel(
    level, share, packed, weights, mates, targets, solved, solved_mate, held, came, result, *outs
):
    *owners, _ = unpack(packed, level)
    pair = []
    for total, vector, blocks in zip(joined(held, came), (solved, solved_mate), (weights, mates)):
        part = products(dot, share, owners, total.astype(BF16), blocks, 0)
        pair.append((vector[...].astype(F32) - part).astype(BF16))
        if not outs:
            break
    result[...] = pair[0]
    if outs:
        pass_on(pushed_sums(level, share, packed, weights, mates, targets, *pair), *outs)


def call(kernel, outs, packed, weights, *rest, fetched=False):
    vmem = pl.BlockSpec(memory_space=pltpu.VMEM)
    specs = [vmem] * (2 + len(rest))
    scratch = []
    if fetched:
        specs[1] = pl.BlockSpec(memory_space=pltpu.HBM)
        weights = pltpu.with_memory_space_constraint(weights, pltpu.HBM)
        scratch = [pltpu.VMEM((2,) + weights.shape[1:], weights.dtype), pltpu.SemaphoreType.DMA((2,))]
    return pl.pallas_call(
        kernel,
        out_shape=outs,
        in_specs=specs,
        out_specs=[vmem] * len(outs),
        scratch_shapes=scratch,
        compiler_params=pltpu.CompilerParams(vmem_limit_bytes=16 * 2**20),
    )(packed, weights, *rest)


def local(right_side, diag_inverse, off_blocks, columns, plan):
    rows, depth, width = right_side.shape
    doms = lax.axis_size("dom")
    levs = lax.axis_size("level")
    levels = levs // 2
    share = depth // levs
    count = 2 * rows
    dom = lax.axis_index("dom")
    lev = lax.axis_index("level")
    near_pairs = [(i, i ^ 1) for i in range(doms)]
    far_pairs = [(i, ((i + 1) ^ 1) - 1) for i in range(1, doms - 1)] + [(0, doms - 1), (doms - 1, 0)]

    weights = jnp.concatenate([diag_inverse[:, None], off_blocks], axis=1)
    weights = lax.all_gather(weights, "level")

    turn = dom % 2
    ids = jnp.arange(levs, dtype=jnp.int32)
    own_level = jnp.sum(jnp.where(ids == lev, plan, 0)) // 2
    inverse = jnp.sum(jnp.where(plan[None, :] == ids[:, None], ids[None, :], 0), axis=1)
    side_of = jnp.where(jnp.arange(levels) % 2 == 1, 2 * turn, 2 - 2 * turn)
    packed = inverse[0::2] + (inverse[1::2] << BITS) + (side_of << (2 * BITS))
    packed = jnp.broadcast_to(packed[:, None], (levels, 128)).astype(jnp.int32)

    here = jnp.where(own_level % 2 == turn, off_blocks[:, 0], off_blocks[:, 2])
    mates = jnp.stack([diag_inverse, here], axis=1)
    by_near = lax.ppermute(mates, "dom", near_pairs)
    by_far = lax.ppermute(mates, "dom", far_pairs)
    mates = jnp.where(own_level % 2 == 1, by_near, by_far)
    first = jnp.einsum("rkb,rbc->rkc", right_side, diag_inverse, preferred_element_type=F32)
    side = jnp.where(own_level == 0, first.astype(BF16), right_side)
    side = side.reshape(rows, levs, share, width)
    side = lax.all_to_all(side, "level", 1, 0, tiled=False)
    side = side.reshape(levs, rows * share, width)[inverse].reshape(levels, count * share, width)

    near_dom = dom + 1 - 2 * turn
    far_dom = (dom - 1 + 2 * turn) % doms
    part = jnp.stack(
        [
            lax.dynamic_slice_in_dim(columns, which * levs * rows, levs * rows, 0)
            for which in (dom, near_dom, far_dom)
        ]
    )
    part = part.reshape(3, levs, rows * 3)[:, inverse].reshape(3, levels, count, 3)
    second = jnp.roll(inverse[1::2], 1)[None, :, None, None]
    met = jnp.where(part // rows % levs == second, rows, 0) + part % rows
    odd = (jnp.arange(levels) % 2 == 1)[:, None]
    meets_own = met[0]
    meets_mate = jnp.where(odd[..., None], met[1], met[2])
    ahead = odd == (turn == 0)
    own_mate = jnp.where(ahead, meets_own[..., 0], meets_own[..., 2])
    mate_own = jnp.where(ahead, meets_mate[..., 0], meets_mate[..., 2])
    k = jnp.arange(share, dtype=jnp.int32)
    span = count * share
    slot = jnp.where(turn == 0, 1, -1) * (jnp.arange(3, dtype=jnp.int32) - 1) + 1
    places = meets_own.transpose(0, 2, 1) * share + slot[None, :, None] * span
    places = (places[..., None] + k).reshape(levels, 3 * span, 1)
    targets = jnp.stack([meets_own[..., 1], mate_own, own_mate + count], axis=1) * share
    targets = (targets[..., None] + k).reshape(levels, 3 * span)
    targets, meets = targets[:, None, :], targets[:, :, None]

    vector = jax.ShapeDtypeStruct((count * share, width), BF16)
    sums = [jax.ShapeDtypeStruct((2 * span, width), kind) for kind in (F32, BF16)]
    paired = levels - 2

    own = side[0]
    far = lax.ppermute(jnp.stack([own, side[paired]]), "dom", far_pairs)
    near = lax.ppermute(jnp.stack([own, side[paired + 1]]), "dom", near_pairs)
    mates, packed, side, places, targets, meets, own, far, near = lax.optimization_barrier(
        (mates, packed, side, places, targets, meets, own, far, near)
    )
    side_mates = [far[1], near[1]]
    far, near = far[0], near[0]
    mates = lax.all_gather(mates, "level")

    def swap(vector, level):
        return lax.ppermute(vector, "dom", far_pairs if level % 2 == 0 else near_pairs)

    solved = [own]
    solved_mate = []
    for level in range(1, paired):
        if level > 1:
            own = solved[-1]
            far, near = swap(own, 0), swap(own, 1)
        fetched = level == paired - 1
        if fetched:
            far, near, mates = lax.optimization_barrier((far, near, mates))
        solved_mate.append(near if level % 2 == 0 else far)
        kernel = functools.partial(forward_kernel, level, share, fetched)
        args = packed, weights, places, side, far, own, near
        solved += call(kernel, [vector], *args, fetched=fetched)

    solved_mate.append(swap(solved[-1], paired - 1))
    kernel = functools.partial(entry_kernel, paired, share)
    held, sent = call(kernel, sums, packed, weights, mates, meets, solved[-1], solved_mate[-1])
    for level in range(paired, levels):
        kernel = functools.partial(forward_pair_kernel, level, share, level == levels - 1)
        args = packed, weights, mates, meets, targets, side, side_mates[level - paired]
        own, mate, held, sent = call(kernel, [vector] * 2 + sums, *args, held, swap(sent, level))
        solved.append(own)
        solved_mate.append(mate)

    results = [own]
    for level in range(levels - 2, -1, -1):
        kernel = functools.partial(backward_kernel, level, share)
        args = packed, weights, mates, targets, solved[level], solved_mate[level], held, swap(sent, level)
        result, *rest = call(kernel, [vector] + (sums if level else []), *args)
        results.append(result)
        held, sent = rest or (held, sent)

    both = jnp.stack([jnp.stack(solved), jnp.stack(results[::-1])])
    both = both.reshape(2, levs, rows, share, width)[:, plan]
    both = lax.all_to_all(both, "level", 1, 0, tiled=False)
    both = both.transpose(1, 2, 0, 3, 4).reshape(2, rows, depth, width)
    return both[0], both[1]


def solution(mesh):
    return jax.shard_map(
        local,
        mesh=mesh,
        in_specs=(
            P(("dom", "level"), None, None),
            P(("dom", "level"), None, None),
            P(("dom", "level"), None, None, None),
            P(),
            P(),
        ),
        out_specs=(P(("dom", "level"), None, None), P(("dom", "level"), None, None)),
        check_vma=False,
    )
```

```python
import functools

import jax
import jax.numpy as jnp
from jax import lax
from jax.experimental import pallas as pl
from jax.experimental.pallas import tpu as pltpu
from jax.sharding import PartitionSpec as P

BF16 = jnp.bfloat16
F32 = jnp.float32


def dot(a, b):
    return lax.dot_general(a, b, (((1,), (0,)), ((), ())), preferred_element_type=F32)


def dot_t(a, b):
    return lax.dot_general(a, b, (((1,), (1,)), ((), ())), preferred_element_type=F32)


def either(low, high, share):
    top = lax.broadcasted_iota(jnp.int32, low.shape, 0) < share
    return jnp.where(top, low, high)


def ones_where(condition):
    return jnp.where(condition, 1.0, 0.0).astype(BF16)


BITS = 8


def unpack(packed, level):
    value = jnp.max(packed[level : level + 1])
    mask = (1 << BITS) - 1
    return value & mask, (value >> BITS) & mask, value >> (2 * BITS)


def products(product, share, owners, vectors, blocks, kind):
    rows = blocks.shape[1]
    totals = []
    for pair in range(rows):
        half, row = divmod(2 * pair, rows)
        part = vectors[2 * share * pair : 2 * share * (pair + 1)]
        wide = [blocks[owners[half], row + one, kind] for one in range(2)]
        if isinstance(kind, slice):
            wide = [block.reshape(-1, block.shape[-1]) for block in wide]
        totals.append(either(*[product(part, block) for block in wide], share))
    return jnp.concatenate(totals, axis=0)


def picked_from(places, around):
    at = lax.broadcasted_iota(jnp.int32, (places.shape[0], around.shape[0]), 1)
    return dot(ones_where(at == places), around)


def forward_kernel(level, share, fetched, packed, weights, places, side, far, own, near, out, *held):
    *owners, _ = unpack(packed, level)
    if fetched:
        held, sems = held
        copies = [
            pltpu.make_async_copy(weights.at[owners[half]], held.at[half], sems.at[half])
            for half in range(2)
        ]
        for copy in copies:
            copy.start()
    span = out.shape[0]
    picked = picked_from(places[level], jnp.concatenate([far[...], own[...], near[...]], axis=0))
    picked = jnp.concatenate([picked[n * span : (n + 1) * span] for n in range(3)], axis=1)
    if fetched:
        for copy in copies:
            copy.wait()
        owners, weights = range(2), held
    total = products(dot, share, owners, picked.astype(BF16), weights, slice(1, None))
    shifted = (side[level].astype(F32) - total).astype(BF16)
    out[...] = products(dot, share, owners, shifted, weights, 0).astype(BF16)


def gathered_sums(level, share, packed, weights, mates, places, own, mate):
    *owners, side = unpack(packed, level)
    span = own.shape[0]
    picked = picked_from(places[level], jnp.concatenate([own, mate], axis=0)).astype(BF16)
    sums = products(dot, share, owners, picked[:span], weights, 2)
    sums += products(dot, share, owners, picked[2 * span :], weights, 1 + side)
    if callable(mates):
        owners, mates, kind = mates()
    else:
        kind = 1
    sums_mate = products(dot, share, owners, picked[span : 2 * span], mates, kind)
    return jnp.concatenate([sums, sums_mate], axis=0)


def pushed_sums(level, share, packed, weights, mates, targets, own, mate):
    *owners, side = unpack(packed, level)
    span = own.shape[0]
    pushed = [
        products(dot_t, share, owners, own, weights, 2),
        products(dot_t, share, owners, mate, mates, 1),
        products(dot_t, share, owners, own, weights, 1 + side),
    ]
    pushed = jnp.concatenate(pushed, axis=0).astype(BF16)
    to = lax.broadcasted_iota(jnp.int32, (2 * span, 3 * span), 0)
    return dot(ones_where(to == targets[level]), pushed)


def pass_on(sums, held, sent):
    held[...] = sums
    sent[...] = sums.astype(BF16)


def joined(held, came):
    span = held.shape[0] // 2
    came = came[...].astype(F32)
    return held[:span] + came[span:], held[span:] + came[:span]


def entry_kernel(level, share, packed, mates, weights, meets, own, mate, held, sent, blocks, sems):
    *owners, _ = unpack(packed, level)
    copies = [
        pltpu.make_async_copy(mates.at[owners[half], :, pl.ds(1, 1)], blocks.at[half], sems.at[half])
        for half in range(2)
    ]
    for copy in copies:
        copy.start()

    def arrived():
        for copy in copies:
            copy.wait()
        return range(2), blocks, 0

    sums = gathered_sums(level, share, packed, weights, arrived, meets, own[...], mate[...])
    pass_on(sums, held, sent)


def forward_pair_kernel(
    level, share, last, packed, weights, mates, meets, targets, side, side_mate, held, came,
    solved, solved_mate, to_hold, to_send,
):
    *owners, _ = unpack(packed, level)
    pair = []
    for total, right, blocks in zip(joined(held, came), (side[level], side_mate[...]), (weights, mates)):
        shifted = (right.astype(F32) - total).astype(BF16)
        pair.append(products(dot, share, owners, shifted, blocks, 0).astype(BF16))
    solved[...], solved_mate[...] = pair
    if last:
        sums = pushed_sums(level, share, packed, weights, mates, targets, *pair)
    else:
        sums = gathered_sums(level + 1, share, packed, weights, mates, meets, *pair)
    pass_on(sums, to_hold, to_send)


def backward_kernel(
    level, share, packed, weights, mates, targets, solved, solved_mate, held, came, result, *outs
):
    *owners, _ = unpack(packed, level)
    pair = []
    for total, vector, blocks in zip(joined(held, came), (solved, solved_mate), (weights, mates)):
        part = products(dot, share, owners, total.astype(BF16), blocks, 0)
        pair.append((vector[...].astype(F32) - part).astype(BF16))
    result[...] = pair[0]
    pass_on(pushed_sums(level, share, packed, weights, mates, targets, *pair), *outs)


def last_kernel(share, packed, weights, held, came, *rest):
    *rest, out = rest
    solved, results = rest[: packed.shape[0]], rest[packed.shape[0] :]
    *owners, _ = unpack(packed, 0)
    total = joined(held, came)[0].astype(BF16)
    part = products(dot, share, owners, total, weights, 0)
    result = (solved[0][...].astype(F32) - part).astype(BF16)
    size = out.shape[1] // 2
    for level in range(packed.shape[0]):
        *owners, _ = unpack(packed, level)
        for which, array in enumerate((solved[level], results[level - 1] if level else result)):
            for half in range(2):
                out[owners[half], which * size : (which + 1) * size] = array[half * size : (half + 1) * size]


def deal_kernel(share, dealt, *outs):
    parts = [dealt[source].astype(F32) for source in range(dealt.shape[0])]
    for which, out in enumerate(outs):
        for row in range(out.shape[0]):
            at = (which * out.shape[0] + row) * share
            out[row] = jnp.concatenate([part[at : at + share] for part in parts], axis=0).astype(BF16)


def call(kernel, outs, packed, blocks, *rest, fetched=None):
    vmem = pl.BlockSpec(memory_space=pltpu.VMEM)
    specs = [vmem] * (2 + len(rest))
    scratch = []
    if fetched:
        specs[1] = pl.BlockSpec(memory_space=pltpu.HBM)
        blocks = pltpu.with_memory_space_constraint(blocks, pltpu.HBM)
        scratch = [pltpu.VMEM(fetched, blocks.dtype), pltpu.SemaphoreType.DMA((2,))]
    return pl.pallas_call(
        kernel,
        out_shape=outs,
        in_specs=specs,
        out_specs=[vmem] * len(outs),
        scratch_shapes=scratch,
        compiler_params=pltpu.CompilerParams(vmem_limit_bytes=16 * 2**20),
    )(packed, blocks, *rest)


def local(right_side, diag_inverse, off_blocks, columns, plan):
    rows, depth, width = right_side.shape
    doms = lax.axis_size("dom")
    levs = lax.axis_size("level")
    levels = levs // 2
    share = depth // levs
    count = 2 * rows
    dom = lax.axis_index("dom")
    lev = lax.axis_index("level")
    near_pairs = [(i, i ^ 1) for i in range(doms)]
    far_pairs = [(i, ((i + 1) ^ 1) - 1) for i in range(1, doms - 1)] + [(0, doms - 1), (doms - 1, 0)]

    weights = jnp.concatenate([diag_inverse[:, None], off_blocks], axis=1)
    weights = lax.all_gather(weights, "level")

    turn = dom % 2
    ids = jnp.arange(levs, dtype=jnp.int32)
    own_level = jnp.sum(jnp.where(ids == lev, plan, 0)) // 2
    inverse = jnp.sum(jnp.where(plan[None, :] == ids[:, None], ids[None, :], 0), axis=1)
    side_of = jnp.where(jnp.arange(levels) % 2 == 1, 2 * turn, 2 - 2 * turn)
    packed = inverse[0::2] + (inverse[1::2] << BITS) + (side_of << (2 * BITS))
    packed = jnp.broadcast_to(packed[:, None], (levels, 128)).astype(jnp.int32)

    here = jnp.where(own_level % 2 == turn, off_blocks[:, 0], off_blocks[:, 2])
    mates = jnp.stack([diag_inverse, here], axis=1)
    by_near = lax.ppermute(mates, "dom", near_pairs)
    by_far = lax.ppermute(mates, "dom", far_pairs)
    mates = jnp.where(own_level % 2 == 1, by_near, by_far)
    first = jnp.einsum("rkb,rbc->rkc", right_side, diag_inverse, preferred_element_type=F32)
    side = jnp.where(own_level == 0, first.astype(BF16), right_side)
    side = side.reshape(rows, levs, share, width)
    side = lax.all_to_all(side, "level", 1, 0, tiled=False)
    side = side.reshape(levs, rows * share, width)[inverse].reshape(levels, count * share, width)

    near_dom = dom + 1 - 2 * turn
    far_dom = (dom - 1 + 2 * turn) % doms
    part = jnp.stack(
        [
            lax.dynamic_slice_in_dim(columns, which * levs * rows, levs * rows, 0)
            for which in (dom, near_dom, far_dom)
        ]
    )
    part = part.reshape(3, levs, rows * 3)[:, inverse].reshape(3, levels, count, 3)
    second = jnp.roll(inverse[1::2], 1)[None, :, None, None]
    met = jnp.where(part // rows % levs == second, rows, 0) + part % rows
    odd = (jnp.arange(levels) % 2 == 1)[:, None]
    meets_own = met[0]
    meets_mate = jnp.where(odd[..., None], met[1], met[2])
    ahead = odd == (turn == 0)
    own_mate = jnp.where(ahead, meets_own[..., 0], meets_own[..., 2])
    mate_own = jnp.where(ahead, meets_mate[..., 0], meets_mate[..., 2])
    k = jnp.arange(share, dtype=jnp.int32)
    span = count * share
    slot = jnp.where(turn == 0, 1, -1) * (jnp.arange(3, dtype=jnp.int32) - 1) + 1
    places = meets_own.transpose(0, 2, 1) * share + slot[None, :, None] * span
    places = (places[..., None] + k).reshape(levels, 3 * span, 1)
    targets = jnp.stack([meets_own[..., 1], mate_own, own_mate + count], axis=1) * share
    targets = (targets[..., None] + k).reshape(levels, 3 * span)
    targets, meets = targets[:, None, :], targets[:, :, None]

    vector = jax.ShapeDtypeStruct((count * share, width), BF16)
    sums = [jax.ShapeDtypeStruct((2 * span, width), kind) for kind in (F32, BF16)]
    paired = levels - 2

    own = side[0]
    far = lax.ppermute(jnp.stack([own, side[paired]]), "dom", far_pairs)
    near = lax.ppermute(jnp.stack([own, side[paired + 1]]), "dom", near_pairs)
    mates, packed, side, places, targets, meets, own, far, near = lax.optimization_barrier(
        (mates, packed, side, places, targets, meets, own, far, near)
    )
    side_mates = [far[1], near[1]]
    far, near = far[0], near[0]
    mates = lax.all_gather(mates, "level")

    def swap(vector, level):
        return lax.ppermute(vector, "dom", far_pairs if level % 2 == 0 else near_pairs)

    solved = [own]
    solved_mate = []
    for level in range(1, paired):
        if level > 1:
            own = solved[-1]
            far, near = swap(own, 0), swap(own, 1)
        fetched = level in (1, paired - 1)
        if level == paired - 1:
            far, near, mates = lax.optimization_barrier((far, near, mates))
        solved_mate.append(near if level % 2 == 0 else far)
        kernel = functools.partial(forward_kernel, level, share, fetched)
        args = packed, weights, places, side, far, own, near
        fetched = (2,) + weights.shape[1:] if fetched else None
        solved += call(kernel, [vector], *args, fetched=fetched)

    solved_mate.append(swap(solved[-1], paired - 1))
    kernel = functools.partial(entry_kernel, paired, share)
    args = packed, mates, weights, meets, solved[-1], solved_mate[-1]
    held, sent = call(kernel, sums, *args, fetched=(2, rows, 1, width, width))
    for level in range(paired, levels):
        kernel = functools.partial(forward_pair_kernel, level, share, level == levels - 1)
        args = packed, weights, mates, meets, targets, side, side_mates[level - paired]
        own, mate, held, sent = call(kernel, [vector] * 2 + sums, *args, held, swap(sent, level))
        solved.append(own)
        solved_mate.append(mate)

    results = [own]
    for level in range(levels - 2, 0, -1):
        kernel = functools.partial(backward_kernel, level, share)
        args = packed, weights, mates, targets, solved[level], solved_mate[level], held, swap(sent, level)
        result, held, sent = call(kernel, [vector] + sums, *args)
        results.append(result)

    dealt = jax.ShapeDtypeStruct((levs, 2 * rows * share, width), BF16)
    kernel = functools.partial(last_kernel, share)
    (dealt,) = call(kernel, [dealt], packed, weights, held, swap(sent, 0), *solved, *results[::-1])
    dealt = lax.all_to_all(dealt, "level", 0, 0, tiled=False)
    vmem = pl.BlockSpec(memory_space=pltpu.VMEM)
    return pl.pallas_call(
        functools.partial(deal_kernel, share),
        out_shape=[jax.ShapeDtypeStruct(right_side.shape, BF16)] * 2,
        in_specs=[vmem],
        out_specs=[vmem] * 2,
    )(dealt)


def solution(mesh):
    return jax.shard_map(
        local,
        mesh=mesh,
        in_specs=(
            P(("dom", "level"), None, None),
            P(("dom", "level"), None, None),
            P(("dom", "level"), None, None, None),
            P(),
            P(),
        ),
        out_specs=(P(("dom", "level"), None, None), P(("dom", "level"), None, None)),
        check_vma=False,
    )
```

```python
import functools

import jax
import jax.numpy as jnp
from jax import lax
from jax.experimental import pallas as pl
from jax.experimental.pallas import tpu as pltpu
from jax.sharding import PartitionSpec as P

BF16 = jnp.bfloat16
F32 = jnp.float32


def dot(a, b):
    return lax.dot_general(a, b, (((1,), (0,)), ((), ())), preferred_element_type=F32)


def dot_t(a, b):
    return lax.dot_general(a, b, (((1,), (1,)), ((), ())), preferred_element_type=F32)


def either(low, high, share):
    top = lax.broadcasted_iota(jnp.int32, low.shape, 0) < share
    return jnp.where(top, low, high)


def ones_where(condition):
    return jnp.where(condition, 1.0, 0.0).astype(BF16)


BITS = 8


def unpack(packed, level):
    value = jnp.max(packed[level : level + 1])
    mask = (1 << BITS) - 1
    return value & mask, (value >> BITS) & mask, value >> (2 * BITS)


def products(product, share, owners, vectors, blocks, kind):
    rows = blocks.shape[1]
    totals = []
    for pair in range(rows):
        half, row = divmod(2 * pair, rows)
        part = vectors[2 * share * pair : 2 * share * (pair + 1)]
        wide = [blocks[owners[half], row + one, kind] for one in range(2)]
        if isinstance(kind, slice):
            wide = [block.reshape(-1, block.shape[-1]) for block in wide]
        totals.append(either(*[product(part, block) for block in wide], share))
    return jnp.concatenate(totals, axis=0)


def picked_from(places, around):
    at = lax.broadcasted_iota(jnp.int32, (places.shape[0], around.shape[0]), 1)
    return dot(ones_where(at == places), around)


def forward_kernel(level, share, fetched, packed, weights, places, side, far, own, near, out, *held):
    *owners, _ = unpack(packed, level)
    if fetched:
        held, sems = held
        copies = [
            pltpu.make_async_copy(weights.at[owners[half]], held.at[half], sems.at[half])
            for half in range(2)
        ]
        for copy in copies:
            copy.start()
    span = out.shape[0]
    picked = picked_from(places[level], jnp.concatenate([far[...], own[...], near[...]], axis=0))
    picked = jnp.concatenate([picked[n * span : (n + 1) * span] for n in range(3)], axis=1)
    if fetched:
        for copy in copies:
            copy.wait()
        owners, weights = range(2), held
    total = products(dot, share, owners, picked.astype(BF16), weights, slice(1, None))
    shifted = (side[level].astype(F32) - total).astype(BF16)
    out[...] = products(dot, share, owners, shifted, weights, 0).astype(BF16)


def gathered_sums(level, share, places, own, mate, blocks):
    span = own.shape[0]
    picked = picked_from(places[level], jnp.concatenate([own, mate], axis=0)).astype(BF16)
    parts = [picked[n * span : (n + 1) * span] for n in range(3)]
    sums = [
        products(dot, share, owners, part, block, kind)
        for part, (owners, block, kind) in zip(parts, blocks())
    ]
    return jnp.concatenate([sums[0] + sums[2], sums[1]], axis=0)


def pushed_sums(level, share, packed, weights, mates, targets, own, mate):
    *owners, side = unpack(packed, level)
    span = own.shape[0]
    pushed = [
        products(dot_t, share, owners, own, weights, 2),
        products(dot_t, share, owners, mate, mates, 1),
        products(dot_t, share, owners, own, weights, 1 + side),
    ]
    pushed = jnp.concatenate(pushed, axis=0).astype(BF16)
    to = lax.broadcasted_iota(jnp.int32, (2 * span, 3 * span), 0)
    return dot(ones_where(to == targets[level]), pushed)


def pass_on(sums, held, sent):
    held[...] = sums
    sent[...] = sums.astype(BF16)


def joined(held, came):
    span = held.shape[0] // 2
    came = came[...].astype(F32)
    return held[:span] + came[span:], held[span:] + came[:span]


def entry_kernel(level, share, packed, weights, mates, meets, own, mate, held, sent, blocks, sems):
    *owners, side = unpack(packed, level)
    copies = []
    for which, (source, kind) in enumerate(((weights, 2), (mates, 1), (weights, 1 + side))):
        for half in range(2):
            rows = source.at[owners[half], :, pl.ds(kind, 1)]
            copies.append(pltpu.make_async_copy(rows, blocks.at[which, half], sems.at[which, half]))
    for copy in copies:
        copy.start()

    def arrived():
        for copy in copies:
            copy.wait()
        return [(range(2), blocks.at[which], 0) for which in range(3)]

    pass_on(gathered_sums(level, share, meets, own[...], mate[...], arrived), held, sent)


def forward_pair_kernel(
    level, share, last, packed, weights, mates, meets, targets, side, side_mate, held, came,
    solved, solved_mate, to_hold, to_send,
):
    *owners, _ = unpack(packed, level)
    pair = []
    for total, right, blocks in zip(joined(held, came), (side[level], side_mate[...]), (weights, mates)):
        shifted = (right.astype(F32) - total).astype(BF16)
        pair.append(products(dot, share, owners, shifted, blocks, 0).astype(BF16))
    solved[...], solved_mate[...] = pair
    if last:
        sums = pushed_sums(level, share, packed, weights, mates, targets, *pair)
    else:
        *owners, up = unpack(packed, level + 1)
        blocks = [(owners, weights, 2), (owners, mates, 1), (owners, weights, 1 + up)]
        sums = gathered_sums(level + 1, share, meets, *pair, lambda: blocks)
    pass_on(sums, to_hold, to_send)


def backward_kernel(
    level, share, packed, weights, mates, targets, solved, solved_mate, held, came, result, *outs
):
    *owners, _ = unpack(packed, level)
    pair = []
    for total, vector, blocks in zip(joined(held, came), (solved, solved_mate), (weights, mates)):
        part = products(dot, share, owners, total.astype(BF16), blocks, 0)
        pair.append((vector[...].astype(F32) - part).astype(BF16))
    result[...] = pair[0]
    pass_on(pushed_sums(level, share, packed, weights, mates, targets, *pair), *outs)


def last_kernel(share, packed, weights, held, came, *rest):
    *rest, out = rest
    solved, results = rest[: packed.shape[0]], rest[packed.shape[0] :]
    *owners, _ = unpack(packed, 0)
    total = joined(held, came)[0].astype(BF16)
    part = products(dot, share, owners, total, weights, 0)
    result = (solved[0][...].astype(F32) - part).astype(BF16)
    size = out.shape[1] // 2
    for level in range(packed.shape[0]):
        *owners, _ = unpack(packed, level)
        for which, array in enumerate((solved[level], results[level - 1] if level else result)):
            for half in range(2):
                out[owners[half], which * size : (which + 1) * size] = array[half * size : (half + 1) * size]


def call(kernel, outs, *args, fetched=0, scratch=(), cost=None):
    specs = [pl.BlockSpec(memory_space=pltpu.VMEM)] * len(args)
    args = list(args)
    for at in range(1, 1 + fetched):
        specs[at] = pl.BlockSpec(memory_space=pltpu.HBM)
        args[at] = pltpu.with_memory_space_constraint(args[at], pltpu.HBM)
    return pl.pallas_call(
        kernel,
        out_shape=outs,
        in_specs=specs,
        out_specs=[pl.BlockSpec(memory_space=pltpu.VMEM)] * len(outs),
        scratch_shapes=scratch,
        cost_estimate=cost,
        compiler_params=pltpu.CompilerParams(vmem_limit_bytes=16 * 2**20),
    )(*args)


def local(right_side, diag_inverse, off_blocks, columns, plan):
    rows, depth, width = right_side.shape
    doms = lax.axis_size("dom")
    levs = lax.axis_size("level")
    levels = levs // 2
    share = depth // levs
    count = 2 * rows
    dom = lax.axis_index("dom")
    lev = lax.axis_index("level")
    near_pairs = [(i, i ^ 1) for i in range(doms)]
    far_pairs = [(i, ((i + 1) ^ 1) - 1) for i in range(1, doms - 1)] + [(0, doms - 1), (doms - 1, 0)]

    weights = jnp.concatenate([diag_inverse[:, None], off_blocks], axis=1)
    weights = lax.all_gather(weights, "level")

    turn = dom % 2
    ids = jnp.arange(levs, dtype=jnp.int32)
    own_level = jnp.sum(jnp.where(ids == lev, plan, 0)) // 2
    inverse = jnp.sum(jnp.where(plan[None, :] == ids[:, None], ids[None, :], 0), axis=1)
    side_of = jnp.where(jnp.arange(levels) % 2 == 1, 2 * turn, 2 - 2 * turn)
    packed = inverse[0::2] + (inverse[1::2] << BITS) + (side_of << (2 * BITS))
    packed = jnp.broadcast_to(packed[:, None], (levels, 128)).astype(jnp.int32)

    here = jnp.where(own_level % 2 == turn, off_blocks[:, 0], off_blocks[:, 2])
    mates = jnp.stack([diag_inverse, here], axis=1)
    by_near = lax.ppermute(mates, "dom", near_pairs)
    by_far = lax.ppermute(mates, "dom", far_pairs)
    mates = jnp.where(own_level % 2 == 1, by_near, by_far)
    first = jnp.einsum("rkb,rbc->rkc", right_side, diag_inverse, preferred_element_type=F32)
    side = jnp.where(own_level == 0, first.astype(BF16), right_side)
    side = side.reshape(rows, levs, share, width)
    side = lax.all_to_all(side, "level", 1, 0, tiled=False)
    side = side.reshape(levs, rows * share, width)[inverse].reshape(levels, count * share, width)

    near_dom = dom + 1 - 2 * turn
    far_dom = (dom - 1 + 2 * turn) % doms
    part = jnp.stack(
        [
            lax.dynamic_slice_in_dim(columns, which * levs * rows, levs * rows, 0)
            for which in (dom, near_dom, far_dom)
        ]
    )
    part = part.reshape(3, levs, rows * 3)[:, inverse].reshape(3, levels, count, 3)
    second = jnp.roll(inverse[1::2], 1)[None, :, None, None]
    met = jnp.where(part // rows % levs == second, rows, 0) + part % rows
    odd = (jnp.arange(levels) % 2 == 1)[:, None]
    meets_own = met[0]
    meets_mate = jnp.where(odd[..., None], met[1], met[2])
    ahead = odd == (turn == 0)
    own_mate = jnp.where(ahead, meets_own[..., 0], meets_own[..., 2])
    mate_own = jnp.where(ahead, meets_mate[..., 0], meets_mate[..., 2])
    k = jnp.arange(share, dtype=jnp.int32)
    span = count * share
    slot = jnp.where(turn == 0, 1, -1) * (jnp.arange(3, dtype=jnp.int32) - 1) + 1
    places = meets_own.transpose(0, 2, 1) * share + slot[None, :, None] * span
    places = (places[..., None] + k).reshape(levels, 3 * span, 1)
    targets = jnp.stack([meets_own[..., 1], mate_own, own_mate + count], axis=1) * share
    targets = (targets[..., None] + k).reshape(levels, 3 * span)
    targets, meets = targets[:, None, :], targets[:, :, None]

    vector = jax.ShapeDtypeStruct((count * share, width), BF16)
    sums = [jax.ShapeDtypeStruct((2 * span, width), kind) for kind in (F32, BF16)]
    paired = levels - 2

    own = side[0]
    far = lax.ppermute(jnp.stack([own, side[paired]]), "dom", far_pairs)
    near = lax.ppermute(jnp.stack([own, side[paired + 1]]), "dom", near_pairs)
    mates, packed, side, places, targets, meets, own, far, near = lax.optimization_barrier(
        (mates, packed, side, places, targets, meets, own, far, near)
    )
    side_mates = [far[1], near[1]]
    far, near = far[0], near[0]
    mates = lax.all_gather(mates, "level")

    def swap(vector, level):
        return lax.ppermute(vector, "dom", far_pairs if level % 2 == 0 else near_pairs)

    solved = [own]
    solved_mate = []
    for level in range(1, paired):
        if level > 1:
            own = solved[-1]
            far, near = swap(own, 0), swap(own, 1)
        solved_mate.append(near if level % 2 == 0 else far)
        kernel = functools.partial(forward_kernel, level, share, level == 1)
        args = packed, weights, places, side, far, own, near
        if level == 1:
            scratch = [pltpu.VMEM((2,) + weights.shape[1:], BF16), pltpu.SemaphoreType.DMA((2,))]
            solved += call(kernel, [vector], *args, fetched=1, scratch=scratch)
        else:
            solved += call(kernel, [vector], *args)

    mate, mates = lax.optimization_barrier((swap(solved[-1], paired - 1), mates))
    solved_mate.append(mate)
    kernel = functools.partial(entry_kernel, paired, share)
    args = packed, weights, mates, meets, solved[-1], mate
    scratch = [
        pltpu.VMEM((3, 2, rows, 1, width, width), BF16),
        pltpu.SemaphoreType.DMA((3, 2)),
    ]
    cost = pl.CostEstimate(flops=0, transcendentals=0, bytes_accessed=3 * weights.size)
    held, sent = call(kernel, sums, *args, fetched=2, scratch=scratch, cost=cost)
    for level in range(paired, levels):
        kernel = functools.partial(forward_pair_kernel, level, share, level == levels - 1)
        args = packed, weights, mates, meets, targets, side, side_mates[level - paired]
        own, mate, held, sent = call(kernel, [vector] * 2 + sums, *args, held, swap(sent, level))
        solved.append(own)
        solved_mate.append(mate)

    results = [own]
    for level in range(levels - 2, 0, -1):
        kernel = functools.partial(backward_kernel, level, share)
        args = packed, weights, mates, targets, solved[level], solved_mate[level], held, swap(sent, level)
        result, held, sent = call(kernel, [vector] + sums, *args)
        results.append(result)

    dealt = jax.ShapeDtypeStruct((levs, 2 * rows * share, width), BF16)
    kernel = functools.partial(last_kernel, share)
    (dealt,) = call(kernel, [dealt], packed, weights, held, swap(sent, 0), *solved, *results[::-1])
    dealt = lax.all_to_all(dealt, "level", 0, 0, tiled=False)
    dealt = dealt.reshape(levs, 2, rows, share, width).transpose(1, 2, 0, 3, 4)
    dealt = dealt.reshape(2, rows, depth, width)
    return dealt[0], dealt[1]


def solution(mesh):
    return jax.shard_map(
        local,
        mesh=mesh,
        in_specs=(
            P(("dom", "level"), None, None),
            P(("dom", "level"), None, None),
            P(("dom", "level"), None, None, None),
            P(),
            P(),
        ),
        out_specs=(P(("dom", "level"), None, None), P(("dom", "level"), None, None)),
        check_vma=False,
    )
```

```python
import functools

import jax
import jax.numpy as jnp
from jax import lax
from jax.experimental import pallas as pl
from jax.experimental.pallas import tpu as pltpu
from jax.sharding import PartitionSpec as P

BF16 = jnp.bfloat16
F32 = jnp.float32


def dot(a, b):
    return lax.dot_general(a, b, (((1,), (0,)), ((), ())), preferred_element_type=F32)


def dot_t(a, b):
    return lax.dot_general(a, b, (((1,), (1,)), ((), ())), preferred_element_type=F32)


def either(low, high, share):
    top = lax.broadcasted_iota(jnp.int32, low.shape, 0) < share
    return jnp.where(top, low, high)


def ones_where(condition):
    return jnp.where(condition, 1.0, 0.0).astype(BF16)


BITS = 8


def unpack(packed, level):
    value = jnp.max(packed[level : level + 1])
    mask = (1 << BITS) - 1
    return value & mask, (value >> BITS) & mask, value >> (2 * BITS)


def products(product, share, owners, vectors, blocks, kind):
    rows = blocks.shape[1]
    totals = []
    for pair in range(rows):
        half, row = divmod(2 * pair, rows)
        part = vectors[2 * share * pair : 2 * share * (pair + 1)]
        wide = [blocks[owners[half], row + one, kind] for one in range(2)]
        if isinstance(kind, slice):
            wide = [block.reshape(-1, block.shape[-1]) for block in wide]
        totals.append(either(*[product(part, block) for block in wide], share))
    return jnp.concatenate(totals, axis=0)


def picked_from(places, around):
    at = lax.broadcasted_iota(jnp.int32, (places.shape[0], around.shape[0]), 1)
    return dot(ones_where(at == places), around)


def forward_kernel(level, share, fetched, packed, weights, places, side, far, own, near, out, *held):
    *owners, _ = unpack(packed, level)
    if fetched:
        held, sems = held
        copies = [
            pltpu.make_async_copy(weights.at[owners[half]], held.at[half], sems.at[half])
            for half in range(2)
        ]
        for copy in copies:
            copy.start()
    span = out.shape[0]
    picked = picked_from(places[level], jnp.concatenate([far[...], own[...], near[...]], axis=0))
    picked = jnp.concatenate([picked[n * span : (n + 1) * span] for n in range(3)], axis=1)
    if fetched:
        for copy in copies:
            copy.wait()
        owners, weights = range(2), held
    total = products(dot, share, owners, picked.astype(BF16), weights, slice(1, None))
    shifted = (side[level].astype(F32) - total).astype(BF16)
    out[...] = products(dot, share, owners, shifted, weights, 0).astype(BF16)


def gathered_sums(level, share, places, own, mate, blocks):
    span = own.shape[0]
    picked = picked_from(places[level], jnp.concatenate([own, mate], axis=0)).astype(BF16)
    parts = [picked[n * span : (n + 1) * span] for n in range(3)]
    sums = [
        products(dot, share, owners, part, block, kind)
        for part, (owners, block, kind) in zip(parts, blocks())
    ]
    return jnp.concatenate([sums[0] + sums[2], sums[1]], axis=0)


def pushed_sums(level, share, packed, weights, mates, targets, own, mate):
    *owners, side = unpack(packed, level)
    span = own.shape[0]
    pushed = [
        products(dot_t, share, owners, own, weights, 2),
        products(dot_t, share, owners, mate, mates, 1),
        products(dot_t, share, owners, own, weights, 1 + side),
    ]
    pushed = jnp.concatenate(pushed, axis=0).astype(BF16)
    to = lax.broadcasted_iota(jnp.int32, (2 * span, 3 * span), 0)
    return dot(ones_where(to == targets[level]), pushed)


def pass_on(sums, held, sent):
    held[...] = sums
    sent[...] = sums.astype(BF16)


def joined(held, came):
    span = held.shape[0] // 2
    came = came[...].astype(F32)
    return held[:span] + came[span:], held[span:] + came[:span]


def entry_kernel(level, share, packed, weights, mates, meets, own, mate, held, sent, blocks, sems):
    *owners, side = unpack(packed, level)
    copies = []
    for which, (source, kind) in enumerate(((weights, 2), (mates, 1), (weights, 1 + side))):
        for half in range(2):
            rows = source.at[owners[half], :, pl.ds(kind, 1)]
            copies.append(pltpu.make_async_copy(rows, blocks.at[which, half], sems.at[which, half]))
    for copy in copies:
        copy.start()

    def arrived():
        for copy in copies:
            copy.wait()
        return [(range(2), blocks.at[which], 0) for which in range(3)]

    pass_on(gathered_sums(level, share, meets, own[...], mate[...], arrived), held, sent)


def forward_pair_kernel(
    level, share, last, packed, weights, mates, meets, targets, side, side_mate, held, came,
    solved, solved_mate, to_hold, to_send,
):
    *owners, _ = unpack(packed, level)
    pair = []
    for total, right, blocks in zip(joined(held, came), (side[level], side_mate[...]), (weights, mates)):
        shifted = (right.astype(F32) - total).astype(BF16)
        pair.append(products(dot, share, owners, shifted, blocks, 0).astype(BF16))
    solved[...], solved_mate[...] = pair
    if last:
        sums = pushed_sums(level, share, packed, weights, mates, targets, *pair)
    else:
        *owners, up = unpack(packed, level + 1)
        blocks = [(owners, weights, 2), (owners, mates, 1), (owners, weights, 1 + up)]
        sums = gathered_sums(level + 1, share, meets, *pair, lambda: blocks)
    pass_on(sums, to_hold, to_send)


def backward_kernel(
    level, share, packed, weights, mates, targets, solved, solved_mate, held, came, result, *outs
):
    *owners, _ = unpack(packed, level)
    pair = []
    for total, vector, blocks in zip(joined(held, came), (solved, solved_mate), (weights, mates)):
        part = products(dot, share, owners, total.astype(BF16), blocks, 0)
        pair.append((vector[...].astype(F32) - part).astype(BF16))
    result[...] = pair[0]
    pass_on(pushed_sums(level, share, packed, weights, mates, targets, *pair), *outs)


def last_kernel(share, packed, weights, held, came, *rest):
    *rest, out = rest
    solved, results = rest[: packed.shape[0]], rest[packed.shape[0] :]
    *owners, _ = unpack(packed, 0)
    total = joined(held, came)[0].astype(BF16)
    part = products(dot, share, owners, total, weights, 0)
    result = (solved[0][...].astype(F32) - part).astype(BF16)
    size = out.shape[1] // 2
    for level in range(packed.shape[0]):
        *owners, _ = unpack(packed, level)
        for which, array in enumerate((solved[level], results[level - 1] if level else result)):
            for half in range(2):
                out[owners[half], which * size : (which + 1) * size] = array[half * size : (half + 1) * size]


def call(kernel, outs, *args, fetched=0, scratch=(), cost=None):
    specs = [pl.BlockSpec(memory_space=pltpu.VMEM)] * len(args)
    args = list(args)
    for at in range(1, 1 + fetched):
        specs[at] = pl.BlockSpec(memory_space=pltpu.HBM)
        args[at] = pltpu.with_memory_space_constraint(args[at], pltpu.HBM)
    return pl.pallas_call(
        kernel,
        out_shape=outs,
        in_specs=specs,
        out_specs=[pl.BlockSpec(memory_space=pltpu.VMEM)] * len(outs),
        scratch_shapes=scratch,
        cost_estimate=cost,
        compiler_params=pltpu.CompilerParams(vmem_limit_bytes=16 * 2**20),
    )(*args)


def local(right_side, diag_inverse, off_blocks, columns, plan):
    rows, depth, width = right_side.shape
    doms = lax.axis_size("dom")
    levs = lax.axis_size("level")
    levels = levs // 2
    share = depth // levs
    count = 2 * rows
    dom = lax.axis_index("dom")
    lev = lax.axis_index("level")
    near_pairs = [(i, i ^ 1) for i in range(doms)]
    far_pairs = [(i, ((i + 1) ^ 1) - 1) for i in range(1, doms - 1)] + [(0, doms - 1), (doms - 1, 0)]

    weights = jnp.concatenate([diag_inverse[:, None], off_blocks], axis=1)
    weights = lax.all_gather(weights, "level")

    turn = dom % 2
    ids = jnp.arange(levs, dtype=jnp.int32)
    own_level = jnp.sum(jnp.where(ids == lev, plan, 0)) // 2
    inverse = jnp.sum(jnp.where(plan[None, :] == ids[:, None], ids[None, :], 0), axis=1)
    side_of = jnp.where(jnp.arange(levels) % 2 == 1, 2 * turn, 2 - 2 * turn)
    packed = inverse[0::2] + (inverse[1::2] << BITS) + (side_of << (2 * BITS))
    packed = jnp.broadcast_to(packed[:, None], (levels, 128)).astype(jnp.int32)

    here = jnp.where(own_level % 2 == turn, off_blocks[:, 0], off_blocks[:, 2])
    mates = jnp.stack([diag_inverse, here], axis=1)
    by_near = lax.ppermute(mates, "dom", near_pairs)
    by_far = lax.ppermute(mates, "dom", far_pairs)
    mates = jnp.where(own_level % 2 == 1, by_near, by_far)
    first = jnp.einsum("rkb,rbc->rkc", right_side, diag_inverse, preferred_element_type=F32)
    side = jnp.where(own_level == 0, first.astype(BF16), right_side)
    side = side.reshape(rows, levs, share, width)
    side = lax.all_to_all(side, "level", 1, 0, tiled=False)
    side = side.reshape(levs, rows * share, width)[inverse].reshape(levels, count * share, width)

    near_dom = dom + 1 - 2 * turn
    far_dom = (dom - 1 + 2 * turn) % doms
    part = jnp.stack(
        [
            lax.dynamic_slice_in_dim(columns, which * levs * rows, levs * rows, 0)
            for which in (dom, near_dom, far_dom)
        ]
    )
    part = part.reshape(3, levs, rows * 3)[:, inverse].reshape(3, levels, count, 3)
    second = jnp.roll(inverse[1::2], 1)[None, :, None, None]
    met = jnp.where(part // rows % levs == second, rows, 0) + part % rows
    odd = (jnp.arange(levels) % 2 == 1)[:, None]
    meets_own = met[0]
    meets_mate = jnp.where(odd[..., None], met[1], met[2])
    ahead = odd == (turn == 0)
    own_mate = jnp.where(ahead, meets_own[..., 0], meets_own[..., 2])
    mate_own = jnp.where(ahead, meets_mate[..., 0], meets_mate[..., 2])
    k = jnp.arange(share, dtype=jnp.int32)
    span = count * share
    slot = jnp.where(turn == 0, 1, -1) * (jnp.arange(3, dtype=jnp.int32) - 1) + 1
    places = meets_own.transpose(0, 2, 1) * share + slot[None, :, None] * span
    places = (places[..., None] + k).reshape(levels, 3 * span, 1)
    targets = jnp.stack([meets_own[..., 1], mate_own, own_mate + count], axis=1) * share
    targets = (targets[..., None] + k).reshape(levels, 3 * span)
    targets, meets = targets[:, None, :], targets[:, :, None]

    vector = jax.ShapeDtypeStruct((count * share, width), BF16)
    sums = [jax.ShapeDtypeStruct((2 * span, width), kind) for kind in (F32, BF16)]
    paired = levels - 2

    own = side[0]
    far = lax.ppermute(jnp.stack([own, side[paired]]), "dom", far_pairs)
    near = lax.ppermute(jnp.stack([own, side[paired + 1]]), "dom", near_pairs)
    mates, packed, side, places, targets, meets, own, far, near = lax.optimization_barrier(
        (mates, packed, side, places, targets, meets, own, far, near)
    )
    side_mates = [far[1], near[1]]
    far, near = far[0], near[0]
    mates = lax.all_gather(mates, "level")

    def swap(vector, level):
        return lax.ppermute(vector, "dom", far_pairs if level % 2 == 0 else near_pairs)

    solved = [own]
    solved_mate = []
    for level in range(1, paired):
        if level > 1:
            own = solved[-1]
            far, near = swap(own, 0), swap(own, 1)
        solved_mate.append(near if level % 2 == 0 else far)
        kernel = functools.partial(forward_kernel, level, share, level == 1)
        args = packed, weights, places, side, far, own, near
        if level == 1:
            scratch = [pltpu.VMEM((2,) + weights.shape[1:], BF16), pltpu.SemaphoreType.DMA((2,))]
            solved += call(kernel, [vector], *args, fetched=1, scratch=scratch)
        else:
            solved += call(kernel, [vector], *args)

    mate, mates = lax.optimization_barrier((swap(solved[-1], paired - 1), mates))
    solved_mate.append(mate)
    kernel = functools.partial(entry_kernel, paired, share)
    args = packed, weights, mates, meets, solved[-1], mate
    scratch = [
        pltpu.VMEM((3, 2, rows, 1, width, width), BF16),
        pltpu.SemaphoreType.DMA((3, 2)),
    ]
    cost = pl.CostEstimate(flops=0, transcendentals=0, bytes_accessed=12 * weights.size)
    held, sent = call(kernel, sums, *args, fetched=2, scratch=scratch, cost=cost)
    for level in range(paired, levels):
        kernel = functools.partial(forward_pair_kernel, level, share, level == levels - 1)
        args = packed, weights, mates, meets, targets, side, side_mates[level - paired]
        own, mate, held, sent = call(kernel, [vector] * 2 + sums, *args, held, swap(sent, level))
        solved.append(own)
        solved_mate.append(mate)

    results = [own]
    for level in range(levels - 2, 0, -1):
        kernel = functools.partial(backward_kernel, level, share)
        args = packed, weights, mates, targets, solved[level], solved_mate[level], held, swap(sent, level)
        result, held, sent = call(kernel, [vector] + sums, *args)
        results.append(result)

    dealt = jax.ShapeDtypeStruct((levs, 2 * rows * share, width), BF16)
    kernel = functools.partial(last_kernel, share)
    (dealt,) = call(kernel, [dealt], packed, weights, held, swap(sent, 0), *solved, *results[::-1])
    dealt = lax.all_to_all(dealt, "level", 0, 0, tiled=False)
    dealt = dealt.reshape(levs, 2, rows, share, width).transpose(1, 2, 0, 3, 4)
    dealt = dealt.reshape(2, rows, depth, width)
    return dealt[0], dealt[1]


def solution(mesh):
    return jax.shard_map(
        local,
        mesh=mesh,
        in_specs=(
            P(("dom", "level"), None, None),
            P(("dom", "level"), None, None),
            P(("dom", "level"), None, None, None),
            P(),
            P(),
        ),
        out_specs=(P(("dom", "level"), None, None), P(("dom", "level"), None, None)),
        check_vma=False,
    )
```

```python
import functools

import jax
import jax.numpy as jnp
from jax import lax
from jax.experimental import pallas as pl
from jax.experimental.pallas import tpu as pltpu
from jax.sharding import PartitionSpec as P

BF16 = jnp.bfloat16
F32 = jnp.float32


def dot(a, b):
    return lax.dot_general(a, b, (((1,), (0,)), ((), ())), preferred_element_type=F32)


def dot_t(a, b):
    return lax.dot_general(a, b, (((1,), (1,)), ((), ())), preferred_element_type=F32)


def either(low, high, share):
    top = lax.broadcasted_iota(jnp.int32, low.shape, 0) < share
    return jnp.where(top, low, high)


def ones_where(condition):
    return jnp.where(condition, 1.0, 0.0).astype(BF16)


BITS = 8


def unpack(packed, level):
    value = jnp.max(packed[level : level + 1])
    mask = (1 << BITS) - 1
    return value & mask, (value >> BITS) & mask, value >> (2 * BITS)


def products(product, share, vectors, blocks, level, kind):
    totals = []
    for row in range(0, blocks.shape[1], 2):
        part = vectors[share * row : share * (row + 2)]
        wide = [blocks[level, row + one, kind] for one in range(2)]
        if isinstance(kind, slice):
            wide = [block.reshape(-1, block.shape[-1]) for block in wide]
        totals.append(either(*[product(part, block) for block in wide], share))
    return jnp.concatenate(totals, axis=0)


def run(copies, sems):
    copies = [pltpu.make_async_copy(*ends, sems.at[which]) for which, ends in enumerate(copies)]
    for copy in copies:
        copy.start()
    return lambda: [copy.wait() for copy in copies]


OWN_DIAG, OWN_OWN, OWN_MATE, MATE_DIAG, MATE_OWN = range(5)


def level_copies(levels, packed, weights, out):
    rows = weights.shape[1]
    copies = []
    for at, level in enumerate(levels):
        *owners, _ = unpack(packed, level)
        for half in range(2):
            copies.append((weights.at[owners[half]], out.at[at, pl.ds(half * rows, rows)]))
    return copies


def arrange_kernel(levels, packed, weights, out, sems):
    run(level_copies(levels, packed, weights, out), sems)()


def arrange_pairs_kernel(levels, packed, weights, mates, out, sems):
    rows = weights.shape[1]
    copies = []
    for at, level in enumerate(levels):
        *owners, side = unpack(packed, level)
        for half in range(2):
            here = pl.ds(half * rows, rows)
            kinds = [(OWN_DIAG, 0), (OWN_OWN, 2), (OWN_MATE, 1 + side)] if level else [(OWN_DIAG, 0)]
            for kind, block in kinds:
                source = weights.at[owners[half], :, pl.ds(block, 1)]
                copies.append((source, out.at[at, here, pl.ds(kind, 1)]))
            if level:
                copies.append((mates.at[owners[half]], out.at[at, here, pl.ds(MATE_DIAG, 2)]))
    run(copies, sems)()


def picked_from(places, around):
    at = lax.broadcasted_iota(jnp.int32, (places.shape[0], around.shape[0]), 1)
    return dot(ones_where(at == places), around)


def forward_kernel(level, at, share, fetched, packed, weights, places, side, far, own, near, out, *held):
    if fetched:
        held, sems = held
        wait = run(level_copies([level], packed, weights, held), sems)
        weights = held
    span = out.shape[0]
    picked = picked_from(places[level], jnp.concatenate([far[...], own[...], near[...]], axis=0))
    picked = jnp.concatenate([picked[n * span : (n + 1) * span] for n in range(3)], axis=1)
    if fetched:
        wait()
    total = products(dot, share, picked.astype(BF16), weights, at, slice(1, None))
    shifted = (side[level].astype(F32) - total).astype(BF16)
    out[...] = products(dot, share, shifted, weights, at, 0).astype(BF16)


def gathered_sums(level, at, share, blocks, places, own, mate):
    span = own.shape[0]
    picked = picked_from(places[level], jnp.concatenate([own, mate], axis=0)).astype(BF16)
    parts = [
        products(dot, share, picked[n * span : (n + 1) * span], blocks, at, kind)
        for n, kind in enumerate((OWN_OWN, MATE_OWN, OWN_MATE))
    ]
    return jnp.concatenate([parts[0] + parts[2], parts[1]], axis=0)


def pushed_sums(level, at, share, blocks, targets, own, mate):
    span = own.shape[0]
    pushed = [
        products(dot_t, share, vectors, blocks, at, kind)
        for vectors, kind in ((own, OWN_OWN), (mate, MATE_OWN), (own, OWN_MATE))
    ]
    pushed = jnp.concatenate(pushed, axis=0).astype(BF16)
    to = lax.broadcasted_iota(jnp.int32, (2 * span, 3 * span), 0)
    return dot(ones_where(to == targets[level]), pushed)


def pass_on(sums, held, sent):
    held[...] = sums
    sent[...] = sums.astype(BF16)


def joined(held, came):
    span = held.shape[0] // 2
    came = came[...].astype(F32)
    return held[:span] + came[span:], held[span:] + came[:span]


def entry_kernel(level, at, share, blocks, meets, own, mate, held, sent):
    pass_on(gathered_sums(level, at, share, blocks, meets, own[...], mate[...]), held, sent)


def forward_pair_kernel(
    level, at, share, last, blocks, meets, targets, side, side_mate, held, came,
    solved, solved_mate, to_hold, to_send,
):
    pair = []
    diags = OWN_DIAG, MATE_DIAG
    for total, right, diag in zip(joined(held, came), (side[level], side_mate[...]), diags):
        shifted = (right.astype(F32) - total).astype(BF16)
        pair.append(products(dot, share, shifted, blocks, at, diag).astype(BF16))
    solved[...], solved_mate[...] = pair
    if last:
        sums = pushed_sums(level, at, share, blocks, targets, *pair)
    else:
        sums = gathered_sums(level + 1, at + 1, share, blocks, meets, *pair)
    pass_on(sums, to_hold, to_send)


def backward_kernel(
    level, at, share, blocks, targets, solved, solved_mate, held, came, result, *outs
):
    pair = []
    diags = OWN_DIAG, MATE_DIAG
    for total, vector, diag in zip(joined(held, came), (solved, solved_mate), diags):
        part = products(dot, share, total.astype(BF16), blocks, at, diag)
        pair.append((vector[...].astype(F32) - part).astype(BF16))
    result[...] = pair[0]
    pass_on(pushed_sums(level, at, share, blocks, targets, *pair), *outs)


def last_kernel(share, packed, blocks, held, came, *rest):
    *rest, out = rest
    solved, results = rest[: packed.shape[0]], rest[packed.shape[0] :]
    part = products(dot, share, joined(held, came)[0].astype(BF16), blocks, 0, OWN_DIAG)
    result = (solved[0][...].astype(F32) - part).astype(BF16)
    size = out.shape[1] // 2
    for level in range(packed.shape[0]):
        *owners, _ = unpack(packed, level)
        for which, array in enumerate((solved[level], results[level - 1] if level else result)):
            for half in range(2):
                out[owners[half], which * size : (which + 1) * size] = array[half * size : (half + 1) * size]


def call(kernel, outs, *args, fetched=0, scratch=()):
    specs = [pl.BlockSpec(memory_space=pltpu.VMEM)] * len(args)
    args = list(args)
    for at in range(1, 1 + fetched):
        specs[at] = pl.BlockSpec(memory_space=pltpu.HBM)
        args[at] = pltpu.with_memory_space_constraint(args[at], pltpu.HBM)
    return pl.pallas_call(
        kernel,
        out_shape=outs,
        in_specs=specs,
        out_specs=[pl.BlockSpec(memory_space=pltpu.VMEM)] * len(outs),
        scratch_shapes=scratch,
        compiler_params=pltpu.CompilerParams(vmem_limit_bytes=16 * 2**20),
    )(*args)


def local(right_side, diag_inverse, off_blocks, columns, plan):
    rows, depth, width = right_side.shape
    doms = lax.axis_size("dom")
    levs = lax.axis_size("level")
    levels = levs // 2
    share = depth // levs
    count = 2 * rows
    dom = lax.axis_index("dom")
    lev = lax.axis_index("level")
    near_pairs = [(i, i ^ 1) for i in range(doms)]
    far_pairs = [(i, ((i + 1) ^ 1) - 1) for i in range(1, doms - 1)] + [(0, doms - 1), (doms - 1, 0)]

    weights = jnp.concatenate([diag_inverse[:, None], off_blocks], axis=1)
    weights = lax.all_gather(weights, "level")

    turn = dom % 2
    ids = jnp.arange(levs, dtype=jnp.int32)
    own_level = jnp.sum(jnp.where(ids == lev, plan, 0)) // 2
    inverse = jnp.sum(jnp.where(plan[None, :] == ids[:, None], ids[None, :], 0), axis=1)
    side_of = jnp.where(jnp.arange(levels) % 2 == 1, 2 * turn, 2 - 2 * turn)
    packed = inverse[0::2] + (inverse[1::2] << BITS) + (side_of << (2 * BITS))
    packed = jnp.broadcast_to(packed[:, None], (levels, 128)).astype(jnp.int32)

    here = jnp.where(own_level % 2 == turn, off_blocks[:, 0], off_blocks[:, 2])
    mates = jnp.stack([diag_inverse, here], axis=1)
    by_near = lax.ppermute(mates, "dom", near_pairs)
    by_far = lax.ppermute(mates, "dom", far_pairs)
    mates = jnp.where(own_level % 2 == 1, by_near, by_far)
    first = jnp.einsum("rkb,rbc->rkc", right_side, diag_inverse, preferred_element_type=F32)
    side = jnp.where(own_level == 0, first.astype(BF16), right_side)
    side = side.reshape(rows, levs, share, width)
    side = lax.all_to_all(side, "level", 1, 0, tiled=False)
    side = side.reshape(levs, rows * share, width)[inverse].reshape(levels, count * share, width)

    near_dom = dom + 1 - 2 * turn
    far_dom = (dom - 1 + 2 * turn) % doms
    part = jnp.stack(
        [
            lax.dynamic_slice_in_dim(columns, which * levs * rows, levs * rows, 0)
            for which in (dom, near_dom, far_dom)
        ]
    )
    part = part.reshape(3, levs, rows * 3)[:, inverse].reshape(3, levels, count, 3)
    second = jnp.roll(inverse[1::2], 1)[None, :, None, None]
    met = jnp.where(part // rows % levs == second, rows, 0) + part % rows
    odd = (jnp.arange(levels) % 2 == 1)[:, None]
    meets_own = met[0]
    meets_mate = jnp.where(odd[..., None], met[1], met[2])
    ahead = odd == (turn == 0)
    own_mate = jnp.where(ahead, meets_own[..., 0], meets_own[..., 2])
    mate_own = jnp.where(ahead, meets_mate[..., 0], meets_mate[..., 2])
    k = jnp.arange(share, dtype=jnp.int32)
    span = count * share
    slot = jnp.where(turn == 0, 1, -1) * (jnp.arange(3, dtype=jnp.int32) - 1) + 1
    places = meets_own.transpose(0, 2, 1) * share + slot[None, :, None] * span
    places = (places[..., None] + k).reshape(levels, 3 * span, 1)
    targets = jnp.stack([meets_own[..., 1], mate_own, own_mate + count], axis=1) * share
    targets = (targets[..., None] + k).reshape(levels, 3 * span)
    targets, meets = targets[:, None, :], targets[:, :, None]

    vector = jax.ShapeDtypeStruct((count * share, width), BF16)
    sums = [jax.ShapeDtypeStruct((2 * span, width), kind) for kind in (F32, BF16)]
    paired = levels - 2

    own = side[0]
    far = lax.ppermute(jnp.stack([own, side[paired]]), "dom", far_pairs)
    near = lax.ppermute(jnp.stack([own, side[paired + 1]]), "dom", near_pairs)
    mates, packed, side, places, targets, meets, own, far, near = lax.optimization_barrier(
        (mates, packed, side, places, targets, meets, own, far, near)
    )
    side_mates = [far[1], near[1]]
    far, near = far[0], near[0]
    mates = lax.all_gather(mates, "level")

    def swap(vector, level):
        return lax.ppermute(vector, "dom", far_pairs if level % 2 == 0 else near_pairs)

    def arranged(kernel, levels_now, kinds, copies, behind, *blocks):
        _, *blocks = lax.optimization_barrier((behind, *blocks))
        shape = (len(levels_now), count, kinds, width, width)
        kernel = functools.partial(kernel, levels_now)
        scratch = [pltpu.SemaphoreType.DMA((copies,))]
        outs = [jax.ShapeDtypeStruct(shape, BF16)]
        return call(kernel, outs, packed, *blocks, fetched=len(blocks), scratch=scratch)[0]

    solved = [own]
    solved_mate = []
    for level in range(1, paired):
        if level > 1:
            own = solved[-1]
            far, near = swap(own, 0), swap(own, 1)
        solved_mate.append(near if level % 2 == 0 else far)
        args = places, side, far, own, near
        if level == 1:
            scratch = [pltpu.VMEM((1, count, 4, width, width), BF16), pltpu.SemaphoreType.DMA((2,))]
            kernel = functools.partial(forward_kernel, level, 0, share, True)
            solved += call(kernel, [vector], packed, weights, *args, fetched=1, scratch=scratch)
            singles = range(2, paired)
            blocks = arranged(arrange_kernel, singles, 4, 2 * len(singles), solved[-1], weights)
        else:
            kernel = functools.partial(forward_kernel, level, level - 2, share, False)
            solved += call(kernel, [vector], packed, blocks, *args)

    solved_mate.append(swap(solved[-1], paired - 1))
    upper = range(paired, levels)
    blocks = arranged(arrange_pairs_kernel, upper, 5, 8 * len(upper), solved[-1], weights, mates)
    kernel = functools.partial(entry_kernel, paired, 0, share)
    held, sent = call(kernel, sums, blocks, meets, solved[-1], solved_mate[-1])
    lower = range(paired)
    below = arranged(arrange_pairs_kernel, lower, 5, 8 * len(lower) - 6, held, weights, mates)
    for level in upper:
        kernel = functools.partial(forward_pair_kernel, level, level - paired, share, level == levels - 1)
        args = blocks, meets, targets, side, side_mates[level - paired]
        own, mate, held, sent = call(kernel, [vector] * 2 + sums, *args, held, swap(sent, level))
        solved.append(own)
        solved_mate.append(mate)

    results = [own]
    for level in range(levels - 2, 0, -1):
        at = level - paired if level in upper else level
        kernel = functools.partial(backward_kernel, level, at, share)
        args = blocks if level in upper else below, targets, solved[level], solved_mate[level]
        result, held, sent = call(kernel, [vector] + sums, *args, held, swap(sent, level))
        results.append(result)

    dealt = jax.ShapeDtypeStruct((levs, 2 * rows * share, width), BF16)
    kernel = functools.partial(last_kernel, share)
    (dealt,) = call(kernel, [dealt], packed, below, held, swap(sent, 0), *solved, *results[::-1])
    dealt = lax.all_to_all(dealt, "level", 0, 0, tiled=False)
    dealt = dealt.reshape(levs, 2, rows, share, width).transpose(1, 2, 0, 3, 4)
    dealt = dealt.reshape(2, rows, depth, width)
    return dealt[0], dealt[1]


def solution(mesh):
    return jax.shard_map(
        local,
        mesh=mesh,
        in_specs=(
            P(("dom", "level"), None, None),
            P(("dom", "level"), None, None),
            P(("dom", "level"), None, None, None),
            P(),
            P(),
        ),
        out_specs=(P(("dom", "level"), None, None), P(("dom", "level"), None, None)),
        check_vma=False,
    )
```

```python
import functools

import jax
import jax.numpy as jnp
from jax import lax
from jax.experimental import pallas as pl
from jax.experimental.pallas import tpu as pltpu
from jax.sharding import PartitionSpec as P

BF16 = jnp.bfloat16
F32 = jnp.float32


def dot(a, b):
    return lax.dot_general(a, b, (((1,), (0,)), ((), ())), preferred_element_type=F32)


def dot_t(a, b):
    return lax.dot_general(a, b, (((1,), (1,)), ((), ())), preferred_element_type=F32)


def either(low, high, share):
    top = lax.broadcasted_iota(jnp.int32, low.shape, 0) < share
    return jnp.where(top, low, high)


def ones_where(condition):
    return jnp.where(condition, 1.0, 0.0).astype(BF16)


BITS = 8


def unpack(packed, level):
    value = jnp.max(packed[level : level + 1])
    mask = (1 << BITS) - 1
    return value & mask, (value >> BITS) & mask, value >> (2 * BITS)


def products(product, share, vectors, blocks, level, kind):
    totals = []
    for row in range(0, blocks.shape[1], 2):
        part = vectors[share * row : share * (row + 2)]
        wide = [blocks[level, row + one, kind] for one in range(2)]
        if isinstance(kind, slice):
            wide = [block.reshape(-1, block.shape[-1]) for block in wide]
        totals.append(either(*[product(part, block) for block in wide], share))
    return jnp.concatenate(totals, axis=0)


OWN_DIAG, OWN_OWN, OWN_MATE, MATE_DIAG, MATE_OWN = range(5)


def arrange_kernel(slots, *rest):
    *pieces, out, sems = rest
    copies = []
    at = 0
    for piece in pieces:
        kinds = pl.ds(MATE_DIAG if piece.shape[2] == 2 else 0, piece.shape[2])
        for sub in range(piece.shape[0]):
            which = at + sub - (2 if piece.shape[2] == 2 else 0)
            slot = jnp.max(slots[which : which + 1])
            copies.append(
                pltpu.make_async_copy(piece.at[sub], out.at[slot, :, kinds], sems.at[len(copies)])
            )
        at += 0 if piece.shape[2] == 2 else piece.shape[0]
    for copy in copies:
        copy.start()
    for copy in copies:
        copy.wait()


def picked_from(places, around):
    at = lax.broadcasted_iota(jnp.int32, (places.shape[0], around.shape[0]), 1)
    return dot(ones_where(at == places), around)


def gathered_sums(level, at, share, blocks, places, own, mate):
    span = own.shape[0]
    picked = picked_from(places[level], jnp.concatenate([own, mate], axis=0)).astype(BF16)
    parts = [
        products(dot, share, picked[n * span : (n + 1) * span], blocks, at, kind)
        for n, kind in enumerate((OWN_OWN, MATE_OWN, OWN_MATE))
    ]
    return jnp.concatenate([parts[0] + parts[2], parts[1]], axis=0)


def pushed_sums(level, at, share, blocks, targets, own, mate):
    span = own.shape[0]
    pushed = [
        products(dot_t, share, vectors, blocks, at, kind)
        for vectors, kind in ((own, OWN_OWN), (mate, MATE_OWN), (own, OWN_MATE))
    ]
    pushed = jnp.concatenate(pushed, axis=0).astype(BF16)
    to = lax.broadcasted_iota(jnp.int32, (2 * span, 3 * span), 0)
    return dot(ones_where(to == targets[level]), pushed)


def pass_on(sums, held, sent):
    held[...] = sums
    sent[...] = sums.astype(BF16)


def joined(held, came):
    span = held.shape[0] // 2
    came = came[...].astype(F32)
    return held[:span] + came[span:], held[span:] + came[:span]


def entry_kernel(level, at, share, blocks, meets, own, mate, held, sent):
    pass_on(gathered_sums(level, at, share, blocks, meets, own[...], mate[...]), held, sent)


def forward_pair_kernel(
    level, at, share, last, blocks, meets, targets, side, side_mate, held, came,
    solved, solved_mate, to_hold, to_send,
):
    pair = []
    diags = OWN_DIAG, MATE_DIAG
    for total, right, diag in zip(joined(held, came), (side[level], side_mate[...]), diags):
        shifted = (right.astype(F32) - total).astype(BF16)
        pair.append(products(dot, share, shifted, blocks, at, diag).astype(BF16))
    solved[...], solved_mate[...] = pair
    if last:
        sums = pushed_sums(level, at, share, blocks, targets, *pair)
    else:
        sums = gathered_sums(level + 1, at + 1, share, blocks, meets, *pair)
    pass_on(sums, to_hold, to_send)


def backward_kernel(
    level, at, share, blocks, targets, solved, solved_mate, held, came, result, *outs
):
    pair = []
    diags = OWN_DIAG, MATE_DIAG
    for total, vector, diag in zip(joined(held, came), (solved, solved_mate), diags):
        part = products(dot, share, total.astype(BF16), blocks, at, diag)
        pair.append((vector[...].astype(F32) - part).astype(BF16))
    result[...] = pair[0]
    pass_on(pushed_sums(level, at, share, blocks, targets, *pair), *outs)


def last_kernel(share, packed, blocks, held, came, *rest):
    *rest, out = rest
    solved, results = rest[: packed.shape[0]], rest[packed.shape[0] :]
    part = products(dot, share, joined(held, came)[0].astype(BF16), blocks, 0, OWN_DIAG)
    result = (solved[0][...].astype(F32) - part).astype(BF16)
    size = out.shape[1] // 2
    for level in range(packed.shape[0]):
        *owners, _ = unpack(packed, level)
        for which, array in enumerate((solved[level], results[level - 1] if level else result)):
            for half in range(2):
                out[owners[half], which * size : (which + 1) * size] = array[half * size : (half + 1) * size]


def call(kernel, outs, *args, anywhere=0, scratch=()):
    vmem, kept = [pl.BlockSpec(memory_space=space) for space in (pltpu.VMEM, pl.ANY)]
    specs = [vmem] + [kept] * anywhere + [vmem] * (len(args) - 1 - anywhere)
    return pl.pallas_call(
        kernel,
        out_shape=outs,
        in_specs=specs,
        out_specs=[vmem] * len(outs),
        scratch_shapes=scratch,
        compiler_params=pltpu.CompilerParams(vmem_limit_bytes=16 * 2**20),
    )(*args)


def local(right_side, diag_inverse, off_blocks, columns, plan):
    rows, depth, width = right_side.shape
    doms = lax.axis_size("dom")
    levs = lax.axis_size("level")
    levels = levs // 2
    share = depth // levs
    count = 2 * rows
    dom = lax.axis_index("dom")
    turn = dom % 2
    lev = lax.axis_index("level")
    near_pairs = [(i, i ^ 1) for i in range(doms)]
    far_pairs = [(i, ((i + 1) ^ 1) - 1) for i in range(1, doms - 1)] + [(0, doms - 1), (doms - 1, 0)]

    ids = jnp.arange(levs, dtype=jnp.int32)
    own_level = jnp.sum(jnp.where(ids == lev, plan, 0)) // 2
    inverse = jnp.sum(jnp.where(plan[None, :] == ids[:, None], ids[None, :], 0), axis=1)
    side_of = jnp.where(jnp.arange(levels) % 2 == 1, 2 * turn, 2 - 2 * turn)
    packed = inverse[0::2] + (inverse[1::2] << BITS) + (side_of << (2 * BITS))
    packed = jnp.broadcast_to(packed[:, None], (levels, 128)).astype(jnp.int32)

    low = own_level % 2 == turn
    pieces = jnp.where(low, off_blocks[:, 2], off_blocks[:, 0])
    pieces = jnp.stack([diag_inverse, off_blocks[:, 1], pieces], axis=1)
    mates = jnp.stack([diag_inverse, jnp.where(low, off_blocks[:, 0], off_blocks[:, 2])], axis=1)

    chips = levs // 2
    ring = [(2 * y, 2 * ((y + 1) % chips)) for y in range(chips)]
    ring += [(2 * y + 1, 2 * ((y - 1) % chips) + 1) for y in range(chips)]
    cores = [(i, i ^ 1) for i in range(levs)]
    pieces = jnp.stack([pieces, lax.ppermute(pieces, "level", cores)])
    came = lax.ppermute(pieces, "level", ring)
    by_near = lax.ppermute(mates, "dom", near_pairs)
    by_far = lax.ppermute(mates, "dom", far_pairs)
    mates = jnp.where(own_level % 2 == 1, by_near, by_far)
    mates = jnp.stack([mates, lax.ppermute(mates, "level", cores)])
    came = jnp.concatenate([came, lax.ppermute(mates, "level", ring)], axis=2)
    core, chip = lev % 2, lev // 2
    arrays = [pieces, mates]
    places = [2 * chip + core, 2 * chip + 1 - core]
    for step in range(1, chips // 2 + 1):
        if step > 1:
            came = lax.ppermute(came if step < chips // 2 else came[:1], "level", ring)
        shared = lax.ppermute(came, "level", cores)
        for array, side in ((came, core), (shared, 1 - core)):
            arrays.append(array)
            there = (chip - step + 2 * step * side) % chips
            places += [2 * there + side, 2 * there + 1 - side][: array.shape[0]]
    places = jnp.stack(places)
    slots = jnp.sum(jnp.where(places[:, None] == ids, plan, 0), axis=1)
    slots = jnp.broadcast_to(slots[:, None], (levs, 128)).astype(jnp.int32)

    first = jnp.einsum("rkb,rbc->rkc", right_side, diag_inverse, preferred_element_type=F32)
    side = jnp.where(own_level == 0, first.astype(BF16), right_side)
    side = side.reshape(rows, levs, share, width)
    side = lax.all_to_all(side, "level", 1, 0, tiled=False)
    side = side.reshape(levs, rows * share, width)[inverse].reshape(levels, count * share, width)

    near_dom = dom + 1 - 2 * turn
    far_dom = (dom - 1 + 2 * turn) % doms
    part = jnp.stack(
        [
            lax.dynamic_slice_in_dim(columns, which * levs * rows, levs * rows, 0)
            for which in (dom, near_dom, far_dom)
        ]
    )
    part = part.reshape(3, levs, rows * 3)[:, inverse].reshape(3, levels, count, 3)
    second = jnp.roll(inverse[1::2], 1)[None, :, None, None]
    met = jnp.where(part // rows % levs == second, rows, 0) + part % rows
    odd = (jnp.arange(levels) % 2 == 1)[:, None]
    meets_own = met[0]
    meets_mate = jnp.where(odd[..., None], met[1], met[2])
    ahead = odd == (turn == 0)
    own_mate = jnp.where(ahead, meets_own[..., 0], meets_own[..., 2])
    mate_own = jnp.where(ahead, meets_mate[..., 0], meets_mate[..., 2])
    k = jnp.arange(share, dtype=jnp.int32)
    span = count * share
    targets = jnp.stack([meets_own[..., 1], mate_own, own_mate + count], axis=1) * share
    targets = (targets[..., None] + k).reshape(levels, 3 * span)
    targets, meets = targets[:, None, :], targets[:, :, None]

    vector = jax.ShapeDtypeStruct((count * share, width), BF16)
    sums = [jax.ShapeDtypeStruct((2 * span, width), kind) for kind in (F32, BF16)]

    def swap(vector, level):
        return lax.ppermute(vector, "dom", far_pairs if level % 2 == 0 else near_pairs)

    side_mates = swap(side[0::2], 0), swap(side[1::2], 1)
    packed, slots, side, targets, meets, side_mates, arrays = lax.optimization_barrier(
        (packed, slots, side, targets, meets, side_mates, arrays)
    )
    kernel_scratch = [pltpu.SemaphoreType.DMA((levs + 2,))]
    outs = [jax.ShapeDtypeStruct((levs, rows, 5, width, width), BF16)]
    (blocks,) = call(arrange_kernel, outs, slots, *arrays, anywhere=len(arrays), scratch=kernel_scratch)
    blocks = blocks.reshape(levels, count, 5, width, width)

    solved = [side[0]]
    solved_mate = [side_mates[0][0]]
    kernel = functools.partial(entry_kernel, 1, 1, share)
    held, sent = call(kernel, sums, blocks, meets, solved[0], solved_mate[0])
    for level in range(1, levels):
        kernel = functools.partial(forward_pair_kernel, level, level, share, level == levels - 1)
        args = blocks, meets, targets, side, side_mates[level % 2][level // 2]
        own, mate, held, sent = call(kernel, [vector] * 2 + sums, *args, held, swap(sent, level))
        solved.append(own)
        solved_mate.append(mate)

    results = [own]
    for level in range(levels - 2, 0, -1):
        kernel = functools.partial(backward_kernel, level, level, share)
        args = blocks, targets, solved[level], solved_mate[level]
        result, held, sent = call(kernel, [vector] + sums, *args, held, swap(sent, level))
        results.append(result)

    dealt = jax.ShapeDtypeStruct((levs, 2 * rows * share, width), BF16)
    kernel = functools.partial(last_kernel, share)
    (dealt,) = call(kernel, [dealt], packed, blocks, held, swap(sent, 0), *solved, *results[::-1])
    dealt = lax.all_to_all(dealt, "level", 0, 0, tiled=False)
    dealt = dealt.reshape(levs, 2, rows, share, width).transpose(1, 2, 0, 3, 4)
    dealt = dealt.reshape(2, rows, depth, width)
    return dealt[0], dealt[1]


def solution(mesh):
    return jax.shard_map(
        local,
        mesh=mesh,
        in_specs=(
            P(("dom", "level"), None, None),
            P(("dom", "level"), None, None),
            P(("dom", "level"), None, None, None),
            P(),
            P(),
        ),
        out_specs=(P(("dom", "level"), None, None), P(("dom", "level"), None, None)),
        check_vma=False,
    )
```

```python
import functools

import jax
import jax.numpy as jnp
from jax import lax
from jax.experimental import pallas as pl
from jax.experimental.pallas import tpu as pltpu
from jax.sharding import PartitionSpec as P

BF16 = jnp.bfloat16
F32 = jnp.float32


def dot(a, b):
    return lax.dot_general(a, b, (((1,), (0,)), ((), ())), preferred_element_type=F32)


def dot_t(a, b):
    return lax.dot_general(a, b, (((1,), (1,)), ((), ())), preferred_element_type=F32)


def either(low, high, share):
    top = lax.broadcasted_iota(jnp.int32, low.shape, 0) < share
    return jnp.where(top, low, high)


def ones_where(condition):
    return jnp.where(condition, 1.0, 0.0).astype(BF16)


BITS = 8


def unpack(packed, level):
    value = jnp.max(packed[level : level + 1])
    mask = (1 << BITS) - 1
    return value & mask, (value >> BITS) & mask, value >> (2 * BITS)


def products(product, share, vectors, blocks, level, kind):
    totals = []
    for row in range(0, blocks.shape[1], 2):
        part = vectors[share * row : share * (row + 2)]
        wide = [blocks[level, row + one, kind] for one in range(2)]
        if isinstance(kind, slice):
            wide = [block.reshape(-1, block.shape[-1]) for block in wide]
        totals.append(either(*[product(part, block) for block in wide], share))
    return jnp.concatenate(totals, axis=0)


def run(copies, sems):
    copies = [pltpu.make_async_copy(*ends, sems.at[which]) for which, ends in enumerate(copies)]
    for copy in copies:
        copy.start()
    return lambda: [copy.wait() for copy in copies]


OWN_DIAG, OWN_OWN, OWN_MATE, MATE_DIAG, MATE_OWN = range(5)


def level_copies(levels, packed, weights, out):
    rows = weights.shape[1]
    copies = []
    for at, level in enumerate(levels):
        *owners, _ = unpack(packed, level)
        for half in range(2):
            copies.append((weights.at[owners[half]], out.at[at, pl.ds(half * rows, rows)]))
    return copies


def arrange_kernel(levels, packed, weights, out, sems):
    run(level_copies(levels, packed, weights, out), sems)()


def arrange_pairs_kernel(levels, packed, weights, mates, out, sems):
    rows = weights.shape[1]
    copies = []
    for at, level in enumerate(levels):
        *owners, side = unpack(packed, level)
        for half in range(2):
            here = pl.ds(half * rows, rows)
            kinds = [(OWN_DIAG, 0), (OWN_OWN, 2), (OWN_MATE, 1 + side)] if level else [(OWN_DIAG, 0)]
            for kind, block in kinds:
                source = weights.at[owners[half], :, pl.ds(block, 1)]
                copies.append((source, out.at[at, here, pl.ds(kind, 1)]))
            if level:
                copies.append((mates.at[owners[half]], out.at[at, here, pl.ds(MATE_DIAG, 2)]))
    run(copies, sems)()


def picked_from(places, around):
    at = lax.broadcasted_iota(jnp.int32, (places.shape[0], around.shape[0]), 1)
    return dot(ones_where(at == places), around)


def forward_kernel(level, at, share, fetched, packed, weights, places, side, far, own, near, out, *held):
    if fetched:
        held, sems = held
        wait = run(level_copies([level], packed, weights, held), sems)
        weights = held
    span = out.shape[0]
    picked = picked_from(places[level], jnp.concatenate([far[...], own[...], near[...]], axis=0))
    picked = jnp.concatenate([picked[n * span : (n + 1) * span] for n in range(3)], axis=1)
    if fetched:
        wait()
    total = products(dot, share, picked.astype(BF16), weights, at, slice(1, None))
    shifted = (side[level].astype(F32) - total).astype(BF16)
    out[...] = products(dot, share, shifted, weights, at, 0).astype(BF16)


def gathered_sums(level, at, share, blocks, places, own, mate):
    span = own.shape[0]
    picked = picked_from(places[level], jnp.concatenate([own, mate], axis=0)).astype(BF16)
    parts = [
        products(dot, share, picked[n * span : (n + 1) * span], blocks, at, kind)
        for n, kind in enumerate((OWN_OWN, MATE_OWN, OWN_MATE))
    ]
    return jnp.concatenate([parts[0] + parts[2], parts[1]], axis=0)


def pushed_sums(level, at, share, blocks, targets, own, mate):
    span = own.shape[0]
    pushed = [
        products(dot_t, share, vectors, blocks, at, kind)
        for vectors, kind in ((own, OWN_OWN), (mate, MATE_OWN), (own, OWN_MATE))
    ]
    pushed = jnp.concatenate(pushed, axis=0).astype(BF16)
    to = lax.broadcasted_iota(jnp.int32, (2 * span, 3 * span), 0)
    return dot(ones_where(to == targets[level]), pushed)


def pass_on(sums, held, sent):
    held[...] = sums
    sent[...] = sums.astype(BF16)


def joined(held, came):
    span = held.shape[0] // 2
    came = came[...].astype(F32)
    return held[:span] + came[span:], held[span:] + came[:span]


def entry_kernel(level, at, share, blocks, meets, own, mate, held, sent):
    pass_on(gathered_sums(level, at, share, blocks, meets, own[...], mate[...]), held, sent)


def forward_pair_kernel(
    level, at, share, last, blocks, meets, targets, side, side_mate, held, came,
    solved, solved_mate, to_hold, to_send,
):
    pair = []
    diags = OWN_DIAG, MATE_DIAG
    for total, right, diag in zip(joined(held, came), (side[level], side_mate[...]), diags):
        shifted = (right.astype(F32) - total).astype(BF16)
        pair.append(products(dot, share, shifted, blocks, at, diag).astype(BF16))
    solved[...], solved_mate[...] = pair
    if last:
        sums = pushed_sums(level, at, share, blocks, targets, *pair)
    else:
        sums = gathered_sums(level + 1, at + 1, share, blocks, meets, *pair)
    pass_on(sums, to_hold, to_send)


def backward_kernel(
    level, at, share, blocks, targets, solved, solved_mate, held, came, result, *outs
):
    pair = []
    diags = OWN_DIAG, MATE_DIAG
    for total, vector, diag in zip(joined(held, came), (solved, solved_mate), diags):
        part = products(dot, share, total.astype(BF16), blocks, at, diag)
        pair.append((vector[...].astype(F32) - part).astype(BF16))
    result[...] = pair[0]
    pass_on(pushed_sums(level, at, share, blocks, targets, *pair), *outs)


def last_kernel(share, packed, blocks, held, came, *rest):
    *rest, out = rest
    solved, results = rest[: packed.shape[0]], rest[packed.shape[0] :]
    part = products(dot, share, joined(held, came)[0].astype(BF16), blocks, 0, OWN_DIAG)
    result = (solved[0][...].astype(F32) - part).astype(BF16)
    size = out.shape[1] // 2
    for level in range(packed.shape[0]):
        *owners, _ = unpack(packed, level)
        for which, array in enumerate((solved[level], results[level - 1] if level else result)):
            for half in range(2):
                out[owners[half], which * size : (which + 1) * size] = array[half * size : (half + 1) * size]


def call(kernel, outs, *args, fetched=0, scratch=()):
    specs = [pl.BlockSpec(memory_space=pltpu.VMEM)] * len(args)
    args = list(args)
    for at in range(1, 1 + fetched):
        specs[at] = pl.BlockSpec(memory_space=pltpu.HBM)
        args[at] = pltpu.with_memory_space_constraint(args[at], pltpu.HBM)
    return pl.pallas_call(
        kernel,
        out_shape=outs,
        in_specs=specs,
        out_specs=[pl.BlockSpec(memory_space=pltpu.VMEM)] * len(outs),
        scratch_shapes=scratch,
        compiler_params=pltpu.CompilerParams(vmem_limit_bytes=16 * 2**20),
    )(*args)


def local(right_side, diag_inverse, off_blocks, columns, plan):
    rows, depth, width = right_side.shape
    doms = lax.axis_size("dom")
    levs = lax.axis_size("level")
    levels = levs // 2
    share = depth // levs
    count = 2 * rows
    dom = lax.axis_index("dom")
    lev = lax.axis_index("level")
    near_pairs = [(i, i ^ 1) for i in range(doms)]
    far_pairs = [(i, ((i + 1) ^ 1) - 1) for i in range(1, doms - 1)] + [(0, doms - 1), (doms - 1, 0)]

    weights = jnp.concatenate([diag_inverse[:, None], off_blocks], axis=1)
    weights = lax.all_gather(weights, "level")

    turn = dom % 2
    ids = jnp.arange(levs, dtype=jnp.int32)
    own_level = jnp.sum(jnp.where(ids == lev, plan, 0)) // 2
    inverse = jnp.sum(jnp.where(plan[None, :] == ids[:, None], ids[None, :], 0), axis=1)
    side_of = jnp.where(jnp.arange(levels) % 2 == 0, 2 * turn, 2 - 2 * turn)
    packed = inverse[0::2] + (inverse[1::2] << BITS) + (side_of << (2 * BITS))
    packed = jnp.broadcast_to(packed[:, None], (levels, 128)).astype(jnp.int32)

    here = jnp.where(own_level % 2 == turn, off_blocks[:, 2], off_blocks[:, 0])
    mates = jnp.stack([diag_inverse, here], axis=1)
    by_near = lax.ppermute(mates, "dom", near_pairs)
    by_far = lax.ppermute(mates, "dom", far_pairs)
    mates = jnp.where(own_level % 2 == 1, by_far, by_near)
    first = jnp.einsum("rkb,rbc->rkc", right_side, diag_inverse, preferred_element_type=F32)
    side = jnp.where(own_level == 0, first.astype(BF16), right_side)
    side = side.reshape(rows, levs, share, width)
    side = lax.all_to_all(side, "level", 1, 0, tiled=False)
    side = side.reshape(levs, rows * share, width)[inverse].reshape(levels, count * share, width)

    near_dom = dom + 1 - 2 * turn
    far_dom = (dom - 1 + 2 * turn) % doms
    part = jnp.stack(
        [
            lax.dynamic_slice_in_dim(columns, which * levs * rows, levs * rows, 0)
            for which in (dom, near_dom, far_dom)
        ]
    )
    part = part.reshape(3, levs, rows * 3)[:, inverse].reshape(3, levels, count, 3)
    second = jnp.roll(inverse[1::2], 1)[None, :, None, None]
    met = jnp.where(part // rows % levs == second, rows, 0) + part % rows
    odd = (jnp.arange(levels) % 2 == 1)[:, None]
    meets_own = met[0]
    meets_mate = jnp.where(odd[..., None], met[2], met[1])
    ahead = odd == (turn == 1)
    own_mate = jnp.where(ahead, meets_own[..., 0], meets_own[..., 2])
    mate_own = jnp.where(ahead, meets_mate[..., 0], meets_mate[..., 2])
    k = jnp.arange(share, dtype=jnp.int32)
    span = count * share
    slot = jnp.where(turn == 0, 1, -1) * (jnp.arange(3, dtype=jnp.int32) - 1) + 1
    places = meets_own.transpose(0, 2, 1) * share + slot[None, :, None] * span
    places = (places[..., None] + k).reshape(levels, 3 * span, 1)
    targets = jnp.stack([meets_own[..., 1], mate_own, own_mate + count], axis=1) * share
    targets = (targets[..., None] + k).reshape(levels, 3 * span)
    targets, meets = targets[:, None, :], targets[:, :, None]

    vector = jax.ShapeDtypeStruct((count * share, width), BF16)
    sums = [jax.ShapeDtypeStruct((2 * span, width), kind) for kind in (F32, BF16)]
    paired = levels - 2

    own = side[0]
    far = lax.ppermute(jnp.stack([own, side[paired + 1]]), "dom", far_pairs)
    near = lax.ppermute(jnp.stack([own, side[paired]]), "dom", near_pairs)
    mates, packed, side, places, targets, meets, own, far, near = lax.optimization_barrier(
        (mates, packed, side, places, targets, meets, own, far, near)
    )
    side_mates = [near[1], far[1]]
    far, near = far[0], near[0]
    mates = lax.all_gather(mates, "level")

    def swap(vector, level):
        return lax.ppermute(vector, "dom", far_pairs if level % 2 else near_pairs)

    def arranged(kernel, levels_now, kinds, copies, behind, *blocks):
        _, *blocks = lax.optimization_barrier((behind, *blocks))
        shape = (len(levels_now), count, kinds, width, width)
        kernel = functools.partial(kernel, levels_now)
        scratch = [pltpu.SemaphoreType.DMA((copies,))]
        outs = [jax.ShapeDtypeStruct(shape, BF16)]
        return call(kernel, outs, packed, *blocks, fetched=len(blocks), scratch=scratch)[0]

    solved = [own]
    solved_mate = []
    for level in range(1, paired):
        if level > 1:
            own = solved[-1]
            far, near = swap(own, 1), swap(own, 0)
        solved_mate.append(far if level % 2 == 0 else near)
        args = places, side, far, own, near
        if level == 1:
            scratch = [pltpu.VMEM((1, count, 4, width, width), BF16), pltpu.SemaphoreType.DMA((2,))]
            kernel = functools.partial(forward_kernel, level, 0, share, True)
            solved += call(kernel, [vector], packed, weights, *args, fetched=1, scratch=scratch)
            singles = range(2, paired)
            blocks = arranged(arrange_kernel, singles, 4, 2 * len(singles), solved[-1], weights)
        else:
            kernel = functools.partial(forward_kernel, level, level - 2, share, False)
            solved += call(kernel, [vector], packed, blocks, *args)

    solved_mate.append(swap(solved[-1], paired - 1))
    upper = range(paired, levels)
    blocks = arranged(arrange_pairs_kernel, upper, 5, 8 * len(upper), solved[-1], weights, mates)
    kernel = functools.partial(entry_kernel, paired, 0, share)
    held, sent = call(kernel, sums, blocks, meets, solved[-1], solved_mate[-1])
    lower = range(paired)
    below = arranged(arrange_pairs_kernel, lower, 5, 8 * len(lower) - 6, held, weights, mates)
    for level in upper:
        kernel = functools.partial(forward_pair_kernel, level, level - paired, share, level == levels - 1)
        args = blocks, meets, targets, side, side_mates[level - paired]
        own, mate, held, sent = call(kernel, [vector] * 2 + sums, *args, held, swap(sent, level))
        solved.append(own)
        solved_mate.append(mate)

    results = [own]
    for level in range(levels - 2, 0, -1):
        at = level - paired if level in upper else level
        kernel = functools.partial(backward_kernel, level, at, share)
        args = blocks if level in upper else below, targets, solved[level], solved_mate[level]
        result, held, sent = call(kernel, [vector] + sums, *args, held, swap(sent, level))
        results.append(result)

    dealt = jax.ShapeDtypeStruct((levs, 2 * rows * share, width), BF16)
    kernel = functools.partial(last_kernel, share)
    (dealt,) = call(kernel, [dealt], packed, below, held, swap(sent, 0), *solved, *results[::-1])
    dealt = lax.all_to_all(dealt, "level", 0, 0, tiled=False)
    dealt = dealt.reshape(levs, 2, rows, share, width).transpose(1, 2, 0, 3, 4)
    dealt = dealt.reshape(2, rows, depth, width)
    return dealt[0], dealt[1]


def solution(mesh):
    return jax.shard_map(
        local,
        mesh=mesh,
        in_specs=(
            P(("dom", "level"), None, None),
            P(("dom", "level"), None, None),
            P(("dom", "level"), None, None, None),
            P(),
            P(),
        ),
        out_specs=(P(("dom", "level"), None, None), P(("dom", "level"), None, None)),
        check_vma=False,
    )
```

```python
import functools

import jax
import jax.numpy as jnp
from jax import lax
from jax.experimental import pallas as pl
from jax.experimental.pallas import tpu as pltpu
from jax.sharding import PartitionSpec as P

BF16 = jnp.bfloat16
F32 = jnp.float32


def dot(a, b):
    return lax.dot_general(a, b, (((1,), (0,)), ((), ())), preferred_element_type=F32)


def dot_t(a, b):
    return lax.dot_general(a, b, (((1,), (1,)), ((), ())), preferred_element_type=F32)


def either(low, high, share):
    top = lax.broadcasted_iota(jnp.int32, low.shape, 0) < share
    return jnp.where(top, low, high)


def ones_where(condition):
    return jnp.where(condition, 1.0, 0.0).astype(BF16)


BITS = 8


def unpack(packed, level):
    value = jnp.max(packed[level : level + 1])
    mask = (1 << BITS) - 1
    return value & mask, (value >> BITS) & mask, value >> (2 * BITS)


def products(product, share, vectors, blocks, level, kind):
    totals = []
    for row in range(0, blocks.shape[1], 2):
        part = vectors[share * row : share * (row + 2)]
        wide = [blocks[level, row + one, kind] for one in range(2)]
        totals.append(either(*[product(part, block) for block in wide], share))
    return jnp.concatenate(totals, axis=0)


def flat_products(share, vectors, blocks, level, off):
    totals = []
    rows = vectors.shape[0] // (2 * share)
    for row in range(0, 2 * rows, 2):
        part = vectors[share * row : share * (row + 2)]
        wide = []
        for one in range(2):
            half, at = divmod(row + one, rows)
            if off:
                n = blocks.shape[2] // rows - 1
                block = blocks[level, half, rows + n * at : rows + n * (at + 1)]
                wide.append(block.reshape(-1, block.shape[-1]))
            else:
                wide.append(blocks[level, half, at])
        totals.append(either(*[dot(part, block) for block in wide], share))
    return jnp.concatenate(totals, axis=0)


def run(copies, sems):
    copies = [pltpu.make_async_copy(*ends, sems.at[which]) for which, ends in enumerate(copies)]
    for copy in copies:
        copy.start()
    return lambda: [copy.wait() for copy in copies]


OWN_DIAG, OWN_OWN, OWN_MATE, MATE_DIAG, MATE_OWN = range(5)


def level_copies(levels, packed, weights, out):
    copies = []
    for at, level in enumerate(levels):
        *owners, _ = unpack(packed, level)
        copies += [(weights.at[owners[half]], out.at[at, half]) for half in range(2)]
    return copies


def arrange_kernel(levels, packed, weights, out, sems):
    run(level_copies(levels, packed, weights, out), sems)()


def arrange_pairs_kernel(levels, packed, weights, mates, out, sems):
    rows = mates.shape[1]
    off = weights.shape[1] - rows
    copies = []
    for at, level in enumerate(levels):
        *owners, side = unpack(packed, level)
        for half in range(2):
            here = pl.ds(half * rows, rows)
            copies.append((weights.at[owners[half], pl.ds(0, rows)], out.at[at, here, OWN_DIAG]))
            if level:
                offs = weights.at[owners[half], pl.ds(rows, off)]
                offs = offs.reshape((rows, off // rows) + weights.shape[2:])
                copies.append((offs.at[:, 1], out.at[at, here, OWN_OWN]))
                copies.append((offs.at[:, side], out.at[at, here, OWN_MATE]))
                copies.append((mates.at[owners[half]], out.at[at, here, pl.ds(MATE_DIAG, 2)]))
    run(copies, sems)()


def picked_from(places, around):
    at = lax.broadcasted_iota(jnp.int32, (places.shape[0], around.shape[0]), 1)
    return dot(ones_where(at == places), around)


def forward_kernel(level, at, share, fetched, packed, weights, places, side, far, own, near, out, *held):
    if fetched:
        held, sems = held
        wait = run(level_copies([level], packed, weights, held), sems)
        weights = held
    span = out.shape[0]
    picked = picked_from(places[level], jnp.concatenate([far[...], own[...], near[...]], axis=0))
    picked = jnp.concatenate([picked[n * span : (n + 1) * span] for n in range(3)], axis=1)
    if fetched:
        wait()
    total = flat_products(share, picked.astype(BF16), weights, at, True)
    shifted = (side[level].astype(F32) - total).astype(BF16)
    out[...] = flat_products(share, shifted, weights, at, False).astype(BF16)


def gathered_sums(level, at, share, blocks, places, own, mate):
    span = own.shape[0]
    picked = picked_from(places[level], jnp.concatenate([own, mate], axis=0)).astype(BF16)
    parts = [
        products(dot, share, picked[n * span : (n + 1) * span], blocks, at, kind)
        for n, kind in enumerate((OWN_OWN, MATE_OWN, OWN_MATE))
    ]
    return jnp.concatenate([parts[0] + parts[2], parts[1]], axis=0)


def pushed_sums(level, at, share, blocks, targets, own, mate):
    span = own.shape[0]
    pushed = [
        products(dot_t, share, vectors, blocks, at, kind)
        for vectors, kind in ((own, OWN_OWN), (mate, MATE_OWN), (own, OWN_MATE))
    ]
    pushed = jnp.concatenate(pushed, axis=0).astype(BF16)
    to = lax.broadcasted_iota(jnp.int32, (2 * span, 3 * span), 0)
    return dot(ones_where(to == targets[level]), pushed)


def pass_on(sums, held, sent):
    held[...] = sums
    sent[...] = sums.astype(BF16)


def joined(held, came):
    span = held.shape[0] // 2
    came = came[...].astype(F32)
    return held[:span] + came[span:], held[span:] + came[:span]


def entry_kernel(level, at, share, blocks, meets, own, mate, held, sent):
    pass_on(gathered_sums(level, at, share, blocks, meets, own[...], mate[...]), held, sent)


def forward_pair_kernel(
    level, at, share, last, blocks, meets, targets, side, side_mate, held, came,
    solved, solved_mate, to_hold, to_send,
):
    pair = []
    diags = OWN_DIAG, MATE_DIAG
    for total, right, diag in zip(joined(held, came), (side[level], side_mate[...]), diags):
        shifted = (right.astype(F32) - total).astype(BF16)
        pair.append(products(dot, share, shifted, blocks, at, diag).astype(BF16))
    solved[...], solved_mate[...] = pair
    if last:
        sums = pushed_sums(level, at, share, blocks, targets, *pair)
    else:
        sums = gathered_sums(level + 1, at + 1, share, blocks, meets, *pair)
    pass_on(sums, to_hold, to_send)


def backward_kernel(
    level, at, share, blocks, targets, solved, solved_mate, held, came, result, *outs
):
    pair = []
    diags = OWN_DIAG, MATE_DIAG
    for total, vector, diag in zip(joined(held, came), (solved, solved_mate), diags):
        part = products(dot, share, total.astype(BF16), blocks, at, diag)
        pair.append((vector[...].astype(F32) - part).astype(BF16))
    result[...] = pair[0]
    pass_on(pushed_sums(level, at, share, blocks, targets, *pair), *outs)


def last_kernel(share, packed, blocks, held, came, *rest):
    *rest, out = rest
    solved, results = rest[: packed.shape[0]], rest[packed.shape[0] :]
    part = products(dot, share, joined(held, came)[0].astype(BF16), blocks, 0, OWN_DIAG)
    result = (solved[0][...].astype(F32) - part).astype(BF16)
    size = out.shape[1] // 2
    for level in range(packed.shape[0]):
        *owners, _ = unpack(packed, level)
        for which, array in enumerate((solved[level], results[level - 1] if level else result)):
            for half in range(2):
                out[owners[half], which * size : (which + 1) * size] = array[half * size : (half + 1) * size]


def call(kernel, outs, *args, fetched=0, scratch=()):
    specs = [pl.BlockSpec(memory_space=pltpu.VMEM)] * len(args)
    args = list(args)
    for at in range(1, 1 + fetched):
        specs[at] = pl.BlockSpec(memory_space=pltpu.HBM)
        args[at] = pltpu.with_memory_space_constraint(args[at], pltpu.HBM)
    return pl.pallas_call(
        kernel,
        out_shape=outs,
        in_specs=specs,
        out_specs=[pl.BlockSpec(memory_space=pltpu.VMEM)] * len(outs),
        scratch_shapes=scratch,
        compiler_params=pltpu.CompilerParams(vmem_limit_bytes=16 * 2**20),
    )(*args)


def local(right_side, diag_inverse, off_blocks, columns, plan):
    rows, depth, width = right_side.shape
    doms = lax.axis_size("dom")
    levs = lax.axis_size("level")
    levels = levs // 2
    share = depth // levs
    count = 2 * rows
    dom = lax.axis_index("dom")
    lev = lax.axis_index("level")
    near_pairs = [(i, i ^ 1) for i in range(doms)]
    far_pairs = [(i, ((i + 1) ^ 1) - 1) for i in range(1, doms - 1)] + [(0, doms - 1), (doms - 1, 0)]

    weights = jnp.concatenate([diag_inverse, off_blocks.reshape((-1,) + off_blocks.shape[2:])], axis=0)
    weights = lax.all_gather(weights, "level")

    turn = dom % 2
    ids = jnp.arange(levs, dtype=jnp.int32)
    own_level = jnp.sum(jnp.where(ids == lev, plan, 0)) // 2
    inverse = jnp.sum(jnp.where(plan[None, :] == ids[:, None], ids[None, :], 0), axis=1)
    side_of = jnp.where(jnp.arange(levels) % 2 == 1, 2 * turn, 2 - 2 * turn)
    packed = inverse[0::2] + (inverse[1::2] << BITS) + (side_of << (2 * BITS))
    packed = jnp.broadcast_to(packed[:, None], (levels, 128)).astype(jnp.int32)

    here = jnp.where(own_level % 2 == turn, off_blocks[:, 0], off_blocks[:, 2])
    mates = jnp.stack([diag_inverse, here], axis=1)
    by_near = lax.ppermute(mates, "dom", near_pairs)
    by_far = lax.ppermute(mates, "dom", far_pairs)
    mates = jnp.where(own_level % 2 == 1, by_near, by_far)
    first = jnp.einsum("rkb,rbc->rkc", right_side, diag_inverse, preferred_element_type=F32)
    side = jnp.where(own_level == 0, first.astype(BF16), right_side)
    side = side.reshape(rows, levs, share, width)
    side = lax.all_to_all(side, "level", 1, 0, tiled=False)
    side = side.reshape(levs, rows * share, width)[inverse].reshape(levels, count * share, width)

    near_dom = dom + 1 - 2 * turn
    far_dom = (dom - 1 + 2 * turn) % doms
    part = jnp.stack(
        [
            lax.dynamic_slice_in_dim(columns, which * levs * rows, levs * rows, 0)
            for which in (dom, near_dom, far_dom)
        ]
    )
    part = part.reshape(3, levs, rows * 3)[:, inverse].reshape(3, levels, count, 3)
    second = jnp.roll(inverse[1::2], 1)[None, :, None, None]
    met = jnp.where(part // rows % levs == second, rows, 0) + part % rows
    odd = (jnp.arange(levels) % 2 == 1)[:, None]
    meets_own = met[0]
    meets_mate = jnp.where(odd[..., None], met[1], met[2])
    ahead = odd == (turn == 0)
    own_mate = jnp.where(ahead, meets_own[..., 0], meets_own[..., 2])
    mate_own = jnp.where(ahead, meets_mate[..., 0], meets_mate[..., 2])
    k = jnp.arange(share, dtype=jnp.int32)
    span = count * share
    slot = jnp.where(turn == 0, 1, -1) * (jnp.arange(3, dtype=jnp.int32) - 1) + 1
    places = meets_own.transpose(0, 2, 1) * share + slot[None, :, None] * span
    places = (places[..., None] + k).reshape(levels, 3 * span, 1)
    targets = jnp.stack([meets_own[..., 1], mate_own, own_mate + count], axis=1) * share
    targets = (targets[..., None] + k).reshape(levels, 3 * span)
    targets, meets = targets[:, None, :], targets[:, :, None]

    vector = jax.ShapeDtypeStruct((count * share, width), BF16)
    sums = [jax.ShapeDtypeStruct((2 * span, width), kind) for kind in (F32, BF16)]
    paired = levels - 2

    own = side[0]
    far = lax.ppermute(jnp.stack([own, side[paired]]), "dom", far_pairs)
    near = lax.ppermute(jnp.stack([own, side[paired + 1]]), "dom", near_pairs)
    mates, packed, side, places, targets, meets, own, far, near = lax.optimization_barrier(
        (mates, packed, side, places, targets, meets, own, far, near)
    )
    side_mates = [far[1], near[1]]
    far, near = far[0], near[0]
    mates = lax.all_gather(mates, "level")

    def swap(vector, level):
        return lax.ppermute(vector, "dom", far_pairs if level % 2 == 0 else near_pairs)

    def arranged(kernel, levels_now, dims, copies, behind, *blocks):
        _, *blocks = lax.optimization_barrier((behind, *blocks))
        shape = (len(levels_now), *dims, width, width)
        kernel = functools.partial(kernel, levels_now)
        scratch = [pltpu.SemaphoreType.DMA((copies,))]
        outs = [jax.ShapeDtypeStruct(shape, BF16)]
        return call(kernel, outs, packed, *blocks, fetched=len(blocks), scratch=scratch)[0]

    solved = [own]
    solved_mate = []
    for level in range(1, paired):
        if level > 1:
            own = solved[-1]
            far, near = swap(own, 0), swap(own, 1)
        solved_mate.append(near if level % 2 == 0 else far)
        args = places, side, far, own, near
        if level == 1:
            scratch = [pltpu.VMEM((1, 2, 4 * rows, width, width), BF16), pltpu.SemaphoreType.DMA((2,))]
            kernel = functools.partial(forward_kernel, level, 0, share, True)
            solved += call(kernel, [vector], packed, weights, *args, fetched=1, scratch=scratch)
            singles = range(2, paired)
            blocks = arranged(arrange_kernel, singles, (2, 4 * rows), 2 * len(singles), solved[-1], weights)
        else:
            kernel = functools.partial(forward_kernel, level, level - 2, share, False)
            solved += call(kernel, [vector], packed, blocks, *args)

    solved_mate.append(swap(solved[-1], paired - 1))
    upper = range(paired, levels)
    blocks = arranged(arrange_pairs_kernel, upper, (count, 5), 8 * len(upper), solved[-1], weights, mates)
    kernel = functools.partial(entry_kernel, paired, 0, share)
    held, sent = call(kernel, sums, blocks, meets, solved[-1], solved_mate[-1])
    lower = range(paired)
    below = arranged(arrange_pairs_kernel, lower, (count, 5), 8 * len(lower) - 6, held, weights, mates)
    for level in upper:
        kernel = functools.partial(forward_pair_kernel, level, level - paired, share, level == levels - 1)
        args = blocks, meets, targets, side, side_mates[level - paired]
        own, mate, held, sent = call(kernel, [vector] * 2 + sums, *args, held, swap(sent, level))
        solved.append(own)
        solved_mate.append(mate)

    results = [own]
    for level in range(levels - 2, 0, -1):
        at = level - paired if level in upper else level
        kernel = functools.partial(backward_kernel, level, at, share)
        args = blocks if level in upper else below, targets, solved[level], solved_mate[level]
        result, held, sent = call(kernel, [vector] + sums, *args, held, swap(sent, level))
        results.append(result)

    dealt = jax.ShapeDtypeStruct((levs, 2 * rows * share, width), BF16)
    kernel = functools.partial(last_kernel, share)
    (dealt,) = call(kernel, [dealt], packed, below, held, swap(sent, 0), *solved, *results[::-1])
    dealt = lax.all_to_all(dealt, "level", 0, 0, tiled=False)
    dealt = dealt.reshape(levs, 2, rows, share, width).transpose(1, 2, 0, 3, 4)
    dealt = dealt.reshape(2, rows, depth, width)
    return dealt[0], dealt[1]


def solution(mesh):
    return jax.shard_map(
        local,
        mesh=mesh,
        in_specs=(
            P(("dom", "level"), None, None),
            P(("dom", "level"), None, None),
            P(("dom", "level"), None, None, None),
            P(),
            P(),
        ),
        out_specs=(P(("dom", "level"), None, None), P(("dom", "level"), None, None)),
        check_vma=False,
    )
```

```python
import functools

import jax
import jax.numpy as jnp
from jax import lax
from jax.experimental import pallas as pl
from jax.experimental.pallas import tpu as pltpu
from jax.sharding import PartitionSpec as P

BF16 = jnp.bfloat16
F32 = jnp.float32


def dot(a, b):
    return lax.dot_general(a, b, (((1,), (0,)), ((), ())), preferred_element_type=F32)


def either(low, high, share):
    top = lax.broadcasted_iota(jnp.int32, low.shape, 0) < share
    return jnp.where(top, low, high)


def ones_where(condition):
    return jnp.where(condition, 1.0, 0.0).astype(BF16)


BITS = 8


def unpack(packed, level):
    value = jnp.max(packed[level : level + 1])
    mask = (1 << BITS) - 1
    return value & mask, (value >> BITS) & mask, value >> (2 * BITS)


def products(share, vectors, blocks, level, kind):
    totals = []
    for row in range(0, blocks.shape[1], 2):
        part = vectors[share * row : share * (row + 2)]
        wide = [blocks[level, row + one, kind] for one in range(2)]
        if isinstance(kind, slice):
            wide = [block.reshape(-1, block.shape[-1]) for block in wide]
        totals.append(either(*[dot(part, block) for block in wide], share))
    return jnp.concatenate(totals, axis=0)


def run(copies, sems):
    copies = [pltpu.make_async_copy(*ends, sems.at[which]) for which, ends in enumerate(copies)]
    for copy in copies:
        copy.start()
    return lambda: [copy.wait() for copy in copies]


OWN_DIAG, OWN_OWN, OWN_MATE, MATE_DIAG, MATE_OWN = range(5)


def level_copies(levels, packed, weights, out):
    rows = weights.shape[1]
    copies = []
    for at, level in enumerate(levels):
        *owners, _ = unpack(packed, level)
        for half in range(2):
            copies.append((weights.at[owners[half]], out.at[at, pl.ds(half * rows, rows)]))
    return copies


def arrange_kernel(levels, packed, weights, out, sems):
    run(level_copies(levels, packed, weights, out), sems)()


def arrange_pairs_kernel(levels, packed, weights, mates, out, sems):
    rows = weights.shape[1]
    copies = []
    for at, level in enumerate(levels):
        *owners, side = unpack(packed, level)
        for half in range(2):
            here = pl.ds(half * rows, rows)
            kinds = [(OWN_DIAG, 0), (OWN_OWN, 2), (OWN_MATE, 1 + side)] if level else [(OWN_DIAG, 0)]
            for kind, block in kinds:
                source = weights.at[owners[half], :, pl.ds(block, 1)]
                copies.append((source, out.at[at, here, pl.ds(kind, 1)]))
            if level:
                copies.append((mates.at[owners[half]], out.at[at, here, pl.ds(MATE_DIAG, 2)]))
    run(copies, sems)()


def picked_from(places, around):
    at = lax.broadcasted_iota(jnp.int32, (places.shape[0], around.shape[0]), 1)
    return dot(ones_where(at == places), around)


def forward_kernel(level, at, share, fetched, packed, weights, places, side, far, own, near, out, *held):
    if fetched:
        held, sems = held
        wait = run(level_copies([level], packed, weights, held), sems)
        weights = held
    span = out.shape[0]
    picked = picked_from(places[level], jnp.concatenate([far[...], own[...], near[...]], axis=0))
    picked = jnp.concatenate([picked[n * span : (n + 1) * span] for n in range(3)], axis=1)
    if fetched:
        wait()
    total = products(share, picked.astype(BF16), weights, at, slice(1, None))
    shifted = (side[level].astype(F32) - total).astype(BF16)
    out[...] = products(share, shifted, weights, at, 0).astype(BF16)


def gathered_sums(level, at, share, blocks, places, own, mate):
    span = own.shape[0]
    picked = picked_from(places[level], jnp.concatenate([own, mate], axis=0)).astype(BF16)
    parts = [
        products(share, picked[n * span : (n + 1) * span], blocks, at, kind)
        for n, kind in enumerate((OWN_OWN, MATE_OWN, OWN_MATE))
    ]
    return jnp.concatenate([parts[0] + parts[2], parts[1]], axis=0)


PUSHED = OWN_OWN, MATE_OWN, OWN_MATE


def turn_kernel(at, blocks, out):
    for row in range(out.shape[1]):
        for which, kind in enumerate(PUSHED):
            out[0, row, which] = blocks[at, row, kind].T


def pushed_sums(level, share, turned, targets, own, mate):
    span = own.shape[0]
    pushed = [
        products(share, vectors, turned, 0, which)
        for which, vectors in enumerate((own, mate, own))
    ]
    pushed = jnp.concatenate(pushed, axis=0).astype(BF16)
    to = lax.broadcasted_iota(jnp.int32, (2 * span, 3 * span), 0)
    return dot(ones_where(to == targets[level]), pushed)


def pass_on(sums, held, sent):
    held[...] = sums
    sent[...] = sums.astype(BF16)


def joined(held, came):
    span = held.shape[0] // 2
    came = came[...].astype(F32)
    return held[:span] + came[span:], held[span:] + came[:span]


def entry_kernel(level, at, share, blocks, meets, own, mate, held, sent):
    pass_on(gathered_sums(level, at, share, blocks, meets, own[...], mate[...]), held, sent)


def forward_pair_kernel(
    level, at, share, last, blocks, turned, meets, targets, side, side_mate, held, came,
    solved, solved_mate, to_hold, to_send,
):
    pair = []
    diags = OWN_DIAG, MATE_DIAG
    for total, right, diag in zip(joined(held, came), (side[level], side_mate[...]), diags):
        shifted = (right.astype(F32) - total).astype(BF16)
        pair.append(products(share, shifted, blocks, at, diag).astype(BF16))
    solved[...], solved_mate[...] = pair
    if last:
        sums = pushed_sums(level, share, turned, targets, *pair)
    else:
        sums = gathered_sums(level + 1, at + 1, share, blocks, meets, *pair)
    pass_on(sums, to_hold, to_send)


def backward_kernel(
    level, at, share, blocks, turned, targets, solved, solved_mate, held, came, result, *outs
):
    pair = []
    diags = OWN_DIAG, MATE_DIAG
    for total, vector, diag in zip(joined(held, came), (solved, solved_mate), diags):
        part = products(share, total.astype(BF16), blocks, at, diag)
        pair.append((vector[...].astype(F32) - part).astype(BF16))
    result[...] = pair[0]
    pass_on(pushed_sums(level, share, turned, targets, *pair), *outs)


def last_kernel(share, packed, blocks, held, came, *rest):
    *rest, out = rest
    solved, results = rest[: packed.shape[0]], rest[packed.shape[0] :]
    part = products(share, joined(held, came)[0].astype(BF16), blocks, 0, OWN_DIAG)
    result = (solved[0][...].astype(F32) - part).astype(BF16)
    size = out.shape[1] // 2
    for level in range(packed.shape[0]):
        *owners, _ = unpack(packed, level)
        for which, array in enumerate((solved[level], results[level - 1] if level else result)):
            for half in range(2):
                out[owners[half], which * size : (which + 1) * size] = array[half * size : (half + 1) * size]


def call(kernel, outs, *args, fetched=0, scratch=()):
    specs = [pl.BlockSpec(memory_space=pltpu.VMEM)] * len(args)
    args = list(args)
    for at in range(1, 1 + fetched):
        specs[at] = pl.BlockSpec(memory_space=pltpu.HBM)
        args[at] = pltpu.with_memory_space_constraint(args[at], pltpu.HBM)
    return pl.pallas_call(
        kernel,
        out_shape=outs,
        in_specs=specs,
        out_specs=[pl.BlockSpec(memory_space=pltpu.VMEM)] * len(outs),
        scratch_shapes=scratch,
        compiler_params=pltpu.CompilerParams(vmem_limit_bytes=16 * 2**20),
    )(*args)


def local(right_side, diag_inverse, off_blocks, columns, plan):
    rows, depth, width = right_side.shape
    doms = lax.axis_size("dom")
    levs = lax.axis_size("level")
    levels = levs // 2
    share = depth // levs
    count = 2 * rows
    dom = lax.axis_index("dom")
    lev = lax.axis_index("level")
    near_pairs = [(i, i ^ 1) for i in range(doms)]
    far_pairs = [(i, ((i + 1) ^ 1) - 1) for i in range(1, doms - 1)] + [(0, doms - 1), (doms - 1, 0)]

    weights = jnp.concatenate([diag_inverse[:, None], off_blocks], axis=1)
    weights = lax.all_gather(weights, "level")

    turn = dom % 2
    ids = jnp.arange(levs, dtype=jnp.int32)
    own_level = jnp.sum(jnp.where(ids == lev, plan, 0)) // 2
    inverse = jnp.sum(jnp.where(plan[None, :] == ids[:, None], ids[None, :], 0), axis=1)
    side_of = jnp.where(jnp.arange(levels) % 2 == 1, 2 * turn, 2 - 2 * turn)
    packed = inverse[0::2] + (inverse[1::2] << BITS) + (side_of << (2 * BITS))
    packed = jnp.broadcast_to(packed[:, None], (levels, 128)).astype(jnp.int32)

    here = jnp.where(own_level % 2 == turn, off_blocks[:, 0], off_blocks[:, 2])
    mates = jnp.stack([diag_inverse, here], axis=1)
    by_near = lax.ppermute(mates, "dom", near_pairs)
    by_far = lax.ppermute(mates, "dom", far_pairs)
    mates = jnp.where(own_level % 2 == 1, by_near, by_far)
    first = jnp.einsum("rkb,rbc->rkc", right_side, diag_inverse, preferred_element_type=F32)
    side = jnp.where(own_level == 0, first.astype(BF16), right_side)
    side = side.reshape(rows, levs, share, width)
    side = lax.all_to_all(side, "level", 1, 0, tiled=False)
    side = side.reshape(levs, rows * share, width)[inverse].reshape(levels, count * share, width)

    near_dom = dom + 1 - 2 * turn
    far_dom = (dom - 1 + 2 * turn) % doms
    part = jnp.stack(
        [
            lax.dynamic_slice_in_dim(columns, which * levs * rows, levs * rows, 0)
            for which in (dom, near_dom, far_dom)
        ]
    )
    part = part.reshape(3, levs, rows * 3)[:, inverse].reshape(3, levels, count, 3)
    second = jnp.roll(inverse[1::2], 1)[None, :, None, None]
    met = jnp.where(part // rows % levs == second, rows, 0) + part % rows
    odd = (jnp.arange(levels) % 2 == 1)[:, None]
    meets_own = met[0]
    meets_mate = jnp.where(odd[..., None], met[1], met[2])
    ahead = odd == (turn == 0)
    own_mate = jnp.where(ahead, meets_own[..., 0], meets_own[..., 2])
    mate_own = jnp.where(ahead, meets_mate[..., 0], meets_mate[..., 2])
    k = jnp.arange(share, dtype=jnp.int32)
    span = count * share
    slot = jnp.where(turn == 0, 1, -1) * (jnp.arange(3, dtype=jnp.int32) - 1) + 1
    places = meets_own.transpose(0, 2, 1) * share + slot[None, :, None] * span
    places = (places[..., None] + k).reshape(levels, 3 * span, 1)
    targets = jnp.stack([meets_own[..., 1], mate_own, own_mate + count], axis=1) * share
    targets = (targets[..., None] + k).reshape(levels, 3 * span)
    targets, meets = targets[:, None, :], targets[:, :, None]

    vector = jax.ShapeDtypeStruct((count * share, width), BF16)
    sums = [jax.ShapeDtypeStruct((2 * span, width), kind) for kind in (F32, BF16)]
    paired = levels - 2

    own = side[0]
    far = lax.ppermute(jnp.stack([own, side[paired]]), "dom", far_pairs)
    near = lax.ppermute(jnp.stack([own, side[paired + 1]]), "dom", near_pairs)
    mates, packed, side, places, targets, meets, own, far, near = lax.optimization_barrier(
        (mates, packed, side, places, targets, meets, own, far, near)
    )
    side_mates = [far[1], near[1]]
    far, near = far[0], near[0]
    mates = lax.all_gather(mates, "level")

    def swap(vector, level):
        return lax.ppermute(vector, "dom", far_pairs if level % 2 == 0 else near_pairs)

    def arranged(kernel, levels_now, kinds, copies, behind, *blocks):
        _, *blocks = lax.optimization_barrier((behind, *blocks))
        shape = (len(levels_now), count, kinds, width, width)
        kernel = functools.partial(kernel, levels_now)
        scratch = [pltpu.SemaphoreType.DMA((copies,))]
        outs = [jax.ShapeDtypeStruct(shape, BF16)]
        return call(kernel, outs, packed, *blocks, fetched=len(blocks), scratch=scratch)[0]

    solved = [own]
    solved_mate = []
    for level in range(1, paired):
        if level > 1:
            own = solved[-1]
            far, near = swap(own, 0), swap(own, 1)
        solved_mate.append(near if level % 2 == 0 else far)
        args = places, side, far, own, near
        if level == 1:
            scratch = [pltpu.VMEM((1, count, 4, width, width), BF16), pltpu.SemaphoreType.DMA((2,))]
            kernel = functools.partial(forward_kernel, level, 0, share, True)
            solved += call(kernel, [vector], packed, weights, *args, fetched=1, scratch=scratch)
            singles = range(2, paired)
            blocks = arranged(arrange_kernel, singles, 4, 2 * len(singles), solved[-1], weights)
        else:
            kernel = functools.partial(forward_kernel, level, level - 2, share, False)
            solved += call(kernel, [vector], packed, blocks, *args)

    solved_mate.append(swap(solved[-1], paired - 1))
    upper = range(paired, levels)
    blocks = arranged(arrange_pairs_kernel, upper, 5, 8 * len(upper), solved[-1], weights, mates)
    kernel = functools.partial(entry_kernel, paired, 0, share)
    held, sent = call(kernel, sums, blocks, meets, solved[-1], solved_mate[-1])
    lower = range(paired)
    below = arranged(arrange_pairs_kernel, lower, 5, 8 * len(lower) - 6, held, weights, mates)
    blocks, below = lax.optimization_barrier((blocks, below))

    def turned(blocks, at, behind):
        _, blocks = lax.optimization_barrier((behind, blocks))
        outs = [jax.ShapeDtypeStruct((1, count, len(PUSHED), width, width), BF16)]
        return call(functools.partial(turn_kernel, at), outs, blocks)[0]

    for level in upper:
        kernel = functools.partial(forward_pair_kernel, level, level - paired, share, level == levels - 1)
        last = level == levels - 1
        ready = turned(blocks, level - paired, sent) if last else targets
        args = blocks, ready, meets, targets, side, side_mates[level - paired]
        own, mate, held, sent = call(kernel, [vector] * 2 + sums, *args, held, swap(sent, level))
        solved.append(own)
        solved_mate.append(mate)

    results = [own]
    for level in range(levels - 2, 0, -1):
        at = level - paired if level in upper else level
        kernel = functools.partial(backward_kernel, level, at, share)
        here = blocks if level in upper else below
        args = here, turned(here, at, sent), targets, solved[level], solved_mate[level]
        result, held, sent = call(kernel, [vector] + sums, *args, held, swap(sent, level))
        results.append(result)

    dealt = jax.ShapeDtypeStruct((levs, 2 * rows * share, width), BF16)
    kernel = functools.partial(last_kernel, share)
    (dealt,) = call(kernel, [dealt], packed, below, held, swap(sent, 0), *solved, *results[::-1])
    dealt = lax.all_to_all(dealt, "level", 0, 0, tiled=False)
    dealt = dealt.reshape(levs, 2, rows, share, width).transpose(1, 2, 0, 3, 4)
    dealt = dealt.reshape(2, rows, depth, width)
    return dealt[0], dealt[1]


def solution(mesh):
    return jax.shard_map(
        local,
        mesh=mesh,
        in_specs=(
            P(("dom", "level"), None, None),
            P(("dom", "level"), None, None),
            P(("dom", "level"), None, None, None),
            P(),
            P(),
        ),
        out_specs=(P(("dom", "level"), None, None), P(("dom", "level"), None, None)),
        check_vma=False,
    )
```

```python
import functools

import jax
import jax.numpy as jnp
from jax import lax
from jax.experimental import pallas as pl
from jax.experimental.pallas import tpu as pltpu
from jax.sharding import PartitionSpec as P

BF16 = jnp.bfloat16
F32 = jnp.float32


def dot(a, b):
    return lax.dot_general(a, b, (((1,), (0,)), ((), ())), preferred_element_type=F32)


def either(low, high, share):
    top = lax.broadcasted_iota(jnp.int32, low.shape, 0) < share
    return jnp.where(top, low, high)


def ones_where(condition):
    return jnp.where(condition, 1.0, 0.0).astype(BF16)


BITS = 8


def unpack(packed, level):
    value = jnp.max(packed[level : level + 1])
    mask = (1 << BITS) - 1
    return value & mask, (value >> BITS) & mask, value >> (2 * BITS)


def products(share, vectors, blocks, level, kind):
    totals = []
    for row in range(0, blocks.shape[1], 2):
        part = vectors[share * row : share * (row + 2)]
        wide = [blocks[level, row + one, kind] for one in range(2)]
        if isinstance(kind, slice):
            wide = [block.reshape(-1, block.shape[-1]) for block in wide]
        totals.append(either(*[dot(part, block) for block in wide], share))
    return jnp.concatenate(totals, axis=0)


def run(copies, sems):
    copies = [pltpu.make_async_copy(*ends, sems.at[which]) for which, ends in enumerate(copies)]
    for copy in copies:
        copy.start()
    return lambda: [copy.wait() for copy in copies]


OWN_DIAG, OWN_OWN, OWN_MATE, MATE_DIAG, MATE_OWN = range(5)


def level_copies(levels, packed, weights, out):
    rows = weights.shape[1]
    copies = []
    for at, level in enumerate(levels):
        *owners, _ = unpack(packed, level)
        for half in range(2):
            copies.append((weights.at[owners[half]], out.at[at, pl.ds(half * rows, rows)]))
    return copies


def arrange_kernel(levels, packed, weights, out, sems):
    run(level_copies(levels, packed, weights, out), sems)()


def arrange_pairs_kernel(levels, packed, weights, mates, out, sems):
    rows = weights.shape[1]
    copies = []
    for at, level in enumerate(levels):
        *owners, side = unpack(packed, level)
        for half in range(2):
            here = pl.ds(half * rows, rows)
            kinds = [(OWN_DIAG, 0), (OWN_OWN, 2), (OWN_MATE, 1 + side)] if level else [(OWN_DIAG, 0)]
            for kind, block in kinds:
                source = weights.at[owners[half], :, pl.ds(block, 1)]
                copies.append((source, out.at[at, here, pl.ds(kind, 1)]))
            if level:
                copies.append((mates.at[owners[half]], out.at[at, here, pl.ds(MATE_DIAG, 2)]))
    run(copies, sems)()


def picked_from(places, around):
    at = lax.broadcasted_iota(jnp.int32, (places.shape[0], around.shape[0]), 1)
    return dot(ones_where(at == places), around)


def forward_kernel(level, at, share, fetched, packed, weights, places, side, far, own, near, out, *held):
    if fetched:
        held, sems = held
        wait = run(level_copies([level], packed, weights, held), sems)
        weights = held
    span = out.shape[0]
    picked = picked_from(places[level], jnp.concatenate([far[...], own[...], near[...]], axis=0))
    picked = jnp.concatenate([picked[n * span : (n + 1) * span] for n in range(3)], axis=1)
    if fetched:
        wait()
    total = products(share, picked.astype(BF16), weights, at, slice(1, None))
    shifted = (side[level].astype(F32) - total).astype(BF16)
    out[...] = products(share, shifted, weights, at, 0).astype(BF16)


def gathered_sums(level, at, share, blocks, places, own, mate):
    span = own.shape[0]
    picked = picked_from(places[level], jnp.concatenate([own, mate], axis=0)).astype(BF16)
    parts = [
        products(share, picked[n * span : (n + 1) * span], blocks, at, kind)
        for n, kind in enumerate((OWN_OWN, MATE_OWN, OWN_MATE))
    ]
    return jnp.concatenate([parts[0] + parts[2], parts[1]], axis=0)


PUSHED = OWN_OWN, MATE_OWN, OWN_MATE


def turn_kernel(at, blocks, out):
    for row in range(out.shape[1]):
        for which, kind in enumerate(PUSHED):
            out[0, row, which] = blocks[at, row, kind].T


def pushed_sums(level, share, turned, targets, own, mate):
    span = own.shape[0]
    pushed = [
        products(share, vectors, turned, 0, which)
        for which, vectors in enumerate((own, mate, own))
    ]
    pushed = jnp.concatenate(pushed, axis=0).astype(BF16)
    to = lax.broadcasted_iota(jnp.int32, (2 * span, 3 * span), 0)
    return dot(ones_where(to == targets[level]), pushed)


def pass_on(sums, held, sent):
    held[...] = sums
    sent[...] = sums.astype(BF16)


def joined(held, came):
    span = held.shape[0] // 2
    came = came[...].astype(F32)
    return held[:span] + came[span:], held[span:] + came[:span]


def entry_kernel(level, at, share, blocks, meets, own, mate, held, sent):
    pass_on(gathered_sums(level, at, share, blocks, meets, own[...], mate[...]), held, sent)


def forward_pair_kernel(
    level, at, share, last, blocks, turned, meets, targets, side, side_mate, held, came,
    solved, solved_mate, to_hold, to_send,
):
    pair = []
    diags = OWN_DIAG, MATE_DIAG
    for total, right, diag in zip(joined(held, came), (side[level], side_mate[...]), diags):
        shifted = (right.astype(F32) - total).astype(BF16)
        pair.append(products(share, shifted, blocks, at, diag).astype(BF16))
    solved[...], solved_mate[...] = pair
    if last:
        sums = pushed_sums(level, share, turned, targets, *pair)
    else:
        sums = gathered_sums(level + 1, at + 1, share, blocks, meets, *pair)
    pass_on(sums, to_hold, to_send)


def backward_kernel(
    level, at, share, blocks, turned, targets, solved, solved_mate, held, came, result, *outs
):
    pair = []
    diags = OWN_DIAG, MATE_DIAG
    for total, vector, diag in zip(joined(held, came), (solved, solved_mate), diags):
        part = products(share, total.astype(BF16), blocks, at, diag)
        pair.append((vector[...].astype(F32) - part).astype(BF16))
    result[...] = pair[0]
    pass_on(pushed_sums(level, share, turned, targets, *pair), *outs)


def last_kernel(share, packed, blocks, held, came, *rest):
    *rest, out = rest
    solved, results = rest[: packed.shape[0]], rest[packed.shape[0] :]
    part = products(share, joined(held, came)[0].astype(BF16), blocks, 0, OWN_DIAG)
    result = (solved[0][...].astype(F32) - part).astype(BF16)
    size = out.shape[1] // 2
    for level in range(packed.shape[0]):
        *owners, _ = unpack(packed, level)
        for which, array in enumerate((solved[level], results[level - 1] if level else result)):
            for half in range(2):
                out[owners[half], which * size : (which + 1) * size] = array[half * size : (half + 1) * size]


def call(kernel, outs, *args, fetched=0, scratch=()):
    specs = [pl.BlockSpec(memory_space=pltpu.VMEM)] * len(args)
    args = list(args)
    for at in range(1, 1 + fetched):
        specs[at] = pl.BlockSpec(memory_space=pltpu.HBM)
        args[at] = pltpu.with_memory_space_constraint(args[at], pltpu.HBM)
    return pl.pallas_call(
        kernel,
        out_shape=outs,
        in_specs=specs,
        out_specs=[pl.BlockSpec(memory_space=pltpu.VMEM)] * len(outs),
        scratch_shapes=scratch,
        compiler_params=pltpu.CompilerParams(vmem_limit_bytes=16 * 2**20),
    )(*args)


def local(right_side, diag_inverse, off_blocks, columns, plan):
    rows, depth, width = right_side.shape
    doms = lax.axis_size("dom")
    levs = lax.axis_size("level")
    levels = levs // 2
    share = depth // levs
    count = 2 * rows
    dom = lax.axis_index("dom")
    lev = lax.axis_index("level")
    near_pairs = [(i, i ^ 1) for i in range(doms)]
    far_pairs = [(i, ((i + 1) ^ 1) - 1) for i in range(1, doms - 1)] + [(0, doms - 1), (doms - 1, 0)]

    weights = jnp.concatenate([diag_inverse[:, None], off_blocks], axis=1)
    weights = lax.all_gather(weights, "level")

    turn = dom % 2
    ids = jnp.arange(levs, dtype=jnp.int32)
    own_level = jnp.sum(jnp.where(ids == lev, plan, 0)) // 2
    inverse = jnp.sum(jnp.where(plan[None, :] == ids[:, None], ids[None, :], 0), axis=1)
    side_of = jnp.where(jnp.arange(levels) % 2 == 1, 2 * turn, 2 - 2 * turn)
    packed = inverse[0::2] + (inverse[1::2] << BITS) + (side_of << (2 * BITS))
    packed = jnp.broadcast_to(packed[:, None], (levels, 128)).astype(jnp.int32)

    here = jnp.where(own_level % 2 == turn, off_blocks[:, 0], off_blocks[:, 2])
    mates = jnp.stack([diag_inverse, here], axis=1)
    by_near = lax.ppermute(mates, "dom", near_pairs)
    by_far = lax.ppermute(mates, "dom", far_pairs)
    mates = jnp.where(own_level % 2 == 1, by_near, by_far)
    first = jnp.einsum("rkb,rbc->rkc", right_side, diag_inverse, preferred_element_type=F32)
    side = jnp.where(own_level == 0, first.astype(BF16), right_side)
    side = side.reshape(rows, levs, share, width)
    side = lax.all_to_all(side, "level", 1, 0, tiled=False)
    side = side.reshape(levs, rows * share, width)[inverse].reshape(levels, count * share, width)

    near_dom = dom + 1 - 2 * turn
    far_dom = (dom - 1 + 2 * turn) % doms
    part = jnp.stack(
        [
            lax.dynamic_slice_in_dim(columns, which * levs * rows, levs * rows, 0)
            for which in (dom, near_dom, far_dom)
        ]
    )
    part = part.reshape(3, levs, rows * 3)[:, inverse].reshape(3, levels, count, 3)
    second = jnp.roll(inverse[1::2], 1)[None, :, None, None]
    met = jnp.where(part // rows % levs == second, rows, 0) + part % rows
    odd = (jnp.arange(levels) % 2 == 1)[:, None]
    meets_own = met[0]
    meets_mate = jnp.where(odd[..., None], met[1], met[2])
    ahead = odd == (turn == 0)
    own_mate = jnp.where(ahead, meets_own[..., 0], meets_own[..., 2])
    mate_own = jnp.where(ahead, meets_mate[..., 0], meets_mate[..., 2])
    k = jnp.arange(share, dtype=jnp.int32)
    span = count * share
    slot = jnp.where(turn == 0, 1, -1) * (jnp.arange(3, dtype=jnp.int32) - 1) + 1
    places = meets_own.transpose(0, 2, 1) * share + slot[None, :, None] * span
    places = (places[..., None] + k).reshape(levels, 3 * span, 1)
    targets = jnp.stack([meets_own[..., 1], mate_own, own_mate + count], axis=1) * share
    targets = (targets[..., None] + k).reshape(levels, 3 * span)
    targets, meets = targets[:, None, :], targets[:, :, None]

    vector = jax.ShapeDtypeStruct((count * share, width), BF16)
    sums = [jax.ShapeDtypeStruct((2 * span, width), kind) for kind in (F32, BF16)]
    paired = levels - 2

    own = side[0]
    far = lax.ppermute(jnp.stack([own, side[paired]]), "dom", far_pairs)
    near = lax.ppermute(jnp.stack([own, side[paired + 1]]), "dom", near_pairs)
    mates, packed, side, places, targets, meets, own, far, near = lax.optimization_barrier(
        (mates, packed, side, places, targets, meets, own, far, near)
    )
    side_mates = [far[1], near[1]]
    far, near = far[0], near[0]
    mates = lax.all_gather(mates, "level")

    def swap(vector, level):
        return lax.ppermute(vector, "dom", far_pairs if level % 2 == 0 else near_pairs)

    def arranged(kernel, levels_now, kinds, copies, behind, *blocks):
        _, *blocks = lax.optimization_barrier((behind, *blocks))
        shape = (len(levels_now), count, kinds, width, width)
        kernel = functools.partial(kernel, levels_now)
        scratch = [pltpu.SemaphoreType.DMA((copies,))]
        outs = [jax.ShapeDtypeStruct(shape, BF16)]
        return call(kernel, outs, packed, *blocks, fetched=len(blocks), scratch=scratch)[0]

    solved = [own]
    solved_mate = []
    for level in range(1, paired):
        if level > 1:
            own = solved[-1]
            far, near = swap(own, 0), swap(own, 1)
        solved_mate.append(near if level % 2 == 0 else far)
        args = places, side, far, own, near
        if level == 1:
            scratch = [pltpu.VMEM((1, count, 4, width, width), BF16), pltpu.SemaphoreType.DMA((2,))]
            kernel = functools.partial(forward_kernel, level, 0, share, True)
            solved += call(kernel, [vector], packed, weights, *args, fetched=1, scratch=scratch)
            singles = range(2, paired)
            blocks = arranged(arrange_kernel, singles, 4, 2 * len(singles), solved[-1], weights)
        else:
            kernel = functools.partial(forward_kernel, level, level - 2, share, False)
            solved += call(kernel, [vector], packed, blocks, *args)

    solved_mate.append(swap(solved[-1], paired - 1))
    upper = range(paired, levels)
    blocks = arranged(arrange_pairs_kernel, upper, 5, 8 * len(upper), solved[-1], weights, mates)
    kernel = functools.partial(entry_kernel, paired, 0, share)
    held, sent = call(kernel, sums, blocks, meets, solved[-1], solved_mate[-1])
    lower = range(paired)
    below = arranged(arrange_pairs_kernel, lower, 5, 8 * len(lower) - 6, held, weights, mates)

    def turned(blocks, at, behind):
        _, blocks = lax.optimization_barrier((behind, blocks))
        outs = [jax.ShapeDtypeStruct((1, count, len(PUSHED), width, width), BF16)]
        return call(functools.partial(turn_kernel, at), outs, blocks)[0]

    for level in upper:
        kernel = functools.partial(forward_pair_kernel, level, level - paired, share, level == levels - 1)
        last = level == levels - 1
        ready = turned(blocks, level - paired, sent) if last else targets
        args = blocks, ready, meets, targets, side, side_mates[level - paired]
        own, mate, held, sent = call(kernel, [vector] * 2 + sums, *args, held, swap(sent, level))
        solved.append(own)
        solved_mate.append(mate)

    results = [own]
    for level in range(levels - 2, 0, -1):
        at = level - paired if level in upper else level
        kernel = functools.partial(backward_kernel, level, at, share)
        here = blocks if level in upper else below
        args = here, turned(here, at, sent), targets, solved[level], solved_mate[level]
        result, held, sent = call(kernel, [vector] + sums, *args, held, swap(sent, level))
        results.append(result)

    dealt = jax.ShapeDtypeStruct((levs, 2 * rows * share, width), BF16)
    kernel = functools.partial(last_kernel, share)
    (dealt,) = call(kernel, [dealt], packed, below, held, swap(sent, 0), *solved, *results[::-1])
    dealt = lax.all_to_all(dealt, "level", 0, 0, tiled=False)
    dealt = dealt.reshape(levs, 2, rows, share, width).transpose(1, 2, 0, 3, 4)
    dealt = dealt.reshape(2, rows, depth, width)
    return dealt[0], dealt[1]


def solution(mesh):
    return jax.shard_map(
        local,
        mesh=mesh,
        in_specs=(
            P(("dom", "level"), None, None),
            P(("dom", "level"), None, None),
            P(("dom", "level"), None, None, None),
            P(),
            P(),
        ),
        out_specs=(P(("dom", "level"), None, None), P(("dom", "level"), None, None)),
        check_vma=False,
    )
```

```python
import functools

import jax
import jax.numpy as jnp
from jax import lax
from jax.experimental import pallas as pl
from jax.experimental.pallas import tpu as pltpu
from jax.sharding import PartitionSpec as P

BF16 = jnp.bfloat16
F32 = jnp.float32


def dot(a, b):
    return lax.dot_general(a, b, (((1,), (0,)), ((), ())), preferred_element_type=F32)


def either(low, high, share):
    top = lax.broadcasted_iota(jnp.int32, low.shape, 0) < share
    return jnp.where(top, low, high)


def ones_where(condition):
    return jnp.where(condition, 1.0, 0.0).astype(BF16)


BITS = 8


def unpack(packed, level):
    value = jnp.max(packed[level : level + 1])
    mask = (1 << BITS) - 1
    return value & mask, (value >> BITS) & mask, value >> (2 * BITS)


def products(share, vectors, blocks, level, kind):
    totals = []
    for row in range(0, blocks.shape[1], 2):
        part = vectors[share * row : share * (row + 2)]
        wide = [blocks[level, row + one, kind] for one in range(2)]
        if isinstance(kind, slice):
            wide = [block.reshape(-1, block.shape[-1]) for block in wide]
        totals.append(either(*[dot(part, block) for block in wide], share))
    return jnp.concatenate(totals, axis=0)


def run(copies, sems):
    copies = [pltpu.make_async_copy(*ends, sems.at[which]) for which, ends in enumerate(copies)]
    for copy in copies:
        copy.start()
    return lambda: [copy.wait() for copy in copies]


OWN_DIAG, OWN_OWN, OWN_MATE, MATE_DIAG, MATE_OWN = range(5)


def level_copies(levels, packed, weights, out):
    rows = weights.shape[1]
    copies = []
    for at, level in enumerate(levels):
        *owners, _ = unpack(packed, level)
        for half in range(2):
            for row in range(0, rows, 2):
                source = weights.at[owners[half], pl.ds(row, 2)]
                copies.append((source, out.at[at, pl.ds(half * rows + row, 2)]))
    return copies


def arrange_kernel(levels, packed, weights, out, sems):
    run(level_copies(levels, packed, weights, out), sems)()


def arrange_pairs_kernel(levels, packed, weights, mates, out, sems):
    rows = weights.shape[1]
    copies = []
    for at, level in enumerate(levels):
        *owners, side = unpack(packed, level)
        for half in range(2):
            here = pl.ds(half * rows, rows)
            kinds = [(OWN_DIAG, 0), (OWN_OWN, 2), (OWN_MATE, 1 + side)] if level else [(OWN_DIAG, 0)]
            for kind, block in kinds:
                source = weights.at[owners[half], :, pl.ds(block, 1)]
                copies.append((source, out.at[at, here, pl.ds(kind, 1)]))
            if level:
                copies.append((mates.at[owners[half]], out.at[at, here, pl.ds(MATE_DIAG, 2)]))
    run(copies, sems)()


def picked_from(places, around):
    at = lax.broadcasted_iota(jnp.int32, (places.shape[0], around.shape[0]), 1)
    return dot(ones_where(at == places), around)


def forward_kernel(level, at, share, fetched, packed, weights, places, side, far, own, near, out, *held):
    if fetched:
        held, sems = held
        wait = run(level_copies([level], packed, weights, held), sems)
        weights = held
    span = out.shape[0]
    picked = picked_from(places[level], jnp.concatenate([far[...], own[...], near[...]], axis=0))
    picked = jnp.concatenate([picked[n * span : (n + 1) * span] for n in range(3)], axis=1)
    if fetched:
        wait()
    total = products(share, picked.astype(BF16), weights, at, slice(1, None))
    shifted = (side[level].astype(F32) - total).astype(BF16)
    out[...] = products(share, shifted, weights, at, 0).astype(BF16)


def gathered_sums(level, at, share, blocks, places, own, mate):
    span = own.shape[0]
    picked = picked_from(places[level], jnp.concatenate([own, mate], axis=0)).astype(BF16)
    parts = [
        products(share, picked[n * span : (n + 1) * span], blocks, at, kind)
        for n, kind in enumerate((OWN_OWN, MATE_OWN, OWN_MATE))
    ]
    return jnp.concatenate([parts[0] + parts[2], parts[1]], axis=0)


PUSHED = OWN_OWN, MATE_OWN, OWN_MATE


def turn_kernel(at, blocks, out):
    for row in range(out.shape[1]):
        for which, kind in enumerate(PUSHED):
            out[0, row, which] = blocks[at, row, kind].T


def pushed_sums(level, share, turned, targets, own, mate):
    span = own.shape[0]
    pushed = [
        products(share, vectors, turned, 0, which)
        for which, vectors in enumerate((own, mate, own))
    ]
    pushed = jnp.concatenate(pushed, axis=0).astype(BF16)
    to = lax.broadcasted_iota(jnp.int32, (2 * span, 3 * span), 0)
    return dot(ones_where(to == targets[level]), pushed)


def pass_on(sums, held, sent):
    held[...] = sums
    sent[...] = sums.astype(BF16)


def joined(held, came):
    span = held.shape[0] // 2
    came = came[...].astype(F32)
    return held[:span] + came[span:], held[span:] + came[:span]


def entry_kernel(level, at, share, blocks, meets, own, mate, held, sent):
    pass_on(gathered_sums(level, at, share, blocks, meets, own[...], mate[...]), held, sent)


def forward_pair_kernel(
    level, at, share, last, blocks, turned, meets, targets, side, side_mate, held, came,
    solved, solved_mate, to_hold, to_send,
):
    pair = []
    diags = OWN_DIAG, MATE_DIAG
    for total, right, diag in zip(joined(held, came), (side[level], side_mate[...]), diags):
        shifted = (right.astype(F32) - total).astype(BF16)
        pair.append(products(share, shifted, blocks, at, diag).astype(BF16))
    solved[...], solved_mate[...] = pair
    if last:
        sums = pushed_sums(level, share, turned, targets, *pair)
    else:
        sums = gathered_sums(level + 1, at + 1, share, blocks, meets, *pair)
    pass_on(sums, to_hold, to_send)


def backward_kernel(
    level, at, share, blocks, turned, targets, solved, solved_mate, held, came, result, *outs
):
    pair = []
    diags = OWN_DIAG, MATE_DIAG
    for total, vector, diag in zip(joined(held, came), (solved, solved_mate), diags):
        part = products(share, total.astype(BF16), blocks, at, diag)
        pair.append((vector[...].astype(F32) - part).astype(BF16))
    result[...] = pair[0]
    pass_on(pushed_sums(level, share, turned, targets, *pair), *outs)


def last_kernel(share, packed, blocks, held, came, *rest):
    *rest, out = rest
    solved, results = rest[: packed.shape[0]], rest[packed.shape[0] :]
    part = products(share, joined(held, came)[0].astype(BF16), blocks, 0, OWN_DIAG)
    result = (solved[0][...].astype(F32) - part).astype(BF16)
    size = out.shape[1] // 2
    for level in range(packed.shape[0]):
        *owners, _ = unpack(packed, level)
        for which, array in enumerate((solved[level], results[level - 1] if level else result)):
            for half in range(2):
                out[owners[half], which * size : (which + 1) * size] = array[half * size : (half + 1) * size]


def call(kernel, outs, *args, fetched=0, scratch=()):
    specs = [pl.BlockSpec(memory_space=pltpu.VMEM)] * len(args)
    args = list(args)
    for at in range(1, 1 + fetched):
        specs[at] = pl.BlockSpec(memory_space=pltpu.HBM)
        args[at] = pltpu.with_memory_space_constraint(args[at], pltpu.HBM)
    return pl.pallas_call(
        kernel,
        out_shape=outs,
        in_specs=specs,
        out_specs=[pl.BlockSpec(memory_space=pltpu.VMEM)] * len(outs),
        scratch_shapes=scratch,
        compiler_params=pltpu.CompilerParams(vmem_limit_bytes=16 * 2**20),
    )(*args)


def local(right_side, diag_inverse, off_blocks, columns, plan):
    rows, depth, width = right_side.shape
    doms = lax.axis_size("dom")
    levs = lax.axis_size("level")
    levels = levs // 2
    share = depth // levs
    count = 2 * rows
    dom = lax.axis_index("dom")
    lev = lax.axis_index("level")
    near_pairs = [(i, i ^ 1) for i in range(doms)]
    far_pairs = [(i, ((i + 1) ^ 1) - 1) for i in range(1, doms - 1)] + [(0, doms - 1), (doms - 1, 0)]

    weights = jnp.concatenate([diag_inverse[:, None], off_blocks], axis=1)
    weights = lax.all_gather(weights, "level")

    turn = dom % 2
    ids = jnp.arange(levs, dtype=jnp.int32)
    own_level = jnp.sum(jnp.where(ids == lev, plan, 0)) // 2
    inverse = jnp.sum(jnp.where(plan[None, :] == ids[:, None], ids[None, :], 0), axis=1)
    side_of = jnp.where(jnp.arange(levels) % 2 == 1, 2 * turn, 2 - 2 * turn)
    packed = inverse[0::2] + (inverse[1::2] << BITS) + (side_of << (2 * BITS))
    packed = jnp.broadcast_to(packed[:, None], (levels, 128)).astype(jnp.int32)

    here = jnp.where(own_level % 2 == turn, off_blocks[:, 0], off_blocks[:, 2])
    mates = jnp.stack([diag_inverse, here], axis=1)
    by_near = lax.ppermute(mates, "dom", near_pairs)
    by_far = lax.ppermute(mates, "dom", far_pairs)
    mates = jnp.where(own_level % 2 == 1, by_near, by_far)
    first = jnp.einsum("rkb,rbc->rkc", right_side, diag_inverse, preferred_element_type=F32)
    side = jnp.where(own_level == 0, first.astype(BF16), right_side)
    side = side.reshape(rows, levs, share, width)
    side = lax.all_to_all(side, "level", 1, 0, tiled=False)
    side = side.reshape(levs, rows * share, width)[inverse].reshape(levels, count * share, width)

    near_dom = dom + 1 - 2 * turn
    far_dom = (dom - 1 + 2 * turn) % doms
    part = jnp.stack(
        [
            lax.dynamic_slice_in_dim(columns, which * levs * rows, levs * rows, 0)
            for which in (dom, near_dom, far_dom)
        ]
    )
    part = part.reshape(3, levs, rows * 3)[:, inverse].reshape(3, levels, count, 3)
    second = jnp.roll(inverse[1::2], 1)[None, :, None, None]
    met = jnp.where(part // rows % levs == second, rows, 0) + part % rows
    odd = (jnp.arange(levels) % 2 == 1)[:, None]
    meets_own = met[0]
    meets_mate = jnp.where(odd[..., None], met[1], met[2])
    ahead = odd == (turn == 0)
    own_mate = jnp.where(ahead, meets_own[..., 0], meets_own[..., 2])
    mate_own = jnp.where(ahead, meets_mate[..., 0], meets_mate[..., 2])
    k = jnp.arange(share, dtype=jnp.int32)
    span = count * share
    slot = jnp.where(turn == 0, 1, -1) * (jnp.arange(3, dtype=jnp.int32) - 1) + 1
    places = meets_own.transpose(0, 2, 1) * share + slot[None, :, None] * span
    places = (places[..., None] + k).reshape(levels, 3 * span, 1)
    targets = jnp.stack([meets_own[..., 1], mate_own, own_mate + count], axis=1) * share
    targets = (targets[..., None] + k).reshape(levels, 3 * span)
    targets, meets = targets[:, None, :], targets[:, :, None]

    vector = jax.ShapeDtypeStruct((count * share, width), BF16)
    sums = [jax.ShapeDtypeStruct((2 * span, width), kind) for kind in (F32, BF16)]
    paired = levels - 2

    own = side[0]
    far = lax.ppermute(jnp.stack([own, side[paired]]), "dom", far_pairs)
    near = lax.ppermute(jnp.stack([own, side[paired + 1]]), "dom", near_pairs)
    mates, packed, side, places, targets, meets, own, far, near = lax.optimization_barrier(
        (mates, packed, side, places, targets, meets, own, far, near)
    )
    side_mates = [far[1], near[1]]
    far, near = far[0], near[0]
    mates = lax.all_gather(mates, "level")

    def swap(vector, level):
        return lax.ppermute(vector, "dom", far_pairs if level % 2 == 0 else near_pairs)

    def arranged(kernel, levels_now, kinds, copies, behind, *blocks):
        _, *blocks = lax.optimization_barrier((behind, *blocks))
        shape = (len(levels_now), count, kinds, width, width)
        kernel = functools.partial(kernel, levels_now)
        scratch = [pltpu.SemaphoreType.DMA((copies,))]
        outs = [jax.ShapeDtypeStruct(shape, BF16)]
        return call(kernel, outs, packed, *blocks, fetched=len(blocks), scratch=scratch)[0]

    solved = [own]
    solved_mate = []
    for level in range(1, paired):
        if level > 1:
            own = solved[-1]
            far, near = swap(own, 0), swap(own, 1)
        solved_mate.append(near if level % 2 == 0 else far)
        args = places, side, far, own, near
        if level == 1:
            scratch = [pltpu.VMEM((1, count, 4, width, width), BF16), pltpu.SemaphoreType.DMA((rows,))]
            kernel = functools.partial(forward_kernel, level, 0, share, True)
            solved += call(kernel, [vector], packed, weights, *args, fetched=1, scratch=scratch)
            singles = range(2, paired)
            blocks = arranged(arrange_kernel, singles, 4, rows * len(singles), solved[-1], weights)
        else:
            kernel = functools.partial(forward_kernel, level, level - 2, share, False)
            solved += call(kernel, [vector], packed, blocks, *args)

    solved_mate.append(swap(solved[-1], paired - 1))
    upper = range(paired, levels)
    blocks = arranged(arrange_pairs_kernel, upper, 5, 8 * len(upper), solved[-1], weights, mates)
    kernel = functools.partial(entry_kernel, paired, 0, share)
    held, sent = call(kernel, sums, blocks, meets, solved[-1], solved_mate[-1])
    lower = range(paired)
    below = arranged(arrange_pairs_kernel, lower, 5, 8 * len(lower) - 6, held, weights, mates)

    def turned(blocks, at, behind):
        _, blocks = lax.optimization_barrier((behind, blocks))
        outs = [jax.ShapeDtypeStruct((1, count, len(PUSHED), width, width), BF16)]
        return call(functools.partial(turn_kernel, at), outs, blocks)[0]

    for level in upper:
        kernel = functools.partial(forward_pair_kernel, level, level - paired, share, level == levels - 1)
        last = level == levels - 1
        ready = turned(blocks, level - paired, sent) if last else targets
        args = blocks, ready, meets, targets, side, side_mates[level - paired]
        own, mate, held, sent = call(kernel, [vector] * 2 + sums, *args, held, swap(sent, level))
        solved.append(own)
        solved_mate.append(mate)

    results = [own]
    for level in range(levels - 2, 0, -1):
        at = level - paired if level in upper else level
        kernel = functools.partial(backward_kernel, level, at, share)
        here = blocks if level in upper else below
        args = here, turned(here, at, sent), targets, solved[level], solved_mate[level]
        result, held, sent = call(kernel, [vector] + sums, *args, held, swap(sent, level))
        results.append(result)

    dealt = jax.ShapeDtypeStruct((levs, 2 * rows * share, width), BF16)
    kernel = functools.partial(last_kernel, share)
    (dealt,) = call(kernel, [dealt], packed, below, held, swap(sent, 0), *solved, *results[::-1])
    dealt = lax.all_to_all(dealt, "level", 0, 0, tiled=False)
    dealt = dealt.reshape(levs, 2, rows, share, width).transpose(1, 2, 0, 3, 4)
    dealt = dealt.reshape(2, rows, depth, width)
    return dealt[0], dealt[1]


def solution(mesh):
    return jax.shard_map(
        local,
        mesh=mesh,
        in_specs=(
            P(("dom", "level"), None, None),
            P(("dom", "level"), None, None),
            P(("dom", "level"), None, None, None),
            P(),
            P(),
        ),
        out_specs=(P(("dom", "level"), None, None), P(("dom", "level"), None, None)),
        check_vma=False,
    )
```
